32 devices in a mesh: fsdp: 2 (over x), expert: 16 (over z, y, core).
Axes of the slice: x: 2, y: 2, z: 4, core: 2. Of those that a mesh axis runs over, the one named last changes fastest.
Arguments:
- tokens: bfloat16 [4096, 1024], P(('fsdp', 'expert')), may hold values from -6 to 6
- attention_gain: float32 [1024], replicated, may hold values from 0.1 to 1.9
- attention_in: bfloat16 [1024, 3072], P(('fsdp', 'expert')), may hold values from -0.1875 to 0.1875
- attention_out: bfloat16 [1024, 1024], P(('fsdp', 'expert')), may hold values from -0.1875 to 0.1875
- expert_gain: float32 [1024], replicated, may hold values from 0.1 to 1.9
- routes: int32 [4096, 6], P(('fsdp', 'expert')), may hold values from 0 to 15, all different within a row; in each aligned block of 128 rows (0 to 127, 128 to 255, ...) at most 60 rows name the same one
- route_weights: float32 [4096, 6], P(('fsdp', 'expert')), may hold values from 0.1 to 1
- gate_weight: bfloat16 [16, 1024, 704], P('expert'), may hold values from -0.1875 to 0.1875
- up_weight: bfloat16 [16, 1024, 704], P('expert'), may hold values from -0.1875 to 0.1875
- down_weight: bfloat16 [16, 704, 1024], P('expert'), may hold values from -0.21875 to 0.21875
Outputs:
- mixed: bfloat16 [4096, 1024], P(('fsdp', 'expert'))
The draws below stay inside these ranges and needn't reach their ends.
Inputs may be any that keep to these rules, and one draw needn't show every extreme that they name: `routes`: the 6 experts of a token differ. Among the token-expert pairs of the tokens of one device, no expert is named more than 60 times, a bound that some block reaches.
All inputs are finite; a program needn't handle non-finite values.
Results may differ from the reference program's by a relative error of at most 0.0075.
Values may be sent and summed in bfloat16 or wider, within the bound.
No kernel may reach another device: no remote copies, remote signals or barrier semaphores. Data moves between devices by JAX's collectives and lax.ppermute only.
A program may use at most 64 MiB of HBM per device.

```python
import math
import jax
import jax.numpy as jnp
import numpy as np
from jax import lax

D = 1024
HEADS = 8
HEAD_DIM = 128
FF = 704
TOP = 6
TOK_DEV = 128
EXPERTS = 16
CAP = 60
TOKENS = 4096


def steps_of(own_key, shape, cuts, smallest, top_value):
    def one(dim, blocks):
        heights = jax.random.uniform(jax.random.fold_in(jax.random.fold_in(own_key, 6), dim), (blocks,), jnp.float32, smallest / len(cuts), top_value / len(cuts))
        return jnp.repeat(jnp.exp(heights), shape[dim] // blocks).reshape((-1,) + (1,) * (len(shape) - dim - 1))

    loudness = one(*cuts[0])
    for cut in cuts[1:]:
        loudness = loudness * one(*cut)
    return loudness


def shared_out(stream_key, own, number, rows, number_of, top, bound, skew):
    order = jax.random.permutation(stream_key, number_of)
    crowded, usual = shares(number_of, rows * top, bound, skew, True), shares(number_of, rows * top, bound, skew, False)
    places = jnp.arange(number_of)

    def named(sizes, turn):
        used = int((sizes > 0).sum())
        fixed = max(1, used // 4)
        passed = fixed + (places - fixed + turn * (used - fixed)) % max(1, number_of - fixed)
        return jnp.zeros((number_of,), jnp.int32).at[order[jnp.where(places < fixed, places, passed)]].set(jnp.asarray(sizes, jnp.int32))

    sizes = jnp.where(number % 4 == 0, named(crowded, number // 4), named(usual, number - number // 4 - 1))
    mixed = jax.random.permutation(jax.random.fold_in(own, 3), number_of)
    giver, receiver = mixed[0:number_of // 2 * 2:2], mixed[1:number_of // 2 * 2:2]
    room = jnp.minimum(sizes[giver] - 1, bound - sizes[receiver]) // 2
    room = jnp.where((giver == order[0]) | (receiver == order[0]) | (sizes[receiver] == 0), 0, jnp.maximum(room, 0))
    passed = jax.random.randint(jax.random.fold_in(own, 4), (number_of // 2,), 0, 1 << 20) % (room + 1)
    sizes = sizes.at[giver].add(-passed).at[receiver].add(passed)
    labels = jnp.searchsorted(jnp.cumsum(sizes), jnp.arange(rows * top), side="right").astype(jnp.int32)
    table = labels.reshape(top, rows).T
    table = table[jax.random.permutation(jax.random.fold_in(own, 1), rows)]
    turn = jax.random.randint(jax.random.fold_in(own, 2), (rows, 1), 0, top)
    return jnp.take_along_axis(table, (jnp.arange(top)[None, :] + turn) % top, axis=1)


def shares(count, total, limit, slope, full):
    portions = [(1 << 20) // math.isqrt(rank ** slope) + 1 for rank in range(1, count + 1)]
    largest = limit if full else min(limit, max(-(-total // count), total * portions[0] // sum(portions)))
    least = 1 if total - largest >= count - 1 else 0
    given, surplus = [largest] + [least] * (count - 1), total - largest - least * (count - 1)
    while surplus > 0:
        movable = [i for i in range(1, count) if given[i] < largest] or [i for i in range(1, count) if given[i] < limit]
        pool, budget = sum([portions[i] for i in movable]), surplus
        for i in movable:
            addition = min(limit - given[i], max(1, budget * portions[i] // pool), surplus)
            given[i] = given[i] + addition
            surplus = surplus - addition
    return np.array(given)


def normal_values(stream_key, extent, deviation, limit, pieces=(), kind=jnp.bfloat16):
    level = steps_of(stream_key, extent, pieces, -0.22, 0.18) if pieces else 1.0
    result = jax.random.normal(stream_key, extent, jnp.float32) * deviation * level
    return jnp.minimum(jnp.maximum(result, -limit), limit).astype(kind)


def setup_inputs(seed: int = 0) -> dict:
    streams_of = jax.random.split(jax.random.key(seed), 11)
    tokens = normal_values(streams_of[0], (TOKENS, D), 1.0, 6.0, ((0, 32),))
    attention_gain = jnp.clip(1.0 + 0.18 * jax.random.normal(streams_of[1], (D,), jnp.float32), 0.1, 1.9)
    attention_in = normal_values(streams_of[2], (D, 3 * HEADS * HEAD_DIM), D ** -0.5, 0.1875, ((0, 32),))
    attention_out = normal_values(streams_of[3], (D, HEADS * HEAD_DIM), (HEADS * HEAD_DIM) ** -0.5, 0.1875, ((0, 32),))
    expert_gain = jnp.clip(1.0 + 0.18 * jax.random.normal(streams_of[4], (D,), jnp.float32), 0.1, 1.9)
    routes_keys = jax.random.split(jax.random.fold_in(streams_of[5], 1), TOKENS // TOK_DEV)
    routes_turns = jax.random.permutation(jax.random.fold_in(streams_of[5], 3), TOKENS // TOK_DEV)
    routes = jax.vmap(lambda own, number: shared_out(jax.random.fold_in(streams_of[5], 2), own, number, TOK_DEV, EXPERTS, TOP, CAP, 2))(routes_keys, routes_turns).reshape((TOKENS, TOP))
    route_weights = jnp.clip(0.1 + 0.9 * jax.random.uniform(streams_of[6], (TOKENS, TOP), jnp.float32) ** steps_of(streams_of[6], (TOKENS, TOP), ((0, 32),), -0.2, 0.2), 0.1, 1.0)
    gate_weight = normal_values(streams_of[7], (EXPERTS, D, FF), D ** -0.5, 0.1875, ((0, 16),))
    up_weight = normal_values(streams_of[8], (EXPERTS, D, FF), D ** -0.5, 0.1875, ((0, 16),))
    down_weight = normal_values(streams_of[9], (EXPERTS, FF, D), FF ** -0.5, 0.21875, ((0, 16),))
    return {"tokens": tokens, "attention_gain": attention_gain, "attention_in": attention_in, "attention_out": attention_out, "expert_gain": expert_gain, "routes": routes, "route_weights": route_weights, "gate_weight": gate_weight, "up_weight": up_weight, "down_weight": down_weight}


def rms_scale(inputs, scale_gain):
    mean_square = lax.optimization_barrier(jnp.mean(inputs * inputs, axis=-1, keepdims=True))
    return inputs * lax.rsqrt(mean_square + 1e-06) * scale_gain

def reference(tokens, attention_gain, attention_in, attention_out, expert_gain, routes, route_weights, gate_weight, up_weight, down_weight):
    stream = tokens.astype(jnp.float32)
    normed = rms_scale(stream, attention_gain).astype(jnp.bfloat16)
    projected = jnp.dot(normed, attention_in, preferred_element_type=jnp.float32).astype(jnp.bfloat16)
    sequences = TOKENS // TOK_DEV
    split_heads = projected.reshape(sequences, TOK_DEV, 3, HEADS, HEAD_DIM).astype(jnp.float32)
    queries = split_heads[:, :, 0]
    key_rows = split_heads[:, :, 1]
    value_rows = split_heads[:, :, 2]
    scores = jnp.einsum('sqhd,skhd->shqk', queries, key_rows) / math.sqrt(HEAD_DIM)
    causal = jnp.arange(TOK_DEV)[:, None] >= jnp.arange(TOK_DEV)[None, :]
    raised = jnp.where(causal, jnp.exp(jnp.where(causal, scores, 0.0)), 0.0)
    attention_probs = (raised / lax.optimization_barrier(jnp.sum(raised, axis=-1, keepdims=True))).astype(jnp.bfloat16)
    heads_out = jnp.einsum('shqk,skhd->sqhd', attention_probs.astype(jnp.float32), value_rows).astype(jnp.bfloat16)
    heads_out = heads_out.reshape(TOKENS, HEADS * HEAD_DIM)
    attended = lax.dot_general(heads_out, attention_out, (((1,), (1,)), ((), ())), preferred_element_type=jnp.float32)
    hidden_stream = stream + attended
    expert_in = rms_scale(hidden_stream, expert_gain).astype(jnp.bfloat16)
    pair_count = TOKENS * TOP
    flat_routes = routes.reshape(pair_count).astype(jnp.int32)
    flat_weights = route_weights.reshape(pair_count)
    sorted_pairs = jnp.argsort(flat_routes, stable=True).astype(jnp.int32)
    expert_ids = jnp.arange(EXPERTS, dtype=jnp.int32)
    counts = lax.optimization_barrier(jnp.sum((flat_routes[:, None] == expert_ids[None, :]).astype(jnp.int32), axis=0, dtype=jnp.int32))
    starts = jnp.cumsum(counts, dtype=jnp.int32) - counts
    slot_limit = TOKENS // TOK_DEV * CAP
    offsets = jnp.arange(slot_limit, dtype=jnp.int32)

    def one_expert(running, packed):
        expert_index, gate_block, up_block, down_block = packed
        position = starts[expert_index] + offsets
        live_slot = offsets < counts[expert_index]
        pair_index = sorted_pairs[jnp.minimum(position, pair_count - 1)]
        token_index = (pair_index // TOP).astype(jnp.int32)
        chosen = expert_in[token_index].astype(jnp.float32)
        gate_value = jnp.dot(chosen, gate_block.astype(jnp.float32), precision=lax.Precision.HIGHEST)
        up_value = jnp.dot(chosen, up_block.astype(jnp.float32), precision=lax.Precision.HIGHEST)
        inner_hidden = (jax.nn.silu(gate_value) * up_value).astype(jnp.bfloat16)
        output = jnp.dot(inner_hidden.astype(jnp.float32), down_block.astype(jnp.float32), precision=lax.Precision.HIGHEST).astype(jnp.bfloat16)
        pair_scale = jnp.where(live_slot, flat_weights[pair_index], 0.0)
        running = running.at[token_index].add(pair_scale[:, None] * output.astype(jnp.float32))
        return (running, None)
    moe_total, _ = lax.scan(one_expert, jnp.zeros((TOKENS, D), jnp.float32), (expert_ids, gate_weight, up_weight, down_weight))
    return (hidden_stream + moe_total).astype(jnp.bfloat16)
```

```python
import math

import jax
import jax.numpy as jnp
from jax import lax
from jax.sharding import PartitionSpec as P

HEAD_DIM = 128
BOTH = ("fsdp", "expert")


def rms_scale(inputs, scale_gain):
    mean_square = jnp.mean(inputs * inputs, axis=-1, keepdims=True)
    return inputs * lax.rsqrt(mean_square + 1e-06) * scale_gain


def group_shape(fsdp_size, expert_size, head_count):
    along_fsdp = math.gcd(fsdp_size, 2)
    return along_fsdp, head_count // along_fsdp


def per_device(
    tokens,
    attention_gain,
    attention_in,
    attention_out,
    expert_gain,
    routes,
    route_weights,
    gate_weight,
    up_weight,
    down_weight,
):
    fsdp_size = lax.axis_size("fsdp")
    expert_size = lax.axis_size("expert")
    row_count, model_width = tokens.shape
    weight_rows, head_width = attention_out.shape
    head_count = head_width // HEAD_DIM
    group_f, group_e = group_shape(fsdp_size, expert_size, head_count)
    groups = [
        [
            (fo * group_f + fi) * expert_size + eo * group_e + ei
            for fi in range(group_f)
            for ei in range(group_e)
        ]
        for fo in range(fsdp_size // group_f)
        for eo in range(expert_size // group_e)
    ]

    stream = tokens.astype(jnp.float32)
    normed = rms_scale(stream, attention_gain).astype(jnp.bfloat16)
    group_rows = lax.all_gather(normed, BOTH, axis_index_groups=groups, axis=0, tiled=True)

    by_head = jnp.concatenate(
        [
            attention_in.reshape(weight_rows, 3, head_count, HEAD_DIM),
            attention_out.reshape(weight_rows, 1, head_count, HEAD_DIM),
        ],
        axis=1,
    )
    by_head = by_head.transpose(2, 0, 1, 3).reshape(
        1, group_f, 1, group_e, weight_rows, 4 * HEAD_DIM
    )
    outgoing = jnp.broadcast_to(
        by_head,
        (
            fsdp_size // group_f,
            group_f,
            expert_size // group_e,
            group_e,
            weight_rows,
            4 * HEAD_DIM,
        ),
    ).reshape(fsdp_size * expert_size, weight_rows, 4 * HEAD_DIM)
    head_weights = lax.all_to_all(outgoing, BOTH, split_axis=0, concat_axis=0, tiled=True)
    head_weights = head_weights.reshape(model_width, 4 * HEAD_DIM)

    projected = jnp.dot(
        group_rows, head_weights[:, : 3 * HEAD_DIM], preferred_element_type=jnp.float32
    ).astype(jnp.bfloat16)
    projected = projected.reshape(head_count, row_count, 3, HEAD_DIM)
    scores = jnp.einsum(
        "sqd,skd->sqk",
        projected[:, :, 0],
        projected[:, :, 1],
        preferred_element_type=jnp.float32,
    ) / math.sqrt(HEAD_DIM)
    causal = jnp.arange(row_count)[:, None] >= jnp.arange(row_count)[None, :]
    raised = jnp.where(causal, jnp.exp(jnp.where(causal, scores, 0.0)), 0.0)
    attention_probs = (raised / jnp.sum(raised, axis=-1, keepdims=True)).astype(jnp.bfloat16)
    heads_out = jnp.einsum(
        "sqk,skd->sqd", attention_probs, projected[:, :, 2], preferred_element_type=jnp.float32
    ).astype(jnp.bfloat16)
    part = lax.dot_general(
        heads_out.reshape(head_count * row_count, HEAD_DIM),
        head_weights[:, 3 * HEAD_DIM :],
        (((1,), (1,)), ((), ())),
        preferred_element_type=jnp.float32,
    ).astype(jnp.bfloat16)
    attended = lax.psum_scatter(
        part, BOTH, scatter_dimension=0, axis_index_groups=groups, tiled=True
    )
    hidden_stream = stream + attended.astype(jnp.float32)
    expert_in = rms_scale(hidden_stream, expert_gain).astype(jnp.bfloat16)

    chosen = routes[:, :, None] == jnp.arange(expert_size, dtype=jnp.int32)
    scale_map = jnp.sum(jnp.where(chosen, route_weights[:, :, None], 0.0), axis=1)
    my_scale = lax.all_to_all(
        scale_map.T.reshape(expert_size, row_count),
        "expert",
        split_axis=0,
        concat_axis=0,
        tiled=True,
    ).reshape(expert_size * row_count, 1)
    all_in = lax.all_gather(expert_in, "expert", axis=0, tiled=True)
    gate_value = jnp.dot(all_in, gate_weight[0], preferred_element_type=jnp.float32)
    up_value = jnp.dot(all_in, up_weight[0], preferred_element_type=jnp.float32)
    inner_hidden = (jax.nn.silu(gate_value) * up_value).astype(jnp.bfloat16)
    result = jnp.dot(inner_hidden, down_weight[0], preferred_element_type=jnp.float32)
    result = (jnp.where(my_scale > 0, result, 0.0) * my_scale).astype(jnp.bfloat16)
    mixture = lax.psum_scatter(result, "expert", scatter_dimension=0, tiled=True)
    return (hidden_stream + mixture.astype(jnp.float32)).astype(jnp.bfloat16)


def solution(mesh):
    placed = (
        P(("fsdp", "expert"), None),
        P(),
        P(("fsdp", "expert"), None),
        P(("fsdp", "expert"), None),
        P(),
        P(("fsdp", "expert"), None),
        P(("fsdp", "expert"), None),
        P("expert", None, None),
        P("expert", None, None),
        P("expert", None, None),
    )
    return jax.shard_map(
        per_device,
        mesh=mesh,
        in_specs=placed,
        out_specs=P(("fsdp", "expert"), None),
        check_vma=False,
    )
```

```python
import functools
import math

import jax
import jax.numpy as jnp
from jax import lax
from jax.experimental import pallas as pl
from jax.experimental.pallas import tpu as pltpu
from jax.sharding import PartitionSpec as P

HEAD_DIM = 128
BOTH = ("fsdp", "expert")
VMEM = pl.BlockSpec(memory_space=pltpu.VMEM)
ANYWHERE = pl.BlockSpec(memory_space=pl.ANY)
NT = (((1,), (1,)), ((), ()))


def dot_nt(left, right):
    return lax.dot_general(left, right, NT, preferred_element_type=jnp.float32)


def rms_scale(inputs, scale_gain):
    mean_square = jnp.mean(inputs * inputs, axis=-1, keepdims=True)
    return inputs * lax.rsqrt(mean_square + 1e-06) * scale_gain


def attention_kernel(block_count, *refs):
    block_refs = refs[:block_count]
    weight_ref, keep_ref, send_ref = refs[block_count:]
    rows = block_refs[0].shape[0]
    half = block_count // 2
    in_weights = weight_ref[:, : 3 * HEAD_DIM]
    out_weights = weight_ref[:, 3 * HEAD_DIM :]
    causal = lax.broadcasted_iota(jnp.int32, (rows, rows), 0) >= lax.broadcasted_iota(
        jnp.int32, (rows, rows), 1
    )
    for first in range(0, block_count, 2):
        pair = jnp.concatenate([block_refs[first][...], block_refs[first + 1][...]], axis=0)
        projected = jnp.dot(pair, in_weights, preferred_element_type=jnp.float32)
        projected = projected.astype(jnp.bfloat16)
        heads = []
        for which in range(2):
            own = projected[which * rows : (which + 1) * rows]
            queries = own[:, :HEAD_DIM]
            keys = own[:, HEAD_DIM : 2 * HEAD_DIM]
            values = own[:, 2 * HEAD_DIM :]
            scores = dot_nt(queries, keys) * (1.0 / math.sqrt(HEAD_DIM))
            raised = jnp.where(causal, jnp.exp(jnp.where(causal, scores, 0.0)), 0.0)
            probs = raised / jnp.sum(raised, axis=-1, keepdims=True)
            heads.append(
                jnp.dot(
                    probs.astype(jnp.bfloat16), values, preferred_element_type=jnp.float32
                ).astype(jnp.bfloat16)
            )
        part = dot_nt(jnp.concatenate(heads, axis=0), out_weights).astype(jnp.bfloat16)
        for which in range(2):
            block = first + which
            target = keep_ref if block < half else send_ref
            target[block % half] = part[which * rows : (which + 1) * rows]


def attention_call(blocks, head_weights):
    count = len(blocks)
    rows, width = blocks[0].shape
    out = jax.ShapeDtypeStruct((count // 2, rows, width), jnp.bfloat16)
    tokens = count * rows
    return pl.pallas_call(
        functools.partial(attention_kernel, count),
        out_shape=(out, out),
        in_specs=[VMEM] * (count + 1),
        out_specs=(VMEM, VMEM),
        compiler_params=pltpu.CompilerParams(vmem_limit_bytes=32 * 2**20),
        cost_estimate=pl.CostEstimate(
            flops=2 * tokens * (width * 4 * HEAD_DIM + 2 * rows * HEAD_DIM),
            bytes_accessed=4 * tokens * width + head_weights.size * 2,
            transcendentals=tokens * rows,
        ),
    )(*blocks, head_weights)


def stream_kernel(tokens_ref, gain_ref, top_ref, top_in_ref, low_ref, low_in_ref, hid_ref, out_ref):
    half = top_ref.shape[0]
    for first, own, other in ((0, top_ref, top_in_ref), (half, low_ref, low_in_ref)):
        rows = pl.ds(first, half)
        hidden = (
            tokens_ref[rows, :].astype(jnp.float32)
            + own[...].astype(jnp.float32)
            + other[...].astype(jnp.float32)
        )
        hid_ref[rows, :] = hidden
        out_ref[rows, :] = rms_scale(hidden, gain_ref[...]).astype(jnp.bfloat16)


def stream_call(tokens, gain, top, top_in, low, low_in):
    return pl.pallas_call(
        stream_kernel,
        out_shape=(
            jax.ShapeDtypeStruct(tokens.shape, jnp.float32),
            jax.ShapeDtypeStruct(tokens.shape, jnp.bfloat16),
        ),
        in_specs=[VMEM] * 6,
        out_specs=(VMEM, VMEM),
        cost_estimate=pl.CostEstimate(
            flops=6 * tokens.size, bytes_accessed=12 * tokens.size, transcendentals=0
        ),
    )(tokens, gain[None, :], top, top_in, low, low_in)


def expert_kernel(tiles, *refs):
    block_refs = refs[:4]
    scale_ref, gate_hbm, up_hbm, down_hbm, keep_ref, send_ref = refs[4:10]
    gate_ref, up_ref, down_ref, sems = refs[10:]
    copies = []
    for index, (start, size) in enumerate(tiles):
        rows = pl.ds(start, size)
        copies.append(
            [
                pltpu.make_async_copy(hbm.at[rows], ref.at[rows], sems.at[index, which])
                for which, (hbm, ref) in enumerate(
                    ((gate_hbm, gate_ref), (up_hbm, up_ref), (down_hbm, down_ref))
                )
            ]
        )
    for tile in copies:
        for copy in tile:
            copy.start()
    inputs = jnp.concatenate([ref[...] for ref in block_refs], axis=0)
    total = None
    for index, (start, size) in enumerate(tiles):
        copies[index][0].wait()
        copies[index][1].wait()
        gate_value = dot_nt(inputs, gate_ref[start : start + size, :])
        up_value = dot_nt(inputs, up_ref[start : start + size, :])
        inner = (gate_value / (1.0 + jnp.exp(-gate_value)) * up_value).astype(jnp.bfloat16)
        copies[index][2].wait()
        term = jnp.dot(inner, down_ref[start : start + size, :], preferred_element_type=jnp.float32)
        total = term if total is None else total + term
    scale = scale_ref[...]
    result = jnp.where(scale > 0, total * scale, 0.0).astype(jnp.bfloat16)
    rows = block_refs[0].shape[0]
    for block in range(4):
        target = keep_ref if block < 2 else send_ref
        target[block % 2] = result[block * rows : (block + 1) * rows]


def expert_call(blocks, scale, gate_rows, up_rows, down_rows):
    rows, width = blocks[0].shape
    hidden = gate_rows.shape[0]
    tiles = [(start, min(256, hidden - start)) for start in range(0, hidden, 256)]
    out = jax.ShapeDtypeStruct((2, rows, width), jnp.bfloat16)
    return pl.pallas_call(
        functools.partial(expert_kernel, tiles),
        out_shape=(out, out),
        in_specs=[VMEM] * 5 + [ANYWHERE] * 3,
        out_specs=(VMEM, VMEM),
        scratch_shapes=[pltpu.VMEM((hidden, width), jnp.bfloat16)] * 3
        + [pltpu.SemaphoreType.DMA((len(tiles), 3))],
        compiler_params=pltpu.CompilerParams(vmem_limit_bytes=40 * 2**20),
        cost_estimate=pl.CostEstimate(
            flops=2 * 4 * rows * width * hidden * 3,
            bytes_accessed=6 * hidden * width + 16 * rows * width,
            transcendentals=4 * rows * hidden,
        ),
    )(*blocks, scale, gate_rows, up_rows, down_rows)


def per_device(
    tokens,
    attention_gain,
    attention_in,
    attention_out,
    expert_gain,
    routes,
    route_weights,
    gate_weight,
    up_weight,
    down_weight,
):
    fsdp_size = lax.axis_size("fsdp")
    expert_size = lax.axis_size("expert")
    row_count, model_width = tokens.shape
    weight_rows, head_width = attention_out.shape
    head_count = head_width // HEAD_DIM
    layers = expert_size // 4

    def swap_pair(value):
        return lax.ppermute(value, "fsdp", [(f, f ^ 1) for f in range(fsdp_size)])

    def swap_side(value):
        return lax.ppermute(value, "expert", [(e, e ^ 2) for e in range(expert_size)])

    def swap_core(value):
        return lax.ppermute(value, "expert", [(e, e ^ 1) for e in range(expert_size)])

    def shift_layer(value, step):
        return lax.ppermute(
            value, "expert", [(e, (e + 4 * step) % expert_size) for e in range(expert_size)]
        )

    my_expert = lax.axis_index("expert")
    chosen = routes[:, :, None] == jnp.arange(expert_size, dtype=jnp.int32)
    scale_map = jnp.sum(jnp.where(chosen, route_weights[:, :, None], 0.0), axis=1).T
    scale_maps = lax.all_gather(scale_map, "expert", axis=0)
    my_scale = lax.dynamic_index_in_dim(scale_maps, my_expert, axis=1, keepdims=False)
    offsets = jnp.arange(expert_size, dtype=jnp.int32)
    senders = (my_expert // 4 - offsets // 4 + layers) % layers * 4 + (
        (my_expert % 4) ^ (offsets % 4 // 2 + offsets % 2 * 2)
    )
    scales = my_scale[senders].reshape(layers, 4 * row_count, 1)

    by_head = jnp.concatenate(
        [
            attention_in.reshape(weight_rows, 3, head_count, HEAD_DIM),
            attention_out.reshape(weight_rows, 1, head_count, HEAD_DIM),
        ],
        axis=1,
    )
    by_head = by_head.transpose(2, 0, 1, 3).reshape(1, 2, 1, 4, weight_rows, 4 * HEAD_DIM)
    outgoing = jnp.broadcast_to(
        by_head, (fsdp_size // 2, 2, layers, 4, weight_rows, 4 * HEAD_DIM)
    ).reshape(fsdp_size * expert_size, weight_rows, 4 * HEAD_DIM)
    head_weights = lax.all_to_all(outgoing, BOTH, split_axis=0, concat_axis=0, tiled=True)
    head_weights = head_weights.reshape(model_width, 4 * HEAD_DIM)

    normed = rms_scale(tokens.astype(jnp.float32), attention_gain).astype(jnp.bfloat16)
    blocks = [normed, swap_pair(normed)]
    blocks += [swap_side(block) for block in blocks]
    blocks += [swap_core(block) for block in blocks]
    keep, send = attention_call(blocks, head_weights)

    def added(*terms):
        total = terms[0].astype(jnp.float32)
        for term in terms[1:]:
            total = total + term.astype(jnp.float32)
        return total.astype(jnp.bfloat16)

    half = row_count // 2
    summed = added(keep, swap_core(send)).reshape(2, 2, row_count, model_width)
    top = added(summed[0, :, :half], swap_side(summed[1, :, :half]))
    low = added(summed[:, 0, half:], swap_pair(summed[:, 1, half:]))
    hidden_stream, expert_in = stream_call(
        tokens, expert_gain, top[0], swap_pair(top[1]), low[0], swap_side(low[1])
    )

    gate_rows = gate_weight[0].T
    up_rows = up_weight[0].T
    down_rows = down_weight[0]
    mixture = hidden_stream
    for step in range(layers):
        block = expert_in if step == 0 else shift_layer(expert_in, step)
        blocks = [block, swap_side(block)]
        blocks += [swap_core(item) for item in blocks]
        keep, send = expert_call(blocks, scales[step], gate_rows, up_rows, down_rows)
        arrived = swap_core(send)
        crossing = added(keep[1], arrived[1])
        mine = added(keep[0], arrived[0], swap_side(crossing))
        mixture = mixture + (mine if step == 0 else shift_layer(mine, -step)).astype(jnp.float32)
    return mixture.astype(jnp.bfloat16)


def solution(mesh):
    placed = (
        P(("fsdp", "expert"), None),
        P(),
        P(("fsdp", "expert"), None),
        P(("fsdp", "expert"), None),
        P(),
        P(("fsdp", "expert"), None),
        P(("fsdp", "expert"), None),
        P("expert", None, None),
        P("expert", None, None),
        P("expert", None, None),
    )
    return jax.shard_map(
        per_device,
        mesh=mesh,
        in_specs=placed,
        out_specs=P(("fsdp", "expert"), None),
        check_vma=False,
    )
```

```python
import functools
import math

import jax
import jax.numpy as jnp
from jax import lax
from jax.experimental import pallas as pl
from jax.experimental.pallas import tpu as pltpu
from jax.sharding import PartitionSpec as P

HEAD_DIM = 128
BOTH = ("fsdp", "expert")
VMEM = pl.BlockSpec(memory_space=pltpu.VMEM)
ANYWHERE = pl.BlockSpec(memory_space=pl.ANY)
NT = (((1,), (1,)), ((), ()))


def dot_nt(left, right):
    return lax.dot_general(left, right, NT, preferred_element_type=jnp.float32)


def rms_scale(inputs, scale_gain):
    mean_square = jnp.mean(inputs * inputs, axis=-1, keepdims=True)
    return inputs * lax.rsqrt(mean_square + 1e-06) * scale_gain


def attention_kernel(block_count, *refs):
    block_refs = refs[:block_count]
    weight_ref = refs[block_count]
    keep_ref, send_ref = refs[-2:]
    rows = block_refs[0].shape[0]
    half = block_count // 2
    in_weights = weight_ref[:, : 3 * HEAD_DIM]
    out_weights = weight_ref[:, 3 * HEAD_DIM :]
    causal = lax.broadcasted_iota(jnp.int32, (rows, rows), 0) >= lax.broadcasted_iota(
        jnp.int32, (rows, rows), 1
    )
    for first in range(0, block_count, 2):
        pair = jnp.concatenate([block_refs[first][...], block_refs[first + 1][...]], axis=0)
        projected = jnp.dot(pair, in_weights, preferred_element_type=jnp.float32)
        projected = projected.astype(jnp.bfloat16)
        heads = []
        for which in range(2):
            own = projected[which * rows : (which + 1) * rows]
            queries = own[:, :HEAD_DIM]
            keys = own[:, HEAD_DIM : 2 * HEAD_DIM]
            values = own[:, 2 * HEAD_DIM :]
            scores = dot_nt(queries, keys) * (1.0 / math.sqrt(HEAD_DIM))
            raised = jnp.where(causal, jnp.exp(jnp.where(causal, scores, 0.0)), 0.0)
            probs = raised / jnp.sum(raised, axis=-1, keepdims=True)
            heads.append(
                jnp.dot(
                    probs.astype(jnp.bfloat16), values, preferred_element_type=jnp.float32
                ).astype(jnp.bfloat16)
            )
        part = dot_nt(jnp.concatenate(heads, axis=0), out_weights).astype(jnp.bfloat16)
        for which in range(2):
            block = first + which
            target = keep_ref if block < half else send_ref
            target[block % half] = part[which * rows : (which + 1) * rows]


def attention_call(blocks, head_weights, after):
    count = len(blocks)
    rows, width = blocks[0].shape
    out = jax.ShapeDtypeStruct((count // 2, rows, width), jnp.bfloat16)
    tokens = count * rows
    return pl.pallas_call(
        functools.partial(attention_kernel, count),
        out_shape=(out, out),
        in_specs=[VMEM] * (count + 1) + [ANYWHERE] * len(after),
        out_specs=(VMEM, VMEM),
        compiler_params=pltpu.CompilerParams(vmem_limit_bytes=24 * 2**20),
        cost_estimate=pl.CostEstimate(
            flops=2 * tokens * (width * 4 * HEAD_DIM + 2 * rows * HEAD_DIM),
            bytes_accessed=4 * tokens * width + head_weights.size * 2,
            transcendentals=tokens * rows,
        ),
    )(*blocks, head_weights, *after)


def stream_kernel(tokens_ref, gain_ref, top_ref, top_in_ref, low_ref, low_in_ref, hid_ref, out_ref):
    half = top_ref.shape[0]
    for first, own, other in ((0, top_ref, top_in_ref), (half, low_ref, low_in_ref)):
        rows = pl.ds(first, half)
        hidden = (
            tokens_ref[rows, :].astype(jnp.float32)
            + own[...].astype(jnp.float32)
            + other[...].astype(jnp.float32)
        )
        hid_ref[rows, :] = hidden
        out_ref[rows, :] = rms_scale(hidden, gain_ref[...]).astype(jnp.bfloat16)


def stream_call(tokens, gain, top, top_in, low, low_in):
    return pl.pallas_call(
        stream_kernel,
        out_shape=(
            jax.ShapeDtypeStruct(tokens.shape, jnp.float32),
            jax.ShapeDtypeStruct(tokens.shape, jnp.bfloat16),
        ),
        in_specs=[VMEM] * 6,
        out_specs=(VMEM, VMEM),
        compiler_params=pltpu.CompilerParams(vmem_limit_bytes=12 * 2**20),
        cost_estimate=pl.CostEstimate(
            flops=6 * tokens.size, bytes_accessed=12 * tokens.size, transcendentals=0
        ),
    )(tokens, gain[None, :], top, top_in, low, low_in)


def expert_kernel(tiles, *refs):
    block_refs = refs[:4]
    scale_ref, gate_ref, up_ref, down_ref = refs[4:8]
    keep_ref, send_ref = refs[-2:]
    inputs = jnp.concatenate([ref[...] for ref in block_refs], axis=0)
    total = None
    for start, size in tiles:
        gate_value = dot_nt(inputs, gate_ref[start : start + size, :])
        up_value = dot_nt(inputs, up_ref[start : start + size, :])
        inner = (gate_value / (1.0 + jnp.exp(-gate_value)) * up_value).astype(jnp.bfloat16)
        term = jnp.dot(inner, down_ref[start : start + size, :], preferred_element_type=jnp.float32)
        total = term if total is None else total + term
    scale = scale_ref[...]
    result = jnp.where(scale > 0, total * scale, 0.0).astype(jnp.bfloat16)
    rows = block_refs[0].shape[0]
    for block in range(4):
        target = keep_ref if block < 2 else send_ref
        target[block % 2] = result[block * rows : (block + 1) * rows]


def expert_call(blocks, scale, gate_rows, up_rows, down_rows, after):
    rows, width = blocks[0].shape
    hidden = gate_rows.shape[0]
    tiles = [(start, min(256, hidden - start)) for start in range(0, hidden, 256)]
    out = jax.ShapeDtypeStruct((2, rows, width), jnp.bfloat16)
    return pl.pallas_call(
        functools.partial(expert_kernel, tiles),
        out_shape=(out, out),
        in_specs=[VMEM] * 8 + [ANYWHERE] * len(after),
        out_specs=(VMEM, VMEM),
        compiler_params=pltpu.CompilerParams(vmem_limit_bytes=24 * 2**20),
        cost_estimate=pl.CostEstimate(
            flops=2 * 4 * rows * width * hidden * 3,
            bytes_accessed=6 * hidden * width + 16 * rows * width,
            transcendentals=4 * rows * hidden,
        ),
    )(*blocks, scale, gate_rows, up_rows, down_rows, *after)


def per_device(
    tokens,
    attention_gain,
    attention_in,
    attention_out,
    expert_gain,
    routes,
    route_weights,
    gate_weight,
    up_weight,
    down_weight,
):
    fsdp_size = lax.axis_size("fsdp")
    expert_size = lax.axis_size("expert")
    row_count, model_width = tokens.shape
    weight_rows, head_width = attention_out.shape
    head_count = head_width // HEAD_DIM
    layers = expert_size // 4

    def swap_pair(value):
        return lax.ppermute(value, "fsdp", [(f, f ^ 1) for f in range(fsdp_size)])

    def swap_side(value):
        return lax.ppermute(value, "expert", [(e, e ^ 2) for e in range(expert_size)])

    def swap_core(value):
        return lax.ppermute(value, "expert", [(e, e ^ 1) for e in range(expert_size)])

    def shift_layer(value, step):
        return lax.ppermute(
            value, "expert", [(e, (e + 4 * step) % expert_size) for e in range(expert_size)]
        )

    my_expert = lax.axis_index("expert")
    chosen = routes[:, :, None] == jnp.arange(expert_size, dtype=jnp.int32)
    scale_map = jnp.sum(jnp.where(chosen, route_weights[:, :, None], 0.0), axis=1).T[None]
    scale_map = jnp.concatenate([scale_map, swap_side(scale_map)], axis=0)
    scale_map = jnp.concatenate([scale_map, swap_core(scale_map)], axis=0)
    scales = [
        lax.dynamic_index_in_dim(
            scale_map if step == 0 else shift_layer(scale_map, -step),
            my_expert,
            axis=1,
            keepdims=False,
        ).reshape(4 * row_count, 1)
        for step in range(layers)
    ]

    by_head = jnp.concatenate(
        [
            attention_in.reshape(weight_rows, 3, head_count, HEAD_DIM),
            attention_out.reshape(weight_rows, 1, head_count, HEAD_DIM),
        ],
        axis=1,
    )
    by_head = by_head.transpose(2, 0, 1, 3).reshape(1, 2, 1, 4, weight_rows, 4 * HEAD_DIM)
    outgoing = jnp.broadcast_to(
        by_head, (fsdp_size // 2, 2, layers, 4, weight_rows, 4 * HEAD_DIM)
    ).reshape(fsdp_size * expert_size, weight_rows, 4 * HEAD_DIM)
    head_weights = lax.all_to_all(outgoing, BOTH, split_axis=0, concat_axis=0, tiled=True)
    head_weights = head_weights.reshape(model_width, 4 * HEAD_DIM)

    normed = rms_scale(tokens.astype(jnp.float32), attention_gain).astype(jnp.bfloat16)
    blocks = [normed, swap_pair(normed)]
    blocks += [swap_side(block) for block in blocks]
    blocks += [swap_core(block) for block in blocks]
    keep, send = attention_call(blocks, head_weights, scales)

    def added(*terms):
        total = terms[0].astype(jnp.float32)
        for term in terms[1:]:
            total = total + term.astype(jnp.float32)
        return total.astype(jnp.bfloat16)

    half = row_count // 2
    summed = added(keep, swap_core(send)).reshape(2, 2, row_count, model_width)
    top = added(summed[0, :, :half], swap_side(summed[1, :, :half]))
    low = added(summed[:, 0, half:], swap_pair(summed[:, 1, half:]))
    hidden_stream, expert_in = stream_call(
        tokens, expert_gain, top[0], swap_pair(top[1]), low[0], swap_side(low[1])
    )

    gate_rows = gate_weight[0].T
    up_rows = up_weight[0].T
    down_rows = down_weight[0]
    held = expert_in
    crossings, sums = [], []
    local = running = None
    for step in range(layers):
        if step > 0:
            held = shift_layer(held, -1)
        blocks = [held, swap_side(held)]
        blocks += [swap_core(item) for item in blocks]
        keep, send = expert_call(
            blocks, scales[step], gate_rows, up_rows, down_rows, crossings[-1:] + sums[-2:-1]
        )
        arrived = swap_core(send)
        crossing = added(keep[1], arrived[1])
        crossings.append(crossing)
        terms = [keep[0], arrived[0], swap_side(crossing)]
        if step == 0:
            local = added(*terms)
            sums.append(local)
        else:
            running = added(*terms, *([] if running is None else [shift_layer(running, -1)]))
            sums.append(running)
    mixture = hidden_stream + local.astype(jnp.float32)
    if running is not None:
        mixture = mixture + shift_layer(running, -1).astype(jnp.float32)
    return mixture.astype(jnp.bfloat16)


def solution(mesh):
    placed = (
        P(("fsdp", "expert"), None),
        P(),
        P(("fsdp", "expert"), None),
        P(("fsdp", "expert"), None),
        P(),
        P(("fsdp", "expert"), None),
        P(("fsdp", "expert"), None),
        P("expert", None, None),
        P("expert", None, None),
        P("expert", None, None),
    )
    return jax.shard_map(
        per_device,
        mesh=mesh,
        in_specs=placed,
        out_specs=P(("fsdp", "expert"), None),
        check_vma=False,
    )
```

```python
import functools
import math

import jax
import jax.numpy as jnp
from jax import lax
from jax.experimental import pallas as pl
from jax.experimental.pallas import tpu as pltpu
from jax.sharding import PartitionSpec as P

HEAD_DIM = 128
BOTH = ("fsdp", "expert")
VMEM = pl.BlockSpec(memory_space=pltpu.VMEM)
ANYWHERE = pl.BlockSpec(memory_space=pl.ANY)
NT = (((1,), (1,)), ((), ()))


def dot_nt(left, right):
    return lax.dot_general(left, right, NT, preferred_element_type=jnp.float32)


def rms_scale(inputs, scale_gain):
    mean_square = jnp.mean(inputs * inputs, axis=-1, keepdims=True)
    return inputs * lax.rsqrt(mean_square + 1e-06) * scale_gain


def by_head_kernel(in_ref, out_ref, by_head_ref):
    head_count = by_head_ref.shape[0]
    for head in range(head_count):
        for part in range(3):
            start = (part * head_count + head) * HEAD_DIM
            by_head_ref[head, :, part * HEAD_DIM : (part + 1) * HEAD_DIM] = in_ref[
                :, start : start + HEAD_DIM
            ]
        by_head_ref[head, :, 3 * HEAD_DIM :] = out_ref[:, head * HEAD_DIM : (head + 1) * HEAD_DIM]


def by_head_call(attention_in, attention_out):
    rows, width = attention_out.shape
    return pl.pallas_call(
        by_head_kernel,
        out_shape=jax.ShapeDtypeStruct((width // HEAD_DIM, rows, 4 * HEAD_DIM), jnp.bfloat16),
        in_specs=[VMEM] * 2,
        out_specs=VMEM,
        compiler_params=pltpu.CompilerParams(vmem_limit_bytes=12 * 2**20),
        cost_estimate=pl.CostEstimate(
            flops=0, bytes_accessed=16 * rows * width, transcendentals=0
        ),
    )(attention_in, attention_out)


def attention_kernel(block_count, piece_count, *refs):
    layer_ref = refs[0]
    block_refs = refs[1 : 1 + block_count]
    piece_refs = refs[1 + block_count : 1 + block_count + piece_count]
    part_ref, weight_ref = refs[-2:]
    rows = block_refs[0].shape[0]
    sides, span, columns = piece_refs[0].shape
    for index, piece_ref in enumerate(piece_refs):
        layer = lax.rem(layer_ref[0] + index, piece_count)
        for side in range(sides):
            start = (side * piece_count + layer) * span
            weight_ref[pl.ds(pl.multiple_of(start, 16), span), :] = piece_ref[side]
    in_weights = weight_ref[:, : 3 * HEAD_DIM]
    out_weights = weight_ref[:, 3 * HEAD_DIM :]
    causal = lax.broadcasted_iota(jnp.int32, (rows, rows), 0) >= lax.broadcasted_iota(
        jnp.int32, (rows, rows), 1
    )
    for first in range(0, block_count, 2):
        pair = jnp.concatenate([block_refs[first][...], block_refs[first + 1][...]], axis=0)
        projected = jnp.dot(pair, in_weights, preferred_element_type=jnp.float32)
        projected = projected.astype(jnp.bfloat16)
        heads = []
        for which in range(2):
            own = projected[which * rows : (which + 1) * rows]
            queries = own[:, :HEAD_DIM]
            keys = own[:, HEAD_DIM : 2 * HEAD_DIM]
            values = own[:, 2 * HEAD_DIM :]
            scores = dot_nt(queries, keys) * (1.0 / math.sqrt(HEAD_DIM))
            raised = jnp.where(causal, jnp.exp(jnp.where(causal, scores, 0.0)), 0.0)
            probs = raised / jnp.sum(raised, axis=-1, keepdims=True)
            heads.append(
                jnp.dot(
                    probs.astype(jnp.bfloat16), values, preferred_element_type=jnp.float32
                ).astype(jnp.bfloat16)
            )
        part = dot_nt(jnp.concatenate(heads, axis=0), out_weights).astype(jnp.bfloat16)
        for which in range(2):
            part_ref[first + which] = part[which * rows : (which + 1) * rows]


def attention_call(layer, blocks, pieces, after):
    count = len(blocks)
    rows, width = blocks[0].shape
    tokens = count * rows
    return pl.pallas_call(
        functools.partial(attention_kernel, count, len(pieces)),
        out_shape=jax.ShapeDtypeStruct((count, rows, width), jnp.bfloat16),
        in_specs=[pl.BlockSpec(memory_space=pltpu.SMEM)]
        + [VMEM] * (count + len(pieces))
        + [ANYWHERE] * len(after),
        out_specs=VMEM,
        scratch_shapes=[pltpu.VMEM((width, 4 * HEAD_DIM), jnp.bfloat16)],
        compiler_params=pltpu.CompilerParams(vmem_limit_bytes=20 * 2**20),
        cost_estimate=pl.CostEstimate(
            flops=2 * tokens * (width * 4 * HEAD_DIM + 2 * rows * HEAD_DIM),
            bytes_accessed=4 * tokens * width + width * 8 * HEAD_DIM,
            transcendentals=tokens * rows,
        ),
    )(layer, *blocks, *pieces, *after)


def sum_kernel(picks, *refs):
    out_ref = refs[-1]
    total = None
    for ref, pick in zip(refs, picks):
        term = (ref[...] if pick is None else ref[pick]).astype(jnp.float32)
        total = term if total is None else total + term
    out_ref[...] = total.astype(out_ref.dtype)


def sum_call(terms, after=()):
    arrays = [term[0] if isinstance(term, tuple) else term for term in terms]
    picks = [term[1] if isinstance(term, tuple) else None for term in terms]
    shape = arrays[0].shape if picks[0] is None else arrays[0].shape[1:]
    return pl.pallas_call(
        functools.partial(sum_kernel, picks),
        out_shape=jax.ShapeDtypeStruct(shape, jnp.bfloat16),
        in_specs=[VMEM] * len(arrays) + [ANYWHERE] * len(after),
        out_specs=VMEM,
        compiler_params=pltpu.CompilerParams(vmem_limit_bytes=12 * 2**20),
        cost_estimate=pl.CostEstimate(
            flops=len(arrays) * math.prod(shape),
            bytes_accessed=2 * (len(arrays) + 1) * math.prod(shape),
            transcendentals=0,
        ),
    )(*arrays, *after)


def stream_kernel(tokens_ref, gain_ref, top_ref, top_in_ref, low_ref, low_in_ref, hid_ref, out_ref):
    half = top_ref.shape[0]
    for first, own, other in ((0, top_ref, top_in_ref), (half, low_ref, low_in_ref)):
        rows = pl.ds(first, half)
        hidden = (
            tokens_ref[rows, :].astype(jnp.float32)
            + own[...].astype(jnp.float32)
            + other[...].astype(jnp.float32)
        )
        hid_ref[rows, :] = hidden
        out_ref[rows, :] = rms_scale(hidden, gain_ref[...]).astype(jnp.bfloat16)


def stream_call(tokens, gain, top, top_in, low, low_in):
    return pl.pallas_call(
        stream_kernel,
        out_shape=(
            jax.ShapeDtypeStruct(tokens.shape, jnp.float32),
            jax.ShapeDtypeStruct(tokens.shape, jnp.bfloat16),
        ),
        in_specs=[VMEM] * 6,
        out_specs=(VMEM, VMEM),
        compiler_params=pltpu.CompilerParams(vmem_limit_bytes=12 * 2**20),
        cost_estimate=pl.CostEstimate(
            flops=6 * tokens.size, bytes_accessed=12 * tokens.size, transcendentals=0
        ),
    )(tokens, gain[None, :], top, top_in, low, low_in)


def expert_kernel(tiles, *refs):
    block_refs = refs[:4]
    scale_ref, gate_ref, up_ref, down_ref = refs[4:8]
    own_ref, side_ref, send_ref = refs[-3:]
    inputs = jnp.concatenate([ref[...] for ref in block_refs], axis=0)
    total = None
    for start, size in tiles:
        gate_value = dot_nt(inputs, gate_ref[start : start + size, :])
        up_value = dot_nt(inputs, up_ref[start : start + size, :])
        inner = (gate_value / (1.0 + jnp.exp(-gate_value)) * up_value).astype(jnp.bfloat16)
        term = jnp.dot(inner, down_ref[start : start + size, :], preferred_element_type=jnp.float32)
        total = term if total is None else total + term
    scale = scale_ref[...]
    result = jnp.where(scale > 0, total * scale, 0.0).astype(jnp.bfloat16)
    rows = block_refs[0].shape[0]
    own_ref[...] = result[:rows]
    side_ref[...] = result[rows : 2 * rows]
    send_ref[0] = result[2 * rows : 3 * rows]
    send_ref[1] = result[3 * rows :]


def expert_call(blocks, scale, gate_rows, up_rows, down_rows, after):
    rows, width = blocks[0].shape
    hidden = gate_rows.shape[0]
    tiles = [(start, min(256, hidden - start)) for start in range(0, hidden, 256)]
    one = jax.ShapeDtypeStruct((rows, width), jnp.bfloat16)
    two = jax.ShapeDtypeStruct((2, rows, width), jnp.bfloat16)
    return pl.pallas_call(
        functools.partial(expert_kernel, tiles),
        out_shape=(one, one, two),
        in_specs=[VMEM] * 8 + [ANYWHERE] * len(after),
        out_specs=(VMEM, VMEM, VMEM),
        compiler_params=pltpu.CompilerParams(vmem_limit_bytes=24 * 2**20),
        cost_estimate=pl.CostEstimate(
            flops=2 * 4 * rows * width * hidden * 3,
            bytes_accessed=6 * hidden * width + 16 * rows * width,
            transcendentals=4 * rows * hidden,
        ),
    )(*blocks, scale, gate_rows, up_rows, down_rows, *after)


def per_device(
    tokens,
    attention_gain,
    attention_in,
    attention_out,
    expert_gain,
    routes,
    route_weights,
    gate_weight,
    up_weight,
    down_weight,
):
    fsdp_size = lax.axis_size("fsdp")
    expert_size = lax.axis_size("expert")
    row_count, model_width = tokens.shape
    weight_rows, head_width = attention_out.shape
    head_count = head_width // HEAD_DIM
    layers = expert_size // 4

    def swap_pair(value):
        return lax.ppermute(value, "fsdp", [(f, f ^ 1) for f in range(fsdp_size)])

    def swap_side(value):
        return lax.ppermute(value, "expert", [(e, e ^ 2) for e in range(expert_size)])

    def swap_core(value):
        return lax.ppermute(value, "expert", [(e, e ^ 1) for e in range(expert_size)])

    def shift_layer(value, step):
        return lax.ppermute(
            value, "expert", [(e, (e + 4 * step) % expert_size) for e in range(expert_size)]
        )

    my_expert = lax.axis_index("expert")
    chosen = routes[:, :, None] == jnp.arange(expert_size, dtype=jnp.int32)
    scale_map = jnp.sum(jnp.where(chosen, route_weights[:, :, None], 0.0), axis=1).T[None]
    scale_map = jnp.concatenate([scale_map, swap_side(scale_map)], axis=0)
    scale_map = jnp.concatenate([scale_map, swap_core(scale_map)], axis=0)
    scales = [
        lax.dynamic_index_in_dim(
            scale_map if step == 0 else shift_layer(scale_map, -step),
            my_expert,
            axis=1,
            keepdims=False,
        ).reshape(4 * row_count, 1)
        for step in range(layers)
    ]

    by_head = by_head_call(attention_in, attention_out)
    if fsdp_size == 2 and weight_rows % 16 == 0:
        groups = [
            [f * expert_size + 4 * layer + e for f in range(2) for e in range(4)]
            for layer in range(layers)
        ]
        piece = lax.all_to_all(
            by_head, BOTH, split_axis=0, concat_axis=0, axis_index_groups=groups, tiled=True
        ).reshape(2, 4 * weight_rows, 4 * HEAD_DIM)
        pieces = [piece]
        for _ in range(1, layers):
            piece = shift_layer(piece, -1)
            pieces.append(piece)
    else:
        outgoing = jnp.broadcast_to(
            by_head.reshape(1, 2, 1, 4, weight_rows, 4 * HEAD_DIM),
            (fsdp_size // 2, 2, layers, 4, weight_rows, 4 * HEAD_DIM),
        ).reshape(fsdp_size * expert_size, weight_rows, 4 * HEAD_DIM)
        head_weights = lax.all_to_all(outgoing, BOTH, split_axis=0, concat_axis=0, tiled=True)
        pieces = [head_weights.reshape(1, model_width, 4 * HEAD_DIM)]

    normed = rms_scale(tokens.astype(jnp.float32), attention_gain).astype(jnp.bfloat16)
    blocks = [normed, swap_pair(normed)]
    blocks += [swap_side(block) for block in blocks]
    blocks += [swap_core(block) for block in blocks]
    layer_index = (my_expert // 4).astype(jnp.int32).reshape(1)
    send = attention_call(layer_index, blocks[4:], pieces, scales)
    keep = attention_call(layer_index, blocks[:4], pieces, [send])

    def added(*terms):
        total = terms[0].astype(jnp.float32)
        for term in terms[1:]:
            total = total + term.astype(jnp.float32)
        return total.astype(jnp.bfloat16)

    half = row_count // 2
    summed = added(keep, swap_core(send)).reshape(2, 2, row_count, model_width)
    top = added(summed[0, :, :half], swap_side(summed[1, :, :half]))
    low = added(summed[:, 0, half:], swap_pair(summed[:, 1, half:]))
    hidden_stream, expert_in = stream_call(
        tokens, expert_gain, top[0], swap_pair(top[1]), low[0], swap_side(low[1])
    )

    gate_rows = gate_weight[0].T
    up_rows = up_weight[0].T
    down_rows = down_weight[0]
    held = [expert_in]
    for _ in range(1, layers):
        held.append(shift_layer(held[-1], -1))
    sides = [swap_side(item) for item in held]
    running = pending = local = None
    older = []
    for step in range(layers):
        blocks = [held[step], sides[step]]
        blocks += [swap_core(item) for item in blocks]
        after = sides[step + 1 : step + 2] + older
        own, side, send = expert_call(blocks, scales[step], gate_rows, up_rows, down_rows, after)
        arrived = swap_core(send)
        crossing = sum_call([side, (arrived, 1)])
        older = [crossing]
        if pending is not None:
            running = sum_call(pending, [crossing])
            older.append(running)
        terms = [own, (arrived, 0), swap_side(crossing)]
        if step == 0:
            local = [own, arrived[0], terms[2]]
        else:
            if step == 1:
                older.append(local[2])
            pending = terms + ([] if running is None else [shift_layer(running, -1)])
    if pending is not None:
        local.append(shift_layer(sum_call(pending), -1))
    mixture = hidden_stream
    for term in local:
        mixture = mixture + term.astype(jnp.float32)
    return mixture.astype(jnp.bfloat16)


def solution(mesh):
    placed = (
        P(("fsdp", "expert"), None),
        P(),
        P(("fsdp", "expert"), None),
        P(("fsdp", "expert"), None),
        P(),
        P(("fsdp", "expert"), None),
        P(("fsdp", "expert"), None),
        P("expert", None, None),
        P("expert", None, None),
        P("expert", None, None),
    )
    return jax.shard_map(
        per_device,
        mesh=mesh,
        in_specs=placed,
        out_specs=P(("fsdp", "expert"), None),
        check_vma=False,
    )
```

```python
import functools
import math

import jax
import jax.numpy as jnp
from jax import lax
from jax.experimental import pallas as pl
from jax.experimental.pallas import tpu as pltpu
from jax.sharding import PartitionSpec as P

HEAD_DIM = 128
BOTH = ("fsdp", "expert")
VMEM = pl.BlockSpec(memory_space=pltpu.VMEM)
SMEM = pl.BlockSpec(memory_space=pltpu.SMEM)
ANYWHERE = pl.BlockSpec(memory_space=pl.ANY)
NT = (((1,), (1,)), ((), ()))


def dot_nt(left, right):
    return lax.dot_general(left, right, NT, preferred_element_type=jnp.float32)


def rms_scale(inputs, scale_gain):
    mean_square = jnp.mean(inputs * inputs, axis=-1, keepdims=True)
    return inputs * lax.rsqrt(mean_square + 1e-06) * scale_gain


def limit(mebibytes):
    return pltpu.CompilerParams(vmem_limit_bytes=mebibytes * 2**20)


def chip_weights_kernel(layers, in_ref, out_ref, sent_ref):
    head_count = out_ref.shape[1] // HEAD_DIM
    pairs = []
    for pair in range(head_count // 2):
        parts = []
        for head in (2 * pair, 2 * pair + 1):
            for part in range(3):
                start = (part * head_count + head) * HEAD_DIM
                parts.append(in_ref[:, start : start + HEAD_DIM])
        parts.append(out_ref[:, 2 * pair * HEAD_DIM : (2 * pair + 2) * HEAD_DIM])
        pairs.append(jnp.concatenate(parts, axis=1))
    for chip in range(sent_ref.shape[0]):
        sent_ref[chip] = pairs[(chip // (2 * layers)) % 2 * 2 + chip % 2]


def chip_weights_call(layers, chips, attention_in, attention_out):
    rows = attention_in.shape[0]
    return pl.pallas_call(
        functools.partial(chip_weights_kernel, layers),
        out_shape=jax.ShapeDtypeStruct((chips, rows, 8 * HEAD_DIM), jnp.bfloat16),
        in_specs=[VMEM] * 2,
        out_specs=VMEM,
        compiler_params=limit(12),
        cost_estimate=pl.CostEstimate(
            flops=0, bytes_accessed=16 * chips * rows * HEAD_DIM, transcendentals=0
        ),
    )(attention_in, attention_out)


def attention_kernel(block_count, piece_count, *refs):
    core_ref = refs[0]
    block_refs = refs[1 : 1 + block_count]
    piece_refs = refs[1 + block_count : 1 + block_count + piece_count]
    keep_top_ref, send_top_ref, keep_low_ref, send_low_ref, weight_ref = refs[-5:]
    rows = block_refs[0].shape[0]
    half = rows // 2
    if piece_count == 1:
        weight_ref = piece_refs[0]
    else:
        chips, span, _ = piece_refs[0].shape
        for chip in range(chips):
            for index, piece_ref in enumerate(piece_refs):
                core = core_ref[0] if index == 0 else 1 - core_ref[0]
                start = pl.multiple_of((2 * chip + core) * span, 16)
                weight_ref[pl.ds(start, span), :] = piece_ref[chip]
    out_weights = weight_ref[:, 6 * HEAD_DIM :]
    causal = lax.broadcasted_iota(jnp.int32, (rows, rows), 0) >= lax.broadcasted_iota(
        jnp.int32, (rows, rows), 1
    )
    inputs = jnp.concatenate([ref[...] for ref in block_refs], axis=0)
    heads = []
    for head in range(2):
        projected = jnp.dot(
            inputs,
            weight_ref[:, 3 * head * HEAD_DIM : 3 * (head + 1) * HEAD_DIM],
            preferred_element_type=jnp.float32,
        ).astype(jnp.bfloat16)
        outs = []
        for block in range(block_count):
            own = projected[block * rows : (block + 1) * rows]
            queries = own[:, :HEAD_DIM]
            keys = own[:, HEAD_DIM : 2 * HEAD_DIM]
            values = own[:, 2 * HEAD_DIM :]
            scores = dot_nt(queries, keys) * (1.0 / math.sqrt(HEAD_DIM))
            raised = jnp.where(causal, jnp.exp(jnp.where(causal, scores, 0.0)), 0.0)
            probs = raised / jnp.sum(raised, axis=-1, keepdims=True)
            outs.append(
                jnp.dot(
                    probs.astype(jnp.bfloat16), values, preferred_element_type=jnp.float32
                ).astype(jnp.bfloat16)
            )
        heads.append(jnp.concatenate(outs, axis=0))
    part = dot_nt(jnp.concatenate(heads, axis=1), out_weights).astype(jnp.bfloat16)
    for block in range(block_count):
        across, along = block // 2, block % 2
        top = send_top_ref if across else keep_top_ref
        low = send_low_ref if along else keep_low_ref
        top[along] = part[block * rows : block * rows + half]
        low[across] = part[block * rows + half : (block + 1) * rows]


def attention_call(core, blocks, pieces, after):
    count = len(blocks)
    rows, width = blocks[0].shape
    tokens = count * rows
    out = jax.ShapeDtypeStruct((count // 2, rows // 2, width), jnp.bfloat16)
    return pl.pallas_call(
        functools.partial(attention_kernel, count, len(pieces)),
        out_shape=(out,) * 4,
        in_specs=[SMEM] + [VMEM] * (count + len(pieces)) + [ANYWHERE] * len(after),
        out_specs=(VMEM,) * 4,
        scratch_shapes=[
            pltpu.VMEM((width, 8 * HEAD_DIM) if len(pieces) > 1 else (16, 128), jnp.bfloat16)
        ],
        compiler_params=limit(24),
        cost_estimate=pl.CostEstimate(
            flops=4 * tokens * (width * 4 * HEAD_DIM + 2 * rows * HEAD_DIM),
            bytes_accessed=4 * tokens * width + width * 16 * HEAD_DIM,
            transcendentals=2 * tokens * rows,
        ),
    )(core, *blocks, *pieces, *after)


def sum_kernel(picks, *refs):
    out_ref = refs[-1]
    total = None
    for ref, pick in zip(refs, picks):
        term = (ref[...] if pick is None else ref[pick]).astype(jnp.float32)
        total = term if total is None else total + term
    out_ref[...] = total.astype(out_ref.dtype)


def sum_call(terms, after=()):
    arrays = [term[0] if isinstance(term, tuple) else term for term in terms]
    picks = [term[1] if isinstance(term, tuple) else None for term in terms]
    shape = arrays[0].shape if picks[0] is None else arrays[0].shape[1:]
    return pl.pallas_call(
        functools.partial(sum_kernel, picks),
        out_shape=jax.ShapeDtypeStruct(shape, jnp.bfloat16),
        in_specs=[VMEM] * len(arrays) + [ANYWHERE] * len(after),
        out_specs=VMEM,
        compiler_params=limit(12),
        cost_estimate=pl.CostEstimate(
            flops=len(arrays) * math.prod(shape),
            bytes_accessed=2 * (len(arrays) + 1) * math.prod(shape),
            transcendentals=0,
        ),
    )(*arrays, *after)


def stream_kernel(tokens_ref, gain_ref, *refs):
    hidden_ref, normed_ref = refs[-2:]
    half = tokens_ref.shape[0] // 2
    for index in range(2):
        keep_ref, near_ref, far_ref = refs[3 * index : 3 * index + 3]
        rows = pl.ds(index * half, half)
        hidden = (
            tokens_ref[rows, :].astype(jnp.float32)
            + keep_ref[0].astype(jnp.float32)
            + near_ref[0].astype(jnp.float32)
            + far_ref[...].astype(jnp.float32)
        )
        hidden_ref[rows, :] = hidden
        normed_ref[rows, :] = rms_scale(hidden, gain_ref[...]).astype(jnp.bfloat16)


def stream_call(tokens, gain, *parts):
    return pl.pallas_call(
        stream_kernel,
        out_shape=(
            jax.ShapeDtypeStruct(tokens.shape, jnp.float32),
            jax.ShapeDtypeStruct(tokens.shape, jnp.bfloat16),
        ),
        in_specs=[VMEM] * 8,
        out_specs=(VMEM, VMEM),
        compiler_params=limit(12),
        cost_estimate=pl.CostEstimate(
            flops=6 * tokens.size, bytes_accessed=14 * tokens.size, transcendentals=0
        ),
    )(tokens, gain[None, :], *parts)


def expert_kernel(tiles, *refs):
    block_refs = refs[:2]
    scale_refs = refs[2:4]
    expert_refs = refs[4:10]
    pass_ref = refs[10]
    own_ref, side_ref, passed_ref = refs[-3:]
    inputs = jnp.concatenate([ref[...] for ref in block_refs], axis=0)
    result = None
    for expert in range(2):
        gate_ref, up_ref, down_ref = expert_refs[3 * expert : 3 * expert + 3]
        total = None
        for start, size in tiles:
            gate_value = dot_nt(inputs, gate_ref[start : start + size, :])
            up_value = dot_nt(inputs, up_ref[start : start + size, :])
            inner = (gate_value / (1.0 + jnp.exp(-gate_value)) * up_value).astype(jnp.bfloat16)
            term = jnp.dot(
                inner, down_ref[start : start + size, :], preferred_element_type=jnp.float32
            )
            total = term if total is None else total + term
        total = total * scale_refs[expert][...]
        result = total if result is None else result + total
    result = result.astype(jnp.bfloat16)
    rows = block_refs[0].shape[0]
    own_ref[...] = result[:rows]
    side_ref[...] = result[rows:]
    passed_ref[...] = pass_ref[...]


def expert_call(blocks, scales, experts, passed, after):
    rows, width = blocks[0].shape
    hidden = experts[0].shape[0]
    tiles = [(start, min(256, hidden - start)) for start in range(0, hidden, 256)]
    one = jax.ShapeDtypeStruct((rows, width), jnp.bfloat16)
    return pl.pallas_call(
        functools.partial(expert_kernel, tiles),
        out_shape=(one,) * 3,
        in_specs=[VMEM] * 11 + [ANYWHERE] * len(after),
        out_specs=(VMEM,) * 3,
        compiler_params=limit(24),
        cost_estimate=pl.CostEstimate(
            flops=2 * 4 * rows * width * hidden * 3,
            bytes_accessed=12 * hidden * width + 12 * rows * width,
            transcendentals=4 * rows * hidden,
        ),
    )(*blocks, *scales, *experts, passed, *after)


def per_device(
    tokens,
    attention_gain,
    attention_in,
    attention_out,
    expert_gain,
    routes,
    route_weights,
    gate_weight,
    up_weight,
    down_weight,
):
    fsdp_size = lax.axis_size("fsdp")
    expert_size = lax.axis_size("expert")
    row_count, model_width = tokens.shape
    weight_rows = attention_out.shape[0]
    layers = expert_size // 4

    def swap_pair(value):
        return lax.ppermute(value, "fsdp", [(f, f ^ 1) for f in range(fsdp_size)])

    def swap_expert(value, mask):
        return lax.ppermute(value, "expert", [(e, e ^ mask) for e in range(expert_size)])

    def swap_core(value):
        return swap_expert(value, 1)

    def swap_side(value):
        return swap_expert(value, 2)

    def swap_layer(value, mask):
        return swap_expert(value, 4 * mask) if mask else value

    my_expert = lax.axis_index("expert")

    chips = fsdp_size * expert_size // 2
    sent = chip_weights_call(layers, chips, attention_in, attention_out)
    same_core = [[2 * chip + core for chip in range(chips)] for core in range(2)]
    got = lax.all_to_all(
        sent, BOTH, split_axis=0, concat_axis=0, axis_index_groups=same_core, tiled=True
    )
    pieces = [got, swap_core(got)]
    if weight_rows % 16:
        in_order = jnp.stack(pieces, axis=1)
        in_order = jnp.where(my_expert % 2 == 0, in_order, in_order[:, ::-1])
        pieces = [in_order.reshape(model_width, 8 * HEAD_DIM)]

    own_expert = [gate_weight[0].T, up_weight[0].T, down_weight[0]]
    other_expert = [swap_core(weight) for weight in own_expert]

    chosen = routes[:, :, None] == jnp.arange(expert_size, dtype=jnp.int32)
    scale_map = jnp.sum(jnp.where(chosen, route_weights[:, :, None], 0.0), axis=1).T[None]
    scale_map = jnp.concatenate([scale_map, swap_side(scale_map)], axis=0)
    scales = []
    for mask in range(layers):
        arrived = swap_layer(scale_map, mask)
        scales.append(
            [
                lax.dynamic_index_in_dim(arrived, expert, axis=1, keepdims=False).reshape(
                    2 * row_count, 1
                )
                for expert in (my_expert, my_expert ^ 1)
            ]
        )

    normed = rms_scale(tokens.astype(jnp.float32), attention_gain).astype(jnp.bfloat16)
    blocks = [normed, swap_pair(normed)]
    blocks += [swap_side(block) for block in blocks]
    core = (my_expert % 2).astype(jnp.int32).reshape(1)
    keep_top, send_top, keep_low, send_low = attention_call(
        core, blocks, pieces, [*other_expert, *[item for pair in scales for item in pair]]
    )

    near_top = swap_side(send_top)
    near_low = swap_pair(send_low)
    far_top = swap_pair(sum_call([(keep_top, 1), (near_top, 1)]))
    far_low = swap_side(sum_call([(keep_low, 1), (near_low, 1)]))
    hidden_stream, expert_in = stream_call(
        tokens, expert_gain, keep_top, near_top, far_top, keep_low, near_low, far_low
    )

    order = [0] + list(range(layers - 1, 0, -1))
    arrivals = [expert_in, *[swap_layer(expert_in, mask) for mask in order[1:2]]]
    held = expert_in
    parts, ready, finals = [], [], []
    for place, mask in enumerate(order):
        block = arrivals[place]
        own, crossing, held = expert_call(
            [block, swap_side(block)],
            scales[mask],
            own_expert + other_expert,
            held,
            ready[:1] if place == 1 else ready[max(place - 2, 0) : max(place - 1, 0)],
        )
        if place + 2 < layers:
            arrivals.append(swap_layer(held, order[place + 2]))
        crossed = swap_side(crossing)
        if place == 0:
            parts = [own, crossed]
            ready.append(crossed)
        else:
            total = sum_call([own, crossed], finals[place - 3 : place - 2] if place >= 3 else [])
            ready.append(total)
            finals.append(swap_layer(total, mask))
    mixture = hidden_stream
    for term in parts + finals:
        mixture = mixture + term.astype(jnp.float32)
    return mixture.astype(jnp.bfloat16)


def solution(mesh):
    placed = (
        P(("fsdp", "expert"), None),
        P(),
        P(("fsdp", "expert"), None),
        P(("fsdp", "expert"), None),
        P(),
        P(("fsdp", "expert"), None),
        P(("fsdp", "expert"), None),
        P("expert", None, None),
        P("expert", None, None),
        P("expert", None, None),
    )
    return jax.shard_map(
        per_device,
        mesh=mesh,
        in_specs=placed,
        out_specs=P(("fsdp", "expert"), None),
        check_vma=False,
    )
```

```python
import functools
import math

import jax
import jax.numpy as jnp
from jax import lax
from jax.experimental import pallas as pl
from jax.experimental.pallas import tpu as pltpu
from jax.sharding import PartitionSpec as P

HEAD_DIM = 128
BOTH = ("fsdp", "expert")
VMEM = pl.BlockSpec(memory_space=pltpu.VMEM)
SMEM = pl.BlockSpec(memory_space=pltpu.SMEM)
HBM = pl.BlockSpec(memory_space=pltpu.HBM)
ANYWHERE = pl.BlockSpec(memory_space=pl.ANY)
NT = (((1,), (1,)), ((), ()))


def dot_nt(left, right):
    return lax.dot_general(left, right, NT, preferred_element_type=jnp.float32)


def rms_scale(inputs, scale_gain):
    mean_square = jnp.mean(inputs * inputs, axis=-1, keepdims=True)
    return inputs * lax.rsqrt(mean_square + 1e-06) * scale_gain


def limit(mebibytes):
    return pltpu.CompilerParams(vmem_limit_bytes=mebibytes * 2**20)


def chip_weights_kernel(layers, in_ref, out_ref, sent_ref):
    head_count = out_ref.shape[1] // HEAD_DIM
    pairs = []
    for pair in range(head_count // 2):
        parts = []
        for head in (2 * pair, 2 * pair + 1):
            for part in range(3):
                start = (part * head_count + head) * HEAD_DIM
                parts.append(in_ref[:, start : start + HEAD_DIM])
        parts.append(out_ref[:, 2 * pair * HEAD_DIM : (2 * pair + 2) * HEAD_DIM])
        pairs.append(jnp.concatenate(parts, axis=1))
    for chip in range(sent_ref.shape[0]):
        sent_ref[chip] = pairs[(chip // (2 * layers)) % 2 * 2 + chip % 2]


def chip_weights_call(layers, chips, attention_in, attention_out):
    rows = attention_in.shape[0]
    return pl.pallas_call(
        functools.partial(chip_weights_kernel, layers),
        out_shape=jax.ShapeDtypeStruct((chips, rows, 8 * HEAD_DIM), jnp.bfloat16),
        in_specs=[VMEM] * 2,
        out_specs=VMEM,
        compiler_params=limit(12),
        cost_estimate=pl.CostEstimate(
            flops=0, bytes_accessed=16 * chips * rows * HEAD_DIM, transcendentals=0
        ),
    )(attention_in, attention_out)


def group_weights_kernel(place_ref, in_hbm, out_hbm, *refs):
    sent_refs = refs[:4]
    in_ref, out_ref, sems = refs[4:]
    copies = [
        pltpu.make_async_copy(in_hbm, in_ref, sems.at[0]),
        pltpu.make_async_copy(out_hbm, out_ref, sems.at[1]),
    ]
    for copy in copies:
        copy.start()
    for copy in copies:
        copy.wait()
    width = out_ref.shape[1]
    for index, sent_ref in enumerate(sent_refs):
        pair = (place_ref[0] ^ (index % 2)) * 2 + (place_ref[2] ^ (index // 2))
        start = pl.multiple_of(pair * (2 * HEAD_DIM), HEAD_DIM)
        for part in range(3):
            both = in_ref[:, pl.ds(pl.multiple_of(start + part * width, HEAD_DIM), 2 * HEAD_DIM)]
            for head in range(2):
                to = (3 * head + part) * HEAD_DIM
                sent_ref[:, to : to + HEAD_DIM] = both[:, head * HEAD_DIM : (head + 1) * HEAD_DIM]
        sent_ref[:, 6 * HEAD_DIM :] = out_ref[:, pl.ds(start, 2 * HEAD_DIM)]


def group_weights_call(place, attention_in, attention_out):
    rows = attention_in.shape[0]
    one = jax.ShapeDtypeStruct((rows, 8 * HEAD_DIM), jnp.bfloat16)
    return pl.pallas_call(
        group_weights_kernel,
        out_shape=(one,) * 4,
        in_specs=[SMEM, HBM, HBM],
        out_specs=(VMEM,) * 4,
        scratch_shapes=[
            pltpu.VMEM(attention_in.shape, jnp.bfloat16),
            pltpu.VMEM(attention_out.shape, jnp.bfloat16),
            pltpu.SemaphoreType.DMA((2,)),
        ],
        compiler_params=limit(8),
        cost_estimate=pl.CostEstimate(
            flops=0, bytes_accessed=128 * rows * HEAD_DIM, transcendentals=0
        ),
    )(place, attention_in, attention_out)


def attention_kernel(block_count, piece_count, *refs):
    place_ref = refs[0]
    block_refs = refs[1 : 1 + block_count]
    piece_refs = refs[1 + block_count : 1 + block_count + piece_count]
    keep_top_ref, send_top_ref, keep_low_ref, send_low_ref, weight_ref = refs[-5:]
    rows = block_refs[0].shape[0]
    half = rows // 2
    if piece_count == 1:
        weight_ref = piece_refs[0]
    else:
        layers = piece_count // 2
        for index, piece_ref in enumerate(piece_refs):
            layer, core = place_ref[1] ^ (index // 2), place_ref[3] ^ (index % 2)
            for chip in range(4):
                pair, side = place_ref[0] ^ (chip % 2), place_ref[2] ^ (chip // 2)
                device = ((pair * layers + layer) * 2 + side) * 2 + core
                span = piece_ref.shape[1]
                start = pl.multiple_of(device * span, 16)
                weight_ref[pl.ds(start, span), :] = piece_ref[chip]
    out_weights = weight_ref[:, 6 * HEAD_DIM :]
    causal = lax.broadcasted_iota(jnp.int32, (rows, rows), 0) >= lax.broadcasted_iota(
        jnp.int32, (rows, rows), 1
    )
    inputs = jnp.concatenate([ref[...] for ref in block_refs], axis=0)
    heads = []
    for head in range(2):
        projected = jnp.dot(
            inputs,
            weight_ref[:, 3 * head * HEAD_DIM : 3 * (head + 1) * HEAD_DIM],
            preferred_element_type=jnp.float32,
        ).astype(jnp.bfloat16)
        outs = []
        for block in range(block_count):
            own = projected[block * rows : (block + 1) * rows]
            queries = own[:, :HEAD_DIM]
            keys = own[:, HEAD_DIM : 2 * HEAD_DIM]
            values = own[:, 2 * HEAD_DIM :]
            scores = dot_nt(queries, keys) * (1.0 / math.sqrt(HEAD_DIM))
            raised = jnp.where(causal, jnp.exp(jnp.where(causal, scores, 0.0)), 0.0)
            probs = raised / jnp.sum(raised, axis=-1, keepdims=True)
            outs.append(
                jnp.dot(
                    probs.astype(jnp.bfloat16), values, preferred_element_type=jnp.float32
                ).astype(jnp.bfloat16)
            )
        heads.append(jnp.concatenate(outs, axis=0))
    part = dot_nt(jnp.concatenate(heads, axis=1), out_weights).astype(jnp.bfloat16)
    for block in range(block_count):
        across, along = block // 2, block % 2
        top = send_top_ref if across else keep_top_ref
        low = send_low_ref if along else keep_low_ref
        top[along] = part[block * rows : block * rows + half]
        low[across] = part[block * rows + half : (block + 1) * rows]


def attention_call(place, blocks, pieces, after):
    count = len(blocks)
    rows, width = blocks[0].shape
    tokens = count * rows
    out = jax.ShapeDtypeStruct((count // 2, rows // 2, width), jnp.bfloat16)
    return pl.pallas_call(
        functools.partial(attention_kernel, count, len(pieces)),
        out_shape=(out,) * 4,
        in_specs=[SMEM] + [VMEM] * (count + len(pieces)) + [ANYWHERE] * len(after),
        out_specs=(VMEM,) * 4,
        scratch_shapes=[
            pltpu.VMEM((width, 8 * HEAD_DIM) if len(pieces) > 1 else (16, 128), jnp.bfloat16)
        ],
        compiler_params=limit(24),
        cost_estimate=pl.CostEstimate(
            flops=4 * tokens * (width * 4 * HEAD_DIM + 2 * rows * HEAD_DIM),
            bytes_accessed=4 * tokens * width + width * 16 * HEAD_DIM,
            transcendentals=2 * tokens * rows,
        ),
    )(place, *blocks, *pieces, *after)


def sum_kernel(picks, *refs):
    out_ref = refs[-1]
    total = None
    for ref, pick in zip(refs, picks):
        term = (ref[...] if pick is None else ref[pick]).astype(jnp.float32)
        total = term if total is None else total + term
    out_ref[...] = total.astype(out_ref.dtype)


def sum_call(terms, after=()):
    arrays = [term[0] if isinstance(term, tuple) else term for term in terms]
    picks = [term[1] if isinstance(term, tuple) else None for term in terms]
    shape = arrays[0].shape if picks[0] is None else arrays[0].shape[1:]
    return pl.pallas_call(
        functools.partial(sum_kernel, picks),
        out_shape=jax.ShapeDtypeStruct(shape, jnp.bfloat16),
        in_specs=[VMEM] * len(arrays) + [ANYWHERE] * len(after),
        out_specs=VMEM,
        compiler_params=limit(12),
        cost_estimate=pl.CostEstimate(
            flops=len(arrays) * math.prod(shape),
            bytes_accessed=2 * (len(arrays) + 1) * math.prod(shape),
            transcendentals=0,
        ),
    )(*arrays, *after)


def stream_kernel(tokens_ref, gain_ref, *refs):
    hidden_ref, normed_ref = refs[-2:]
    half = tokens_ref.shape[0] // 2
    for index in range(2):
        keep_ref, near_ref, far_ref = refs[3 * index : 3 * index + 3]
        rows = pl.ds(index * half, half)
        hidden = (
            tokens_ref[rows, :].astype(jnp.float32)
            + keep_ref[0].astype(jnp.float32)
            + near_ref[0].astype(jnp.float32)
            + far_ref[...].astype(jnp.float32)
        )
        hidden_ref[rows, :] = hidden
        normed_ref[rows, :] = rms_scale(hidden, gain_ref[...]).astype(jnp.bfloat16)


def stream_call(tokens, gain, *parts):
    return pl.pallas_call(
        stream_kernel,
        out_shape=(
            jax.ShapeDtypeStruct(tokens.shape, jnp.float32),
            jax.ShapeDtypeStruct(tokens.shape, jnp.bfloat16),
        ),
        in_specs=[VMEM] * 8,
        out_specs=(VMEM, VMEM),
        compiler_params=limit(12),
        cost_estimate=pl.CostEstimate(
            flops=6 * tokens.size, bytes_accessed=14 * tokens.size, transcendentals=0
        ),
    )(tokens, gain[None, :], *parts)


def expert_kernel(tiles, *refs):
    expert_ref = refs[0]
    block_refs = refs[1:3]
    scale_ref = refs[3]
    weight_refs = refs[4:10]
    own_ref, side_ref = refs[-2:]
    inputs = jnp.concatenate([ref[...] for ref in block_refs], axis=0)
    result = None
    for expert in range(2):
        gate_ref, up_ref, down_ref = weight_refs[3 * expert : 3 * expert + 3]
        scale = jnp.concatenate(
            [scale_ref[block, pl.ds(expert_ref[expert], 1), :] for block in range(2)], axis=1
        )
        for start, size in tiles:
            gate_value = dot_nt(gate_ref[start : start + size, :], inputs)
            up_value = dot_nt(up_ref[start : start + size, :], inputs)
            inner = gate_value / (1.0 + jnp.exp(-gate_value)) * (up_value * scale)
            term = lax.dot_general(
                inner.astype(jnp.bfloat16),
                down_ref[start : start + size, :],
                (((0,), (0,)), ((), ())),
                preferred_element_type=jnp.float32,
            )
            result = term if result is None else result + term
    result = result.astype(jnp.bfloat16)
    rows = block_refs[0].shape[0]
    own_ref[...] = result[:rows]
    side_ref[...] = result[rows:]


def expert_call(experts, blocks, scale_map, weights, after):
    rows, width = blocks[0].shape
    hidden = weights[0].shape[0]
    tiles = [(start, min(256, hidden - start)) for start in range(0, hidden, 256)]
    one = jax.ShapeDtypeStruct((rows, width), jnp.bfloat16)
    return pl.pallas_call(
        functools.partial(expert_kernel, tiles),
        out_shape=(one,) * 2,
        in_specs=[SMEM] + [VMEM] * 9 + [ANYWHERE] * len(after),
        out_specs=(VMEM,) * 2,
        compiler_params=limit(22),
        cost_estimate=pl.CostEstimate(
            flops=2 * 4 * rows * width * hidden * 3,
            bytes_accessed=12 * hidden * width + 8 * rows * width,
            transcendentals=4 * rows * hidden,
        ),
    )(experts, *blocks, scale_map, *weights, *after)


def per_device(
    tokens,
    attention_gain,
    attention_in,
    attention_out,
    expert_gain,
    routes,
    route_weights,
    gate_weight,
    up_weight,
    down_weight,
):
    fsdp_size = lax.axis_size("fsdp")
    expert_size = lax.axis_size("expert")
    row_count, model_width = tokens.shape
    weight_rows = attention_out.shape[0]
    layers = expert_size // 4

    def swap_pair(value):
        return lax.ppermute(value, "fsdp", [(f, f ^ 1) for f in range(fsdp_size)])

    def swap_expert(value, mask):
        return lax.ppermute(value, "expert", [(e, e ^ mask) for e in range(expert_size)])

    def swap_core(value):
        return swap_expert(value, 1)

    def swap_side(value):
        return swap_expert(value, 2)

    def swap_layer(value, mask):
        return swap_expert(value, 4 * mask) if mask else value

    hold = lax.optimization_barrier
    my_pair = lax.axis_index("fsdp").astype(jnp.int32)
    my_expert = lax.axis_index("expert").astype(jnp.int32)
    place = jnp.stack([my_pair, my_expert // 4, my_expert // 2 % 2, my_expert % 2])
    experts = jnp.stack([my_expert, my_expert ^ 1])
    chips = fsdp_size * expert_size // 2
    as_tree = fsdp_size == 2 and layers == 4 and weight_rows % 16 == 0

    own_expert = [gate_weight[0].T, up_weight[0].T, down_weight[0]]
    other_expert = [swap_core(weight) for weight in own_expert]

    chosen = routes[:, :, None] == jnp.arange(expert_size, dtype=jnp.int32)
    scale_map = jnp.sum(jnp.where(chosen, route_weights[:, :, None], 0.0), axis=1).T[None]
    scale_map = jnp.concatenate([scale_map, swap_side(scale_map)], axis=0)

    normed = rms_scale(tokens.astype(jnp.float32), attention_gain).astype(jnp.bfloat16)
    if as_tree:
        mine, by_pair, by_side, by_both = group_weights_call(place, attention_in, attention_out)
        both_ways = [
            (f * expert_size + e, (f ^ 1) * expert_size + (e ^ 2))
            for f in range(fsdp_size)
            for e in range(expert_size)
        ]
        rows_here = jnp.stack(
            [mine, swap_pair(by_pair), swap_side(by_side), lax.ppermute(by_both, BOTH, both_ways)]
        )
        rows_here, normed, scale_map = hold((rows_here, normed, scale_map))
        far = swap_layer(rows_here, 2)
        near = swap_layer(rows_here, 1)
        blocks = [normed, swap_pair(normed), swap_side(normed)]
        far, other_expert = hold((far, other_expert))
        pieces = []
        for piece in (rows_here, near, far, swap_layer(far, 1)):
            pieces += [piece, swap_core(piece)]
    else:
        sent = chip_weights_call(layers, chips, attention_in, attention_out)
        same_core = [[2 * chip + core for chip in range(chips)] for core in range(2)]
        got = lax.all_to_all(
            sent, BOTH, split_axis=0, concat_axis=0, axis_index_groups=same_core, tiled=True
        )
        in_order = jnp.stack([got, swap_core(got)], axis=1)
        in_order = jnp.where(my_expert % 2 == 0, in_order, in_order[:, ::-1])
        pieces = [in_order.reshape(model_width, 8 * HEAD_DIM)]
        blocks = [normed, swap_pair(normed), swap_side(normed)]
    blocks.append(swap_side(blocks[1]))
    keep_top, send_top, keep_low, send_low = attention_call(place, blocks, pieces, [])

    near_top = swap_side(send_top)
    near_low = swap_pair(send_low)
    scale_map, keep_top = hold((scale_map, keep_top))
    scale_maps = [swap_layer(scale_map, mask) for mask in range(layers)]
    far_top = swap_pair(sum_call([(keep_top, 1), (near_top, 1)]))
    far_low = swap_side(sum_call([(keep_low, 1), (near_low, 1)]))
    far_top, far_low, scale_maps = hold((far_top, far_low, scale_maps))
    hidden_stream, expert_in = stream_call(
        tokens, expert_gain, keep_top, near_top, far_top, keep_low, near_low, far_low
    )

    arrivals = {0: expert_in}
    order = [0] + sorted(range(1, layers), key=lambda mask: (mask == 1, mask))
    parts, ready, finals, crossings = [], [], [], []
    for step, mask in enumerate(order):
        low = mask & -mask
        block = swap_layer(arrivals[mask ^ low], low)
        if step > 0:
            block, _ = hold((block, crossings[0 if step == 1 else -2]))
        arrivals[mask] = block
        own, crossing = expert_call(
            experts,
            [block, swap_side(block)],
            scale_maps[mask],
            own_expert + other_expert,
            ready[:1] if step == 1 else ready[max(step - 2, 0) : max(step - 1, 0)],
        )
        crossings.append(crossing)
        crossed = swap_side(crossing)
        if step == 0:
            parts = [own, crossed]
            ready.append(crossed)
        else:
            total = sum_call([own, crossed], finals[step - 3 : step - 2] if step >= 3 else [])
            ready.append(total)
            finals.append(swap_layer(total, mask))
    mixture = hidden_stream
    for term in parts + finals:
        mixture = mixture + term.astype(jnp.float32)
    return mixture.astype(jnp.bfloat16)


def solution(mesh):
    placed = (
        P(("fsdp", "expert"), None),
        P(),
        P(("fsdp", "expert"), None),
        P(("fsdp", "expert"), None),
        P(),
        P(("fsdp", "expert"), None),
        P(("fsdp", "expert"), None),
        P("expert", None, None),
        P("expert", None, None),
        P("expert", None, None),
    )
    return jax.shard_map(
        per_device,
        mesh=mesh,
        in_specs=placed,
        out_specs=P(("fsdp", "expert"), None),
        check_vma=False,
    )
```

```python
import functools
import math

import jax
import jax.numpy as jnp
from jax import lax
from jax.experimental import pallas as pl
from jax.experimental.pallas import tpu as pltpu
from jax.sharding import PartitionSpec as P

HEAD_DIM = 128
BOTH = ("fsdp", "expert")
VMEM = pl.BlockSpec(memory_space=pltpu.VMEM)
SMEM = pl.BlockSpec(memory_space=pltpu.SMEM)
HBM = pl.BlockSpec(memory_space=pltpu.HBM)
ANYWHERE = pl.BlockSpec(memory_space=pl.ANY)
NT = (((1,), (1,)), ((), ()))


def dot_nt(left, right):
    return lax.dot_general(left, right, NT, preferred_element_type=jnp.float32)


def rms_scale(inputs, scale_gain):
    mean_square = jnp.mean(inputs * inputs, axis=-1, keepdims=True)
    return inputs * lax.rsqrt(mean_square + 1e-06) * scale_gain


def limit(mebibytes):
    return pltpu.CompilerParams(vmem_limit_bytes=mebibytes * 2**20)


def chip_weights_kernel(layers, in_ref, out_ref, sent_ref):
    head_count = out_ref.shape[1] // HEAD_DIM
    pairs = []
    for pair in range(head_count // 2):
        parts = []
        for head in (2 * pair, 2 * pair + 1):
            for part in range(3):
                start = (part * head_count + head) * HEAD_DIM
                parts.append(in_ref[:, start : start + HEAD_DIM])
        parts.append(out_ref[:, 2 * pair * HEAD_DIM : (2 * pair + 2) * HEAD_DIM])
        pairs.append(jnp.concatenate(parts, axis=1))
    for chip in range(sent_ref.shape[0]):
        sent_ref[chip] = pairs[(chip // (2 * layers)) % 2 * 2 + chip % 2]


def chip_weights_call(layers, chips, attention_in, attention_out):
    rows = attention_in.shape[0]
    return pl.pallas_call(
        functools.partial(chip_weights_kernel, layers),
        out_shape=jax.ShapeDtypeStruct((chips, rows, 8 * HEAD_DIM), jnp.bfloat16),
        in_specs=[VMEM] * 2,
        out_specs=VMEM,
        compiler_params=limit(12),
        cost_estimate=pl.CostEstimate(
            flops=0, bytes_accessed=16 * chips * rows * HEAD_DIM, transcendentals=0
        ),
    )(attention_in, attention_out)


def group_weights_kernel(place_ref, in_hbm, out_hbm, *refs):
    sent_refs = refs[:4]
    in_ref, out_ref, sems = refs[4:]
    copies = [
        pltpu.make_async_copy(in_hbm, in_ref, sems.at[0]),
        pltpu.make_async_copy(out_hbm, out_ref, sems.at[1]),
    ]
    for copy in copies:
        copy.start()
    for copy in copies:
        copy.wait()
    width = out_ref.shape[1]
    for index, sent_ref in enumerate(sent_refs):
        pair = (place_ref[0] ^ (index % 2)) * 2 + (place_ref[2] ^ (index // 2))
        start = pl.multiple_of(pair * (2 * HEAD_DIM), HEAD_DIM)
        for part in range(3):
            both = in_ref[:, pl.ds(pl.multiple_of(start + part * width, HEAD_DIM), 2 * HEAD_DIM)]
            for head in range(2):
                to = (3 * head + part) * HEAD_DIM
                sent_ref[:, to : to + HEAD_DIM] = both[:, head * HEAD_DIM : (head + 1) * HEAD_DIM]
        sent_ref[:, 6 * HEAD_DIM :] = out_ref[:, pl.ds(start, 2 * HEAD_DIM)]


def group_weights_call(place, attention_in, attention_out):
    rows = attention_in.shape[0]
    one = jax.ShapeDtypeStruct((rows, 8 * HEAD_DIM), jnp.bfloat16)
    return pl.pallas_call(
        group_weights_kernel,
        out_shape=(one,) * 4,
        in_specs=[SMEM, HBM, HBM],
        out_specs=(VMEM,) * 4,
        scratch_shapes=[
            pltpu.VMEM(attention_in.shape, jnp.bfloat16),
            pltpu.VMEM(attention_out.shape, jnp.bfloat16),
            pltpu.SemaphoreType.DMA((2,)),
        ],
        compiler_params=limit(8),
        cost_estimate=pl.CostEstimate(
            flops=0, bytes_accessed=128 * rows * HEAD_DIM, transcendentals=0
        ),
    )(place, attention_in, attention_out)


def attention_kernel(block_count, piece_count, *refs):
    place_ref, gain_ref = refs[:2]
    block_refs = refs[2 : 2 + block_count]
    piece_refs = refs[2 + block_count : 2 + block_count + piece_count]
    keep_top_ref, send_top_ref, keep_low_ref, send_low_ref, weight_ref = refs[-5:]
    rows = block_refs[0].shape[0]
    half = rows // 2
    if piece_count == 1:
        weight_ref = piece_refs[0]
    else:
        layers = piece_count // 2
        for index, piece_ref in enumerate(piece_refs):
            layer, core = place_ref[1] ^ (index // 2), place_ref[3] ^ (index % 2)
            for chip in range(4):
                pair, side = place_ref[0] ^ (chip % 2), place_ref[2] ^ (chip // 2)
                device = ((pair * layers + layer) * 2 + side) * 2 + core
                span = piece_ref.shape[1]
                start = pl.multiple_of(device * span, 16)
                weight_ref[pl.ds(start, span), :] = piece_ref[chip]
    out_weights = weight_ref[:, 6 * HEAD_DIM :]
    causal = lax.broadcasted_iota(jnp.int32, (rows, rows), 0) >= lax.broadcasted_iota(
        jnp.int32, (rows, rows), 1
    )
    inputs = jnp.concatenate(
        [
            rms_scale(ref[...].astype(jnp.float32), gain_ref[...]).astype(jnp.bfloat16)
            for ref in block_refs
        ],
        axis=0,
    )
    heads = []
    for head in range(2):
        projected = jnp.dot(
            inputs,
            weight_ref[:, 3 * head * HEAD_DIM : 3 * (head + 1) * HEAD_DIM],
            preferred_element_type=jnp.float32,
        ).astype(jnp.bfloat16)
        outs = []
        for block in range(block_count):
            own = projected[block * rows : (block + 1) * rows]
            queries = own[:, :HEAD_DIM]
            keys = own[:, HEAD_DIM : 2 * HEAD_DIM]
            values = own[:, 2 * HEAD_DIM :]
            scores = dot_nt(queries, keys) * (1.0 / math.sqrt(HEAD_DIM))
            raised = jnp.where(causal, jnp.exp(jnp.where(causal, scores, 0.0)), 0.0)
            probs = raised / jnp.sum(raised, axis=-1, keepdims=True)
            outs.append(
                jnp.dot(
                    probs.astype(jnp.bfloat16), values, preferred_element_type=jnp.float32
                ).astype(jnp.bfloat16)
            )
        heads.append(jnp.concatenate(outs, axis=0))
    part = dot_nt(jnp.concatenate(heads, axis=1), out_weights).astype(jnp.bfloat16)
    for block in range(block_count):
        across, along = block // 2, block % 2
        top = send_top_ref if across else keep_top_ref
        low = send_low_ref if along else keep_low_ref
        top[along] = part[block * rows : block * rows + half]
        low[across] = part[block * rows + half : (block + 1) * rows]


def attention_call(place, gain, blocks, pieces, after):
    count = len(blocks)
    rows, width = blocks[0].shape
    tokens = count * rows
    out = jax.ShapeDtypeStruct((count // 2, rows // 2, width), jnp.bfloat16)
    return pl.pallas_call(
        functools.partial(attention_kernel, count, len(pieces)),
        out_shape=(out,) * 4,
        in_specs=[SMEM] + [VMEM] * (1 + count + len(pieces)) + [ANYWHERE] * len(after),
        out_specs=(VMEM,) * 4,
        scratch_shapes=[
            pltpu.VMEM((width, 8 * HEAD_DIM) if len(pieces) > 1 else (16, 128), jnp.bfloat16)
        ],
        compiler_params=limit(16),
        cost_estimate=pl.CostEstimate(
            flops=4 * tokens * (width * 4 * HEAD_DIM + 2 * rows * HEAD_DIM),
            bytes_accessed=4 * tokens * width + width * 16 * HEAD_DIM,
            transcendentals=2 * tokens * rows,
        ),
    )(place, gain[None, :], *blocks, *pieces, *after)


def sum_kernel(picks, *refs):
    out_ref = refs[-1]
    total = None
    for ref, pick in zip(refs, picks):
        term = (ref[...] if pick is None else ref[pick]).astype(jnp.float32)
        total = term if total is None else total + term
    out_ref[...] = total.astype(out_ref.dtype)


def sum_call(terms, after=()):
    arrays = [term[0] if isinstance(term, tuple) else term for term in terms]
    picks = [term[1] if isinstance(term, tuple) else None for term in terms]
    shape = arrays[0].shape if picks[0] is None else arrays[0].shape[1:]
    return pl.pallas_call(
        functools.partial(sum_kernel, picks),
        out_shape=jax.ShapeDtypeStruct(shape, jnp.bfloat16),
        in_specs=[VMEM] * len(arrays) + [ANYWHERE] * len(after),
        out_specs=VMEM,
        compiler_params=limit(12),
        cost_estimate=pl.CostEstimate(
            flops=len(arrays) * math.prod(shape),
            bytes_accessed=2 * (len(arrays) + 1) * math.prod(shape),
            transcendentals=0,
        ),
    )(*arrays, *after)


def stream_kernel(tokens_ref, gain_ref, *refs):
    hidden_ref, normed_ref = refs[-2:]
    half = tokens_ref.shape[0] // 2
    for index in range(2):
        keep_ref, near_ref, far_ref = refs[3 * index : 3 * index + 3]
        rows = pl.ds(index * half, half)
        hidden = (
            tokens_ref[rows, :].astype(jnp.float32)
            + keep_ref[0].astype(jnp.float32)
            + near_ref[0].astype(jnp.float32)
            + far_ref[...].astype(jnp.float32)
        )
        hidden_ref[rows, :] = hidden
        normed_ref[rows, :] = rms_scale(hidden, gain_ref[...]).astype(jnp.bfloat16)


def stream_call(tokens, gain, *parts):
    return pl.pallas_call(
        stream_kernel,
        out_shape=(
            jax.ShapeDtypeStruct(tokens.shape, jnp.float32),
            jax.ShapeDtypeStruct(tokens.shape, jnp.bfloat16),
        ),
        in_specs=[VMEM] * 8,
        out_specs=(VMEM, VMEM),
        compiler_params=limit(12),
        cost_estimate=pl.CostEstimate(
            flops=6 * tokens.size, bytes_accessed=14 * tokens.size, transcendentals=0
        ),
    )(tokens, gain[None, :], *parts)


def expert_kernel(tiles, *refs):
    expert_ref = refs[0]
    block_refs = refs[1:3]
    scale_ref = refs[3]
    weight_refs = refs[4:10]
    own_ref, side_ref = refs[-2:]
    inputs = jnp.concatenate([ref[...] for ref in block_refs], axis=0)
    result = None
    for expert in range(2):
        gate_ref, up_ref, down_ref = weight_refs[3 * expert : 3 * expert + 3]
        scale = jnp.concatenate(
            [scale_ref[block, pl.ds(expert_ref[expert], 1), :] for block in range(2)], axis=1
        )
        for start, size in tiles:
            gate_value = dot_nt(gate_ref[start : start + size, :], inputs)
            up_value = dot_nt(up_ref[start : start + size, :], inputs)
            inner = gate_value / (1.0 + jnp.exp(-gate_value)) * (up_value * scale)
            term = jnp.dot(
                down_ref[:, start : start + size],
                inner.astype(jnp.bfloat16),
                preferred_element_type=jnp.float32,
            )
            result = term if result is None else result + term
    result = result.astype(jnp.bfloat16)
    rows = block_refs[0].shape[0]
    own_ref[...] = result[:, :rows]
    side_ref[...] = result[:, rows:]


def expert_call(experts, blocks, scale_map, weights, after):
    rows, width = blocks[0].shape
    hidden = weights[0].shape[0]
    tiles = [(start, min(256, hidden - start)) for start in range(0, hidden, 256)]
    one = jax.ShapeDtypeStruct((width, rows), jnp.bfloat16)
    return pl.pallas_call(
        functools.partial(expert_kernel, tiles),
        out_shape=(one,) * 2,
        in_specs=[SMEM] + [VMEM] * 9 + [ANYWHERE] * len(after),
        out_specs=(VMEM,) * 2,
        compiler_params=limit(20),
        cost_estimate=pl.CostEstimate(
            flops=2 * 4 * rows * width * hidden * 3,
            bytes_accessed=12 * hidden * width + 8 * rows * width,
            transcendentals=4 * rows * hidden,
        ),
    )(experts, *blocks, scale_map, *weights, *after)


def turn_kernel(*refs):
    count = len(refs) // 2
    for source_ref, target_ref in zip(refs[:count], refs[-count:]):
        target_ref[...] = source_ref[...].T


def turn_call(arrays, after):
    return pl.pallas_call(
        turn_kernel,
        out_shape=[jax.ShapeDtypeStruct(array.shape[::-1], array.dtype) for array in arrays],
        in_specs=[VMEM] * len(arrays) + [ANYWHERE],
        out_specs=[VMEM] * len(arrays),
        compiler_params=limit(16),
        cost_estimate=pl.CostEstimate(
            flops=0, bytes_accessed=4 * sum(array.size for array in arrays), transcendentals=0
        ),
    )(*arrays, after)


def mix_kernel(hidden_ref, *refs):
    total = refs[0][...].astype(jnp.float32)
    for ref in refs[1:-1]:
        total = total + ref[...].astype(jnp.float32)
    refs[-1][...] = (hidden_ref[...] + total.T).astype(jnp.bfloat16)


def mix_call(hidden, terms):
    return pl.pallas_call(
        mix_kernel,
        out_shape=jax.ShapeDtypeStruct(hidden.shape, jnp.bfloat16),
        in_specs=[VMEM] * (1 + len(terms)),
        out_specs=VMEM,
        compiler_params=limit(12),
        cost_estimate=pl.CostEstimate(
            flops=(1 + len(terms)) * hidden.size,
            bytes_accessed=(6 + 2 * len(terms)) * hidden.size,
            transcendentals=0,
        ),
    )(hidden, *terms)


def per_device(
    tokens,
    attention_gain,
    attention_in,
    attention_out,
    expert_gain,
    routes,
    route_weights,
    gate_weight,
    up_weight,
    down_weight,
):
    fsdp_size = lax.axis_size("fsdp")
    expert_size = lax.axis_size("expert")
    row_count, model_width = tokens.shape
    weight_rows = attention_out.shape[0]
    layers = expert_size // 4

    def swap_pair(value):
        return lax.ppermute(value, "fsdp", [(f, f ^ 1) for f in range(fsdp_size)])

    def swap_expert(value, mask):
        return lax.ppermute(value, "expert", [(e, e ^ mask) for e in range(expert_size)])

    def swap_core(value):
        return swap_expert(value, 1)

    def swap_side(value):
        return swap_expert(value, 2)

    def swap_layer(value, mask):
        return swap_expert(value, 4 * mask) if mask else value

    hold = lax.optimization_barrier
    my_pair = lax.axis_index("fsdp").astype(jnp.int32)
    my_expert = lax.axis_index("expert").astype(jnp.int32)
    place = jnp.stack([my_pair, my_expert // 4, my_expert // 2 % 2, my_expert % 2])
    experts = jnp.stack([my_expert, my_expert ^ 1])
    chips = fsdp_size * expert_size // 2
    as_tree = fsdp_size == 2 and layers == 4 and weight_rows % 16 == 0

    blocks = [tokens, swap_pair(tokens), swap_side(tokens)]
    if as_tree:
        sent = group_weights_call(place, attention_in, attention_out)
        (mine, by_pair, by_side, by_both), blocks = hold((sent, blocks))
        both_ways = [
            (f * expert_size + e, (f ^ 1) * expert_size + (e ^ 2))
            for f in range(fsdp_size)
            for e in range(expert_size)
        ]
        rows_here = jnp.stack(
            [mine, swap_pair(by_pair), swap_side(by_side), lax.ppermute(by_both, BOTH, both_ways)]
        )
        far = swap_layer(rows_here, 2)
        near = swap_layer(rows_here, 1)
    else:
        sent = chip_weights_call(layers, chips, attention_in, attention_out)
        same_core = [[2 * chip + core for chip in range(chips)] for core in range(2)]
        got = lax.all_to_all(
            sent, BOTH, split_axis=0, concat_axis=0, axis_index_groups=same_core, tiled=True
        )
        in_order = jnp.stack([got, swap_core(got)], axis=1)
        in_order = jnp.where(my_expert % 2 == 0, in_order, in_order[:, ::-1])
        pieces = [in_order.reshape(model_width, 8 * HEAD_DIM)]

    own_expert = [gate_weight[0].T, up_weight[0].T, down_weight[0]]
    other_expert = [swap_core(weight) for weight in own_expert]

    if as_tree:
        far, near, other_expert, route_weights = hold((far, near, other_expert, route_weights))
        pieces = []
        for piece in (rows_here, near, far, swap_layer(far, 1)):
            pieces += [piece, swap_core(piece)]
    chosen = routes[:, :, None] == jnp.arange(expert_size, dtype=jnp.int32)
    scale_map = jnp.sum(jnp.where(chosen, route_weights[:, :, None], 0.0), axis=1).T[None]
    scale_map = jnp.concatenate([scale_map, swap_side(scale_map)], axis=0)

    blocks.append(swap_side(blocks[1]))
    keep_top, send_top, keep_low, send_low = attention_call(
        place, attention_gain, blocks, pieces, [scale_map]
    )

    near_top = swap_side(send_top)
    near_low = swap_pair(send_low)
    scale_map, keep_top = hold((scale_map, keep_top))
    scale_maps = [swap_layer(scale_map, mask) for mask in range(layers)]
    downs = list(turn_call([weights[2] for weights in (own_expert, other_expert)], keep_top))
    near_top, near_low, scale_maps, downs = hold((near_top, near_low, scale_maps, downs))
    experts_here = own_expert[:2] + downs[:1] + other_expert[:2] + downs[1:]
    far_top = swap_pair(sum_call([(keep_top, 1), (near_top, 1)]))
    far_low = swap_side(sum_call([(keep_low, 1), (near_low, 1)]))
    hidden_stream, expert_in = stream_call(
        tokens, expert_gain, keep_top, near_top, far_top, keep_low, near_low, far_low
    )

    arrivals = {0: expert_in}
    order = [0] + sorted(range(1, layers), key=lambda mask: (mask == 1, mask))
    parts, ready, finals, crossings = [], [], [], []
    for step, mask in enumerate(order):
        low = mask & -mask
        source = arrivals[mask ^ low]
        if mask == 1 and step >= 2:
            source, _ = hold((source, block))
        block = swap_layer(source, low)
        if step == 1:
            block, _ = hold((block, crossings[0]))
        arrivals[mask] = block
        own, crossing = expert_call(
            experts,
            [block, swap_side(block)],
            scale_maps[mask],
            experts_here,
            ready[:1] if step == 1 else ready[max(step - 2, 0) : max(step - 1, 0)] + crossings[-1:],
        )
        crossings.append(crossing)
        crossed = swap_side(crossing)
        if step == 0:
            parts = [own, crossed]
            ready.append(crossed)
        else:
            total = sum_call([own, crossed])
            ready.append(total)
            finals.append(swap_layer(total, mask))
    return mix_call(hidden_stream, parts + finals)


def solution(mesh):
    placed = (
        P(("fsdp", "expert"), None),
        P(),
        P(("fsdp", "expert"), None),
        P(("fsdp", "expert"), None),
        P(),
        P(("fsdp", "expert"), None),
        P(("fsdp", "expert"), None),
        P("expert", None, None),
        P("expert", None, None),
        P("expert", None, None),
    )
    return jax.shard_map(
        per_device,
        mesh=mesh,
        in_specs=placed,
        out_specs=P(("fsdp", "expert"), None),
        check_vma=False,
    )
```

```python
import functools
import math

import jax
import jax.numpy as jnp
from jax import lax
from jax.experimental import pallas as pl
from jax.experimental.pallas import tpu as pltpu
from jax.sharding import PartitionSpec as P

HEAD_DIM = 128
BOTH = ("fsdp", "expert")
VMEM = pl.BlockSpec(memory_space=pltpu.VMEM)
SMEM = pl.BlockSpec(memory_space=pltpu.SMEM)
HBM = pl.BlockSpec(memory_space=pltpu.HBM)
ANYWHERE = pl.BlockSpec(memory_space=pl.ANY)
NT = (((1,), (1,)), ((), ()))


def dot_nt(left, right):
    return lax.dot_general(left, right, NT, preferred_element_type=jnp.float32)


def rms_scale(inputs, scale_gain):
    mean_square = jnp.mean(inputs * inputs, axis=-1, keepdims=True)
    return inputs * lax.rsqrt(mean_square + 1e-06) * scale_gain


def limit(mebibytes):
    return pltpu.CompilerParams(vmem_limit_bytes=mebibytes * 2**20)


def chip_weights_kernel(layers, in_ref, out_ref, sent_ref):
    head_count = out_ref.shape[1] // HEAD_DIM
    pairs = []
    for pair in range(head_count // 2):
        parts = []
        for head in (2 * pair, 2 * pair + 1):
            for part in range(3):
                start = (part * head_count + head) * HEAD_DIM
                parts.append(in_ref[:, start : start + HEAD_DIM])
        parts.append(out_ref[:, 2 * pair * HEAD_DIM : (2 * pair + 2) * HEAD_DIM])
        pairs.append(jnp.concatenate(parts, axis=1))
    for chip in range(sent_ref.shape[0]):
        sent_ref[chip] = pairs[(chip // (2 * layers)) % 2 * 2 + chip % 2]


def chip_weights_call(layers, chips, attention_in, attention_out):
    rows = attention_in.shape[0]
    return pl.pallas_call(
        functools.partial(chip_weights_kernel, layers),
        out_shape=jax.ShapeDtypeStruct((chips, rows, 8 * HEAD_DIM), jnp.bfloat16),
        in_specs=[VMEM] * 2,
        out_specs=VMEM,
        compiler_params=limit(12),
        cost_estimate=pl.CostEstimate(
            flops=0, bytes_accessed=16 * chips * rows * HEAD_DIM, transcendentals=0
        ),
    )(attention_in, attention_out)


def group_weights_kernel(place_ref, in_hbm, out_hbm, *refs):
    sent_refs = refs[:4]
    in_ref, out_ref, sems = refs[4:]
    copies = [
        pltpu.make_async_copy(in_hbm, in_ref, sems.at[0]),
        pltpu.make_async_copy(out_hbm, out_ref, sems.at[1]),
    ]
    for copy in copies:
        copy.start()
    for copy in copies:
        copy.wait()
    width = out_ref.shape[1]
    for index, sent_ref in enumerate(sent_refs):
        pair = (place_ref[0] ^ (index % 2)) * 2 + (place_ref[2] ^ (index // 2))
        start = pl.multiple_of(pair * (2 * HEAD_DIM), HEAD_DIM)
        for part in range(3):
            both = in_ref[:, pl.ds(pl.multiple_of(start + part * width, HEAD_DIM), 2 * HEAD_DIM)]
            for head in range(2):
                to = (3 * head + part) * HEAD_DIM
                sent_ref[:, to : to + HEAD_DIM] = both[:, head * HEAD_DIM : (head + 1) * HEAD_DIM]
        sent_ref[:, 6 * HEAD_DIM :] = out_ref[:, pl.ds(start, 2 * HEAD_DIM)]


def group_weights_call(place, attention_in, attention_out):
    rows = attention_in.shape[0]
    one = jax.ShapeDtypeStruct((rows, 8 * HEAD_DIM), jnp.bfloat16)
    return pl.pallas_call(
        group_weights_kernel,
        out_shape=(one,) * 4,
        in_specs=[SMEM, HBM, HBM],
        out_specs=(VMEM,) * 4,
        scratch_shapes=[
            pltpu.VMEM(attention_in.shape, jnp.bfloat16),
            pltpu.VMEM(attention_out.shape, jnp.bfloat16),
            pltpu.SemaphoreType.DMA((2,)),
        ],
        compiler_params=limit(8),
        cost_estimate=pl.CostEstimate(
            flops=0, bytes_accessed=128 * rows * HEAD_DIM, transcendentals=0
        ),
    )(place, attention_in, attention_out)


def attention_kernel(block_count, piece_count, *refs):
    place_ref, gain_ref = refs[:2]
    block_refs = refs[2 : 2 + block_count]
    piece_refs = refs[2 + block_count : 2 + block_count + piece_count]
    keep_top_ref, send_top_ref, keep_low_ref, send_low_ref, weight_ref = refs[-5:]
    rows = block_refs[0].shape[0]
    half = rows // 2
    if piece_count == 1:
        weight_ref = piece_refs[0]
    else:
        layers = piece_count // 2
        for index, piece_ref in enumerate(piece_refs):
            layer, core = place_ref[1] ^ (index // 2), place_ref[3] ^ (index % 2)
            for chip in range(4):
                pair, side = place_ref[0] ^ (chip % 2), place_ref[2] ^ (chip // 2)
                device = ((pair * layers + layer) * 2 + side) * 2 + core
                span = piece_ref.shape[1]
                start = pl.multiple_of(device * span, 16)
                weight_ref[pl.ds(start, span), :] = piece_ref[chip]
    out_weights = weight_ref[:, 6 * HEAD_DIM :]
    causal = lax.broadcasted_iota(jnp.int32, (rows, rows), 0) >= lax.broadcasted_iota(
        jnp.int32, (rows, rows), 1
    )
    inputs = jnp.concatenate(
        [
            rms_scale(ref[...].astype(jnp.float32), gain_ref[...]).astype(jnp.bfloat16)
            for ref in block_refs
        ],
        axis=0,
    )
    heads = []
    for head in range(2):
        projected = jnp.dot(
            inputs,
            weight_ref[:, 3 * head * HEAD_DIM : 3 * (head + 1) * HEAD_DIM],
            preferred_element_type=jnp.float32,
        ).astype(jnp.bfloat16)
        outs = []
        for block in range(block_count):
            own = projected[block * rows : (block + 1) * rows]
            queries = own[:, :HEAD_DIM]
            keys = own[:, HEAD_DIM : 2 * HEAD_DIM]
            values = own[:, 2 * HEAD_DIM :]
            scores = dot_nt(queries, keys) * (1.0 / math.sqrt(HEAD_DIM))
            raised = jnp.where(causal, jnp.exp(jnp.where(causal, scores, 0.0)), 0.0)
            probs = raised / jnp.sum(raised, axis=-1, keepdims=True)
            outs.append(
                jnp.dot(
                    probs.astype(jnp.bfloat16), values, preferred_element_type=jnp.float32
                ).astype(jnp.bfloat16)
            )
        heads.append(jnp.concatenate(outs, axis=0))
    part = dot_nt(jnp.concatenate(heads, axis=1), out_weights).astype(jnp.bfloat16)
    for block in range(block_count):
        across, along = block // 2, block % 2
        top = send_top_ref if across else keep_top_ref
        low = send_low_ref if along else keep_low_ref
        top[along] = part[block * rows : block * rows + half]
        low[across] = part[block * rows + half : (block + 1) * rows]


def attention_call(place, gain, blocks, pieces, after):
    count = len(blocks)
    rows, width = blocks[0].shape
    tokens = count * rows
    out = jax.ShapeDtypeStruct((count // 2, rows // 2, width), jnp.bfloat16)
    return pl.pallas_call(
        functools.partial(attention_kernel, count, len(pieces)),
        out_shape=(out,) * 4,
        in_specs=[SMEM] + [VMEM] * (1 + count + len(pieces)) + [ANYWHERE] * len(after),
        out_specs=(VMEM,) * 4,
        scratch_shapes=[
            pltpu.VMEM((width, 8 * HEAD_DIM) if len(pieces) > 1 else (16, 128), jnp.bfloat16)
        ],
        compiler_params=limit(16),
        cost_estimate=pl.CostEstimate(
            flops=4 * tokens * (width * 4 * HEAD_DIM + 2 * rows * HEAD_DIM),
            bytes_accessed=4 * tokens * width + width * 16 * HEAD_DIM,
            transcendentals=2 * tokens * rows,
        ),
    )(place, gain[None, :], *blocks, *pieces, *after)


def sum_kernel(picks, *refs):
    out_ref = refs[-1]
    total = None
    for ref, pick in zip(refs, picks):
        term = (ref[...] if pick is None else ref[pick]).astype(jnp.float32)
        total = term if total is None else total + term
    out_ref[...] = total.astype(out_ref.dtype)


def sum_call(terms, after=()):
    arrays = [term[0] if isinstance(term, tuple) else term for term in terms]
    picks = [term[1] if isinstance(term, tuple) else None for term in terms]
    shape = arrays[0].shape if picks[0] is None else arrays[0].shape[1:]
    return pl.pallas_call(
        functools.partial(sum_kernel, picks),
        out_shape=jax.ShapeDtypeStruct(shape, jnp.bfloat16),
        in_specs=[VMEM] * len(arrays) + [ANYWHERE] * len(after),
        out_specs=VMEM,
        compiler_params=limit(12),
        cost_estimate=pl.CostEstimate(
            flops=len(arrays) * math.prod(shape),
            bytes_accessed=2 * (len(arrays) + 1) * math.prod(shape),
            transcendentals=0,
        ),
    )(*arrays, *after)


def stream_kernel(tokens_ref, gain_ref, *refs):
    hidden_ref, normed_ref = refs[-2:]
    half = tokens_ref.shape[0] // 2
    for index in range(2):
        keep_ref, near_ref, far_ref = refs[3 * index : 3 * index + 3]
        rows = pl.ds(index * half, half)
        hidden = (
            tokens_ref[rows, :].astype(jnp.float32)
            + keep_ref[0].astype(jnp.float32)
            + near_ref[0].astype(jnp.float32)
            + far_ref[...].astype(jnp.float32)
        )
        hidden_ref[rows, :] = hidden
        normed_ref[rows, :] = rms_scale(hidden, gain_ref[...]).astype(jnp.bfloat16)


def stream_call(tokens, gain, *parts):
    return pl.pallas_call(
        stream_kernel,
        out_shape=(
            jax.ShapeDtypeStruct(tokens.shape, jnp.float32),
            jax.ShapeDtypeStruct(tokens.shape, jnp.bfloat16),
        ),
        in_specs=[VMEM] * 8,
        out_specs=(VMEM, VMEM),
        compiler_params=limit(12),
        cost_estimate=pl.CostEstimate(
            flops=6 * tokens.size, bytes_accessed=14 * tokens.size, transcendentals=0
        ),
    )(tokens, gain[None, :], *parts)


def expert_kernel(tiles, *refs):
    expert_ref = refs[0]
    block_refs = refs[1:3]
    scale_ref = refs[3]
    weight_refs = refs[4:10]
    own_ref, side_ref, *held_refs, sems = refs[-6:]
    copies = []
    for expert in range(2):
        slot = iter(range(2 * len(tiles) + 1))
        downs = [
            pltpu.make_async_copy(
                weight_refs[3 * expert + 2], held_refs[2].at[expert], sems.at[expert, next(slot)]
            )
        ]
        pairs = [
            [
                pltpu.make_async_copy(
                    weight_refs[3 * expert + which].at[pl.ds(start, size)],
                    held_refs[which].at[expert, pl.ds(start, size)],
                    sems.at[expert, next(slot)],
                )
                for which in range(2)
            ]
            for start, size in tiles
        ]
        copies.append([pairs[0], downs, *pairs[1:]])
        for group in copies[-1]:
            for copy in group:
                copy.start()
    inputs = jnp.concatenate([ref[...] for ref in block_refs], axis=0)
    result = None
    for expert in range(2):
        gate_ref, up_ref, down_ref = [ref.at[expert] for ref in held_refs]
        first, downs, *others = copies[expert]
        pairs = [first, *others]
        scale = jnp.concatenate(
            [scale_ref[block, pl.ds(expert_ref[expert], 1), :] for block in range(2)], axis=1
        )
        for index, (start, size) in enumerate(tiles):
            pairs[index][0].wait()
            gate_value = dot_nt(gate_ref[start : start + size, :], inputs)
            pairs[index][1].wait()
            up_value = dot_nt(up_ref[start : start + size, :], inputs)
            inner = gate_value / (1.0 + jnp.exp(-gate_value)) * (up_value * scale)
            if index == 0:
                downs[0].wait()
            term = jnp.dot(
                down_ref[:, start : start + size],
                inner.astype(jnp.bfloat16),
                preferred_element_type=jnp.float32,
            )
            result = term if result is None else result + term
    result = result.astype(jnp.bfloat16)
    rows = block_refs[0].shape[0]
    own_ref[...] = result[:, :rows]
    side_ref[...] = result[:, rows:]


def expert_call(experts, blocks, scale_map, weights, after):
    rows, width = blocks[0].shape
    hidden = weights[0].shape[0]
    tiles = [(start, min(256, hidden - start)) for start in range(0, hidden, 256)]
    one = jax.ShapeDtypeStruct((width, rows), jnp.bfloat16)
    return pl.pallas_call(
        functools.partial(expert_kernel, tiles),
        out_shape=(one,) * 2,
        in_specs=[SMEM] + [VMEM] * 3 + [HBM] * 6 + [ANYWHERE] * len(after),
        out_specs=(VMEM,) * 2,
        scratch_shapes=[
            pltpu.VMEM((2, hidden, width), jnp.bfloat16),
            pltpu.VMEM((2, hidden, width), jnp.bfloat16),
            pltpu.VMEM((2, *weights[2].shape), jnp.bfloat16),
            pltpu.SemaphoreType.DMA((2, 2 * len(tiles) + 1)),
        ],
        compiler_params=limit(52),
        cost_estimate=pl.CostEstimate(
            flops=2 * 4 * rows * width * hidden * 3,
            bytes_accessed=12 * hidden * width + 8 * rows * width,
            transcendentals=4 * rows * hidden,
        ),
    )(experts, *blocks, scale_map, *weights, *after)


def turn_kernel(source_ref, *refs):
    target_ref = refs[-1]
    columns = source_ref.shape[0]
    target_ref[:, :columns] = source_ref[...].T
    if target_ref.shape[1] > columns:
        rest = (target_ref.shape[0], target_ref.shape[1] - columns)
        target_ref[:, columns:] = jnp.zeros(rest, target_ref.dtype)


def turn_call(array, after):
    rows, columns = array.shape
    return pl.pallas_call(
        turn_kernel,
        out_shape=jax.ShapeDtypeStruct((columns, -(-rows // 128) * 128), array.dtype),
        in_specs=[VMEM, ANYWHERE],
        out_specs=VMEM,
        compiler_params=limit(16),
        cost_estimate=pl.CostEstimate(
            flops=0, bytes_accessed=4 * array.size, transcendentals=0
        ),
    )(array, after)


def mix_kernel(hidden_ref, *refs):
    total = refs[0][...].astype(jnp.float32)
    for ref in refs[1:-1]:
        total = total + ref[...].astype(jnp.float32)
    refs[-1][...] = (hidden_ref[...] + total.T).astype(jnp.bfloat16)


def mix_call(hidden, terms):
    return pl.pallas_call(
        mix_kernel,
        out_shape=jax.ShapeDtypeStruct(hidden.shape, jnp.bfloat16),
        in_specs=[VMEM] * (1 + len(terms)),
        out_specs=VMEM,
        compiler_params=limit(12),
        cost_estimate=pl.CostEstimate(
            flops=(1 + len(terms)) * hidden.size,
            bytes_accessed=(6 + 2 * len(terms)) * hidden.size,
            transcendentals=0,
        ),
    )(hidden, *terms)


def per_device(
    tokens,
    attention_gain,
    attention_in,
    attention_out,
    expert_gain,
    routes,
    route_weights,
    gate_weight,
    up_weight,
    down_weight,
):
    fsdp_size = lax.axis_size("fsdp")
    expert_size = lax.axis_size("expert")
    row_count, model_width = tokens.shape
    weight_rows = attention_out.shape[0]
    layers = expert_size // 4

    def swap_pair(value):
        return lax.ppermute(value, "fsdp", [(f, f ^ 1) for f in range(fsdp_size)])

    def swap_expert(value, mask):
        return lax.ppermute(value, "expert", [(e, e ^ mask) for e in range(expert_size)])

    def swap_core(value):
        return swap_expert(value, 1)

    def swap_side(value):
        return swap_expert(value, 2)

    def swap_layer(value, mask):
        return swap_expert(value, 4 * mask) if mask else value

    hold = lax.optimization_barrier
    my_pair = lax.axis_index("fsdp").astype(jnp.int32)
    my_expert = lax.axis_index("expert").astype(jnp.int32)
    place = jnp.stack([my_pair, my_expert // 4, my_expert // 2 % 2, my_expert % 2])
    experts = jnp.stack([my_expert, my_expert ^ 1])
    chips = fsdp_size * expert_size // 2
    as_tree = fsdp_size == 2 and layers == 4 and weight_rows % 16 == 0

    blocks = [tokens, swap_pair(tokens), swap_side(tokens)]
    gate_rows, up_rows, down_rows = gate_weight[0].T, up_weight[0].T, down_weight[0]
    if as_tree:
        mine, by_pair, by_side, by_both = group_weights_call(place, attention_in, attention_out)
        both_ways = [
            (f * expert_size + e, (f ^ 1) * expert_size + (e ^ 2))
            for f in range(fsdp_size)
            for e in range(expert_size)
        ]
        rows_here = jnp.stack(
            [mine, swap_pair(by_pair), swap_side(by_side), lax.ppermute(by_both, BOTH, both_ways)]
        )
        rows_here, blocks, gate_rows, up_rows = hold((rows_here, blocks, gate_rows, up_rows))
        far = swap_layer(rows_here, 2)
        near = swap_layer(rows_here, 1)
        ordering = rows_here
    else:
        sent = chip_weights_call(layers, chips, attention_in, attention_out)
        same_core = [[2 * chip + core for chip in range(chips)] for core in range(2)]
        got = lax.all_to_all(
            sent, BOTH, split_axis=0, concat_axis=0, axis_index_groups=same_core, tiled=True
        )
        in_order = jnp.stack([got, swap_core(got)], axis=1)
        in_order = jnp.where(my_expert % 2 == 0, in_order, in_order[:, ::-1])
        pieces = [in_order.reshape(model_width, 8 * HEAD_DIM)]
        ordering = got
    blocks.append(swap_side(blocks[1]))
    downs = [turn_call(down_rows, ordering)]
    own_expert = [gate_rows, up_rows]
    other_expert = [swap_core(weight) for weight in own_expert]
    if as_tree:
        far, near, other_expert, route_weights, blocks, downs = hold(
            (far, near, other_expert, route_weights, blocks, downs)
        )
        pieces = []
        for piece in (rows_here, near, far, swap_layer(far, 1)):
            pieces += [piece, swap_core(piece)]
    downs.append(swap_core(downs[0]))
    experts_here = own_expert + downs[:1] + other_expert + downs[1:]

    chosen = routes[:, :, None] == jnp.arange(expert_size, dtype=jnp.int32)
    scale_map = jnp.sum(jnp.where(chosen, route_weights[:, :, None], 0.0), axis=1).T[None]
    scale_map = jnp.concatenate([scale_map, swap_side(scale_map)], axis=0)

    keep_top, send_top, keep_low, send_low = attention_call(
        place, attention_gain, blocks, pieces, [scale_map, downs[1]]
    )

    near_top = swap_side(send_top)
    near_low = swap_pair(send_low)
    scale_map, keep_top = hold((scale_map, keep_top))
    scale_maps = [swap_layer(scale_map, mask) for mask in range(layers)]
    near_top, near_low, scale_maps = hold((near_top, near_low, scale_maps))
    far_top = swap_pair(sum_call([(keep_top, 1), (near_top, 1)]))
    far_low = swap_side(sum_call([(keep_low, 1), (near_low, 1)]))
    hidden_stream, expert_in = stream_call(
        tokens, expert_gain, keep_top, near_top, far_top, keep_low, near_low, far_low
    )

    arrivals = {0: expert_in}
    order = [0] + sorted(range(1, layers), key=lambda mask: (mask == 1, mask))
    parts, ready, finals, crossings = [], [], [], []
    for step, mask in enumerate(order):
        low = mask & -mask
        source = arrivals[mask ^ low]
        if mask == 1 and step >= 2:
            source, _ = hold((source, block))
        block = swap_layer(source, low)
        if step == 1:
            block, _ = hold((block, crossings[0]))
        arrivals[mask] = block
        own, crossing = expert_call(
            experts,
            [block, swap_side(block)],
            scale_maps[mask],
            experts_here,
            ready[:1] if step == 1 else ready[max(step - 2, 0) : max(step - 1, 0)] + crossings[-1:],
        )
        crossings.append(crossing)
        crossed = swap_side(crossing)
        if step == 0:
            parts = [own, crossed]
            ready.append(crossed)
        else:
            total = sum_call([own, crossed])
            ready.append(total)
            finals.append(swap_layer(total, mask))
    return mix_call(hidden_stream, parts + finals)


def solution(mesh):
    placed = (
        P(("fsdp", "expert"), None),
        P(),
        P(("fsdp", "expert"), None),
        P(("fsdp", "expert"), None),
        P(),
        P(("fsdp", "expert"), None),
        P(("fsdp", "expert"), None),
        P("expert", None, None),
        P("expert", None, None),
        P("expert", None, None),
    )
    return jax.shard_map(
        per_device,
        mesh=mesh,
        in_specs=placed,
        out_specs=P(("fsdp", "expert"), None),
        check_vma=False,
    )
```

```python
import functools
import math

import jax
import jax.numpy as jnp
from jax import lax
from jax.experimental import pallas as pl
from jax.experimental.pallas import tpu as pltpu
from jax.sharding import PartitionSpec as P

HEAD_DIM = 128
BOTH = ("fsdp", "expert")
VMEM = pl.BlockSpec(memory_space=pltpu.VMEM)
SMEM = pl.BlockSpec(memory_space=pltpu.SMEM)
HBM = pl.BlockSpec(memory_space=pltpu.HBM)
ANYWHERE = pl.BlockSpec(memory_space=pl.ANY)
NT = (((1,), (1,)), ((), ()))


def dot_nt(left, right):
    return lax.dot_general(left, right, NT, preferred_element_type=jnp.float32)


def rms_scale(inputs, scale_gain):
    mean_square = jnp.mean(inputs * inputs, axis=-1, keepdims=True)
    return inputs * lax.rsqrt(mean_square + 1e-06) * scale_gain


def limit(mebibytes):
    return pltpu.CompilerParams(vmem_limit_bytes=mebibytes * 2**20)


def chip_weights_kernel(layers, in_ref, out_ref, sent_ref):
    head_count = out_ref.shape[1] // HEAD_DIM
    pairs = []
    for pair in range(head_count // 2):
        parts = []
        for head in (2 * pair, 2 * pair + 1):
            for part in range(3):
                start = (part * head_count + head) * HEAD_DIM
                parts.append(in_ref[:, start : start + HEAD_DIM])
        parts.append(out_ref[:, 2 * pair * HEAD_DIM : (2 * pair + 2) * HEAD_DIM])
        pairs.append(jnp.concatenate(parts, axis=1))
    for chip in range(sent_ref.shape[0]):
        sent_ref[chip] = pairs[(chip // (2 * layers)) % 2 * 2 + chip % 2]


def chip_weights_call(layers, chips, attention_in, attention_out):
    rows = attention_in.shape[0]
    return pl.pallas_call(
        functools.partial(chip_weights_kernel, layers),
        out_shape=jax.ShapeDtypeStruct((chips, rows, 8 * HEAD_DIM), jnp.bfloat16),
        in_specs=[VMEM] * 2,
        out_specs=VMEM,
        compiler_params=limit(12),
        cost_estimate=pl.CostEstimate(
            flops=0, bytes_accessed=16 * chips * rows * HEAD_DIM, transcendentals=0
        ),
    )(attention_in, attention_out)


def group_weights_kernel(place_ref, in_hbm, out_hbm, *refs):
    sent_refs = refs[:4]
    in_ref, out_ref, sems = refs[4:]
    copies = [
        pltpu.make_async_copy(in_hbm, in_ref, sems.at[0]),
        pltpu.make_async_copy(out_hbm, out_ref, sems.at[1]),
    ]
    for copy in copies:
        copy.start()
    for copy in copies:
        copy.wait()
    width = out_ref.shape[1]
    for index, sent_ref in enumerate(sent_refs):
        pair = (place_ref[0] ^ (index % 2)) * 2 + (place_ref[2] ^ (index // 2))
        start = pl.multiple_of(pair * (2 * HEAD_DIM), HEAD_DIM)
        for part in range(3):
            both = in_ref[:, pl.ds(pl.multiple_of(start + part * width, HEAD_DIM), 2 * HEAD_DIM)]
            for head in range(2):
                to = (3 * head + part) * HEAD_DIM
                sent_ref[:, to : to + HEAD_DIM] = both[:, head * HEAD_DIM : (head + 1) * HEAD_DIM]
        sent_ref[:, 6 * HEAD_DIM :] = out_ref[:, pl.ds(start, 2 * HEAD_DIM)]


def group_weights_call(place, attention_in, attention_out):
    rows = attention_in.shape[0]
    one = jax.ShapeDtypeStruct((rows, 8 * HEAD_DIM), jnp.bfloat16)
    return pl.pallas_call(
        group_weights_kernel,
        out_shape=(one,) * 4,
        in_specs=[SMEM, HBM, HBM],
        out_specs=(VMEM,) * 4,
        scratch_shapes=[
            pltpu.VMEM(attention_in.shape, jnp.bfloat16),
            pltpu.VMEM(attention_out.shape, jnp.bfloat16),
            pltpu.SemaphoreType.DMA((2,)),
        ],
        compiler_params=limit(8),
        cost_estimate=pl.CostEstimate(
            flops=0, bytes_accessed=128 * rows * HEAD_DIM, transcendentals=0
        ),
    )(place, attention_in, attention_out)


def attention_kernel(block_count, piece_count, *refs):
    place_ref, gain_ref = refs[:2]
    block_refs = refs[2 : 2 + block_count]
    piece_refs = refs[2 + block_count : 2 + block_count + piece_count]
    keep_top_ref, send_top_ref, keep_low_ref, send_low_ref, weight_ref = refs[-5:]
    rows = block_refs[0].shape[0]
    half = rows // 2
    if piece_count == 1:
        weight_ref = piece_refs[0]
    else:
        layers = piece_count // 2
        for index, piece_ref in enumerate(piece_refs):
            layer, core = place_ref[1] ^ (index // 2), place_ref[3] ^ (index % 2)
            for chip in range(4):
                pair, side = place_ref[0] ^ (chip % 2), place_ref[2] ^ (chip // 2)
                device = ((pair * layers + layer) * 2 + side) * 2 + core
                span = piece_ref.shape[1]
                start = pl.multiple_of(device * span, 16)
                weight_ref[pl.ds(start, span), :] = piece_ref[chip]
    out_weights = weight_ref[:, 6 * HEAD_DIM :]
    causal = lax.broadcasted_iota(jnp.int32, (rows, rows), 0) >= lax.broadcasted_iota(
        jnp.int32, (rows, rows), 1
    )
    inputs = jnp.concatenate(
        [
            rms_scale(ref[...].astype(jnp.float32), gain_ref[...]).astype(jnp.bfloat16)
            for ref in block_refs
        ],
        axis=0,
    )
    heads = []
    for head in range(2):
        projected = jnp.dot(
            inputs,
            weight_ref[:, 3 * head * HEAD_DIM : 3 * (head + 1) * HEAD_DIM],
            preferred_element_type=jnp.float32,
        ).astype(jnp.bfloat16)
        outs = []
        for block in range(block_count):
            own = projected[block * rows : (block + 1) * rows]
            queries = own[:, :HEAD_DIM]
            keys = own[:, HEAD_DIM : 2 * HEAD_DIM]
            values = own[:, 2 * HEAD_DIM :]
            scores = dot_nt(queries, keys) * (1.0 / math.sqrt(HEAD_DIM))
            raised = jnp.where(causal, jnp.exp(jnp.where(causal, scores, 0.0)), 0.0)
            probs = raised / jnp.sum(raised, axis=-1, keepdims=True)
            outs.append(
                jnp.dot(
                    probs.astype(jnp.bfloat16), values, preferred_element_type=jnp.float32
                ).astype(jnp.bfloat16)
            )
        heads.append(jnp.concatenate(outs, axis=0))
    part = dot_nt(jnp.concatenate(heads, axis=1), out_weights).astype(jnp.bfloat16)
    for block in range(block_count):
        across, along = block // 2, block % 2
        top = send_top_ref if across else keep_top_ref
        low = send_low_ref if along else keep_low_ref
        top[along] = part[block * rows : block * rows + half]
        low[across] = part[block * rows + half : (block + 1) * rows]


def attention_call(place, gain, blocks, pieces, after):
    count = len(blocks)
    rows, width = blocks[0].shape
    tokens = count * rows
    out = jax.ShapeDtypeStruct((count // 2, rows // 2, width), jnp.bfloat16)
    return pl.pallas_call(
        functools.partial(attention_kernel, count, len(pieces)),
        out_shape=(out,) * 4,
        in_specs=[SMEM] + [VMEM] * (1 + count + len(pieces)) + [ANYWHERE] * len(after),
        out_specs=(VMEM,) * 4,
        scratch_shapes=[
            pltpu.VMEM((width, 8 * HEAD_DIM) if len(pieces) > 1 else (16, 128), jnp.bfloat16)
        ],
        compiler_params=limit(16),
        cost_estimate=pl.CostEstimate(
            flops=4 * tokens * (width * 4 * HEAD_DIM + 2 * rows * HEAD_DIM),
            bytes_accessed=4 * tokens * width + width * 16 * HEAD_DIM,
            transcendentals=2 * tokens * rows,
        ),
    )(place, gain[None, :], *blocks, *pieces, *after)


def sum_kernel(picks, *refs):
    out_ref = refs[-1]
    total = None
    for ref, pick in zip(refs, picks):
        term = (ref[...] if pick is None else ref[pick]).astype(jnp.float32)
        total = term if total is None else total + term
    out_ref[...] = total.astype(out_ref.dtype)


def sum_call(terms, after=()):
    arrays = [term[0] if isinstance(term, tuple) else term for term in terms]
    picks = [term[1] if isinstance(term, tuple) else None for term in terms]
    shape = arrays[0].shape if picks[0] is None else arrays[0].shape[1:]
    return pl.pallas_call(
        functools.partial(sum_kernel, picks),
        out_shape=jax.ShapeDtypeStruct(shape, jnp.bfloat16),
        in_specs=[VMEM] * len(arrays) + [ANYWHERE] * len(after),
        out_specs=VMEM,
        compiler_params=limit(12),
        cost_estimate=pl.CostEstimate(
            flops=len(arrays) * math.prod(shape),
            bytes_accessed=2 * (len(arrays) + 1) * math.prod(shape),
            transcendentals=0,
        ),
    )(*arrays, *after)


def stream_kernel(tokens_ref, gain_ref, *refs):
    hidden_ref, normed_ref = refs[-2:]
    half = tokens_ref.shape[0] // 2
    for index in range(2):
        keep_ref, near_ref, far_ref = refs[3 * index : 3 * index + 3]
        rows = pl.ds(index * half, half)
        hidden = (
            tokens_ref[rows, :].astype(jnp.float32)
            + keep_ref[0].astype(jnp.float32)
            + near_ref[0].astype(jnp.float32)
            + far_ref[...].astype(jnp.float32)
        )
        hidden_ref[rows, :] = hidden
        normed_ref[rows, :] = rms_scale(hidden, gain_ref[...]).astype(jnp.bfloat16)


def stream_call(tokens, gain, *parts):
    return pl.pallas_call(
        stream_kernel,
        out_shape=(
            jax.ShapeDtypeStruct(tokens.shape, jnp.float32),
            jax.ShapeDtypeStruct(tokens.shape, jnp.bfloat16),
        ),
        in_specs=[VMEM] * 8,
        out_specs=(VMEM, VMEM),
        compiler_params=limit(12),
        cost_estimate=pl.CostEstimate(
            flops=6 * tokens.size, bytes_accessed=14 * tokens.size, transcendentals=0
        ),
    )(tokens, gain[None, :], *parts)


def expert_kernel(tiles, *refs):
    expert_ref = refs[0]
    block_refs = refs[1:3]
    scale_ref = refs[3]
    weight_refs = refs[4:10]
    own_ref, side_ref = refs[-2:]
    inputs = jnp.concatenate([ref[...] for ref in block_refs], axis=0)
    result = None
    for expert in range(2):
        gate_ref, up_ref, down_ref = weight_refs[3 * expert : 3 * expert + 3]
        scale = jnp.concatenate(
            [scale_ref[block, pl.ds(expert_ref[expert], 1), :] for block in range(2)], axis=1
        )
        for start, size in tiles:
            gate_value = dot_nt(gate_ref[start : start + size, :], inputs)
            up_value = dot_nt(up_ref[start : start + size, :], inputs)
            inner = gate_value / (1.0 + jnp.exp(-gate_value)) * (up_value * scale)
            term = jnp.dot(
                down_ref[:, start : start + size],
                inner.astype(jnp.bfloat16),
                preferred_element_type=jnp.float32,
            )
            result = term if result is None else result + term
    result = result.astype(jnp.bfloat16)
    rows = block_refs[0].shape[0]
    own_ref[...] = result[:, :rows]
    side_ref[...] = result[:, rows:]


def expert_call(experts, blocks, scale_map, weights, after):
    rows, width = blocks[0].shape
    hidden = weights[0].shape[0]
    tiles = [(start, min(256, hidden - start)) for start in range(0, hidden, 256)]
    one = jax.ShapeDtypeStruct((width, rows), jnp.bfloat16)
    return pl.pallas_call(
        functools.partial(expert_kernel, tiles),
        out_shape=(one,) * 2,
        in_specs=[SMEM] + [VMEM] * 9 + [ANYWHERE] * len(after),
        out_specs=(VMEM,) * 2,
        compiler_params=limit(20),
        cost_estimate=pl.CostEstimate(
            flops=2 * 4 * rows * width * hidden * 3,
            bytes_accessed=12 * hidden * width + 8 * rows * width,
            transcendentals=4 * rows * hidden,
        ),
    )(experts, *blocks, scale_map, *weights, *after)


def load_kernel(gate_hbm, up_hbm, down_hbm, after_ref, gate_ref, up_ref, turned_ref, down_ref, sems):
    copies = [
        pltpu.make_async_copy(source, target, sems.at[index])
        for index, (source, target) in enumerate(
            ((down_hbm, down_ref), (gate_hbm, gate_ref), (up_hbm, up_ref))
        )
    ]
    for copy in copies:
        copy.start()
    copies[0].wait()
    columns, rows = down_ref.shape
    turned_ref[:, :columns] = down_ref[...].T
    if turned_ref.shape[1] > columns:
        turned_ref[:, columns:] = jnp.zeros((rows, turned_ref.shape[1] - columns), turned_ref.dtype)
    for copy in copies[1:]:
        copy.wait()


def load_call(weights, after):
    gate, _, down = weights
    rows, columns = down.shape
    return pl.pallas_call(
        load_kernel,
        out_shape=(
            jax.ShapeDtypeStruct(gate.shape, gate.dtype),
            jax.ShapeDtypeStruct(gate.shape, gate.dtype),
            jax.ShapeDtypeStruct((columns, -(-rows // 128) * 128), down.dtype),
        ),
        in_specs=[HBM] * 3 + [ANYWHERE],
        out_specs=(VMEM,) * 3,
        scratch_shapes=[pltpu.VMEM(down.shape, down.dtype), pltpu.SemaphoreType.DMA((3,))],
        compiler_params=limit(16),
        cost_estimate=pl.CostEstimate(
            flops=0, bytes_accessed=12 * gate.size, transcendentals=0
        ),
    )(*weights, after)


def mix_kernel(hidden_ref, *refs):
    total = refs[0][...].astype(jnp.float32)
    for ref in refs[1:-1]:
        total = total + ref[...].astype(jnp.float32)
    refs[-1][...] = (hidden_ref[...] + total.T).astype(jnp.bfloat16)


def mix_call(hidden, terms):
    return pl.pallas_call(
        mix_kernel,
        out_shape=jax.ShapeDtypeStruct(hidden.shape, jnp.bfloat16),
        in_specs=[VMEM] * (1 + len(terms)),
        out_specs=VMEM,
        compiler_params=limit(12),
        cost_estimate=pl.CostEstimate(
            flops=(1 + len(terms)) * hidden.size,
            bytes_accessed=(6 + 2 * len(terms)) * hidden.size,
            transcendentals=0,
        ),
    )(hidden, *terms)


def per_device(
    tokens,
    attention_gain,
    attention_in,
    attention_out,
    expert_gain,
    routes,
    route_weights,
    gate_weight,
    up_weight,
    down_weight,
):
    fsdp_size = lax.axis_size("fsdp")
    expert_size = lax.axis_size("expert")
    row_count, model_width = tokens.shape
    weight_rows = attention_out.shape[0]
    layers = expert_size // 4

    def swap_pair(value):
        return lax.ppermute(value, "fsdp", [(f, f ^ 1) for f in range(fsdp_size)])

    def swap_expert(value, mask):
        return lax.ppermute(value, "expert", [(e, e ^ mask) for e in range(expert_size)])

    def swap_core(value):
        return swap_expert(value, 1)

    def swap_side(value):
        return swap_expert(value, 2)

    def swap_layer(value, mask):
        return swap_expert(value, 4 * mask) if mask else value

    hold = lax.optimization_barrier
    my_pair = lax.axis_index("fsdp").astype(jnp.int32)
    my_expert = lax.axis_index("expert").astype(jnp.int32)
    place = jnp.stack([my_pair, my_expert // 4, my_expert // 2 % 2, my_expert % 2])
    experts = jnp.stack([my_expert, my_expert ^ 1])
    chips = fsdp_size * expert_size // 2
    as_tree = fsdp_size == 2 and layers == 4 and weight_rows % 16 == 0

    blocks = [tokens, swap_pair(tokens), swap_side(tokens)]
    gate_rows, up_rows, down_rows = gate_weight[0].T, up_weight[0].T, down_weight[0]
    if as_tree:
        mine, by_pair, by_side, by_both = group_weights_call(place, attention_in, attention_out)
        both_ways = [
            (f * expert_size + e, (f ^ 1) * expert_size + (e ^ 2))
            for f in range(fsdp_size)
            for e in range(expert_size)
        ]
        rows_here = jnp.stack(
            [mine, swap_pair(by_pair), swap_side(by_side), lax.ppermute(by_both, BOTH, both_ways)]
        )
        rows_here, blocks, gate_rows, up_rows = hold((rows_here, blocks, gate_rows, up_rows))
        far = swap_layer(rows_here, 2)
        near = swap_layer(rows_here, 1)
    else:
        sent = chip_weights_call(layers, chips, attention_in, attention_out)
        same_core = [[2 * chip + core for chip in range(chips)] for core in range(2)]
        got = lax.all_to_all(
            sent, BOTH, split_axis=0, concat_axis=0, axis_index_groups=same_core, tiled=True
        )
        in_order = jnp.stack([got, swap_core(got)], axis=1)
        in_order = jnp.where(my_expert % 2 == 0, in_order, in_order[:, ::-1])
        pieces = [in_order.reshape(model_width, 8 * HEAD_DIM)]
    blocks.append(swap_side(blocks[1]))
    own_expert = [gate_rows, up_rows, down_rows]
    other_expert = [swap_core(gate_rows), swap_core(up_rows)]
    if as_tree:
        far, near, other_expert, route_weights, blocks, down_rows = hold(
            (far, near, other_expert, route_weights, blocks, down_rows)
        )
        pieces = []
        for piece in (rows_here, near, far, swap_layer(far, 1)):
            pieces += [piece, swap_core(piece)]
    other_expert.append(swap_core(down_rows))

    chosen = routes[:, :, None] == jnp.arange(expert_size, dtype=jnp.int32)
    scale_map = jnp.sum(jnp.where(chosen, route_weights[:, :, None], 0.0), axis=1).T[None]
    scale_map = jnp.concatenate([scale_map, swap_side(scale_map)], axis=0)

    keep_top, send_top, keep_low, send_low = attention_call(
        place, attention_gain, blocks, pieces, [scale_map, other_expert[2]]
    )

    near_top = swap_side(send_top)
    near_low = swap_pair(send_low)
    own_expert = load_call(own_expert, keep_top)
    near_top, near_low, own_expert = hold((near_top, near_low, own_expert))
    far_top = swap_pair(sum_call([(keep_top, 1), (near_top, 1)]))
    far_low = swap_side(sum_call([(keep_low, 1), (near_low, 1)]))
    other_expert = load_call(other_expert, near_low)
    far_top, far_low, other_expert = hold((far_top, far_low, other_expert))
    hidden_stream, expert_in = stream_call(
        tokens, expert_gain, keep_top, near_top, far_top, keep_low, near_low, far_low
    )

    arrivals = {0: expert_in}
    order = [0] + sorted(range(1, layers), key=lambda mask: (mask == 1, mask))
    sums, finals, crossings = [], [], []
    for step, mask in enumerate(order):
        low = mask & -mask
        source = arrivals[mask ^ low]
        if mask == 1 and step >= 2:
            source, _ = hold((source, block))
        block = swap_layer(source, low)
        if step == 1:
            block, scale_map, _ = hold((block, scale_map, crossings[0]))
        arrivals[mask] = block
        own, crossing = expert_call(
            experts,
            [block, swap_side(block)],
            swap_layer(scale_map, mask),
            [*own_expert, *other_expert],
            (sums[step - 3 : step - 2] if step >= 3 else []) + crossings[-1:],
        )
        crossings.append(crossing)
        if step == 0:
            first = own
        else:
            sums.append(sum_call([own, swap_side(crossing)]))
            finals.append(swap_layer(sums[-1], mask))
    crossing, _ = hold((crossings[0], crossings[-1]))
    return mix_call(hidden_stream, [first, *finals, swap_side(crossing)])


def solution(mesh):
    placed = (
        P(("fsdp", "expert"), None),
        P(),
        P(("fsdp", "expert"), None),
        P(("fsdp", "expert"), None),
        P(),
        P(("fsdp", "expert"), None),
        P(("fsdp", "expert"), None),
        P("expert", None, None),
        P("expert", None, None),
        P("expert", None, None),
    )
    return jax.shard_map(
        per_device,
        mesh=mesh,
        in_specs=placed,
        out_specs=P(("fsdp", "expert"), None),
        check_vma=False,
    )
```

```python
import functools
import math

import jax
import jax.numpy as jnp
from jax import lax
from jax.experimental import pallas as pl
from jax.experimental.pallas import tpu as pltpu
from jax.sharding import PartitionSpec as P

HEAD_DIM = 128
BOTH = ("fsdp", "expert")
VMEM = pl.BlockSpec(memory_space=pltpu.VMEM)
SMEM = pl.BlockSpec(memory_space=pltpu.SMEM)
HBM = pl.BlockSpec(memory_space=pltpu.HBM)
ANYWHERE = pl.BlockSpec(memory_space=pl.ANY)
NT = (((1,), (1,)), ((), ()))


def dot_nt(left, right):
    return lax.dot_general(left, right, NT, preferred_element_type=jnp.float32)


def rms_scale(inputs, scale_gain):
    mean_square = jnp.mean(inputs * inputs, axis=-1, keepdims=True)
    return inputs * lax.rsqrt(mean_square + 1e-06) * scale_gain


def limit(mebibytes):
    return pltpu.CompilerParams(vmem_limit_bytes=mebibytes * 2**20)


def chip_weights_kernel(layers, in_ref, out_ref, sent_ref):
    head_count = out_ref.shape[1] // HEAD_DIM
    pairs = []
    for pair in range(head_count // 2):
        parts = []
        for head in (2 * pair, 2 * pair + 1):
            for part in range(3):
                start = (part * head_count + head) * HEAD_DIM
                parts.append(in_ref[:, start : start + HEAD_DIM])
        parts.append(out_ref[:, 2 * pair * HEAD_DIM : (2 * pair + 2) * HEAD_DIM])
        pairs.append(jnp.concatenate(parts, axis=1))
    for chip in range(sent_ref.shape[0]):
        sent_ref[chip] = pairs[(chip // (2 * layers)) % 2 * 2 + chip % 2]


def chip_weights_call(layers, chips, attention_in, attention_out):
    rows = attention_in.shape[0]
    return pl.pallas_call(
        functools.partial(chip_weights_kernel, layers),
        out_shape=jax.ShapeDtypeStruct((chips, rows, 8 * HEAD_DIM), jnp.bfloat16),
        in_specs=[VMEM] * 2,
        out_specs=VMEM,
        compiler_params=limit(12),
        cost_estimate=pl.CostEstimate(
            flops=0, bytes_accessed=16 * chips * rows * HEAD_DIM, transcendentals=0
        ),
    )(attention_in, attention_out)


def group_weights_kernel(place_ref, in_hbm, out_hbm, *refs):
    sent_refs = refs[:4]
    in_ref, out_ref, sems = refs[4:]
    copies = [
        pltpu.make_async_copy(in_hbm, in_ref, sems.at[0]),
        pltpu.make_async_copy(out_hbm, out_ref, sems.at[1]),
    ]
    for copy in copies:
        copy.start()
    for copy in copies:
        copy.wait()
    width = out_ref.shape[1]
    for index, sent_ref in enumerate(sent_refs):
        pair = (place_ref[0] ^ (index % 2)) * 2 + (place_ref[2] ^ (index // 2))
        start = pl.multiple_of(pair * (2 * HEAD_DIM), HEAD_DIM)
        for part in range(3):
            both = in_ref[:, pl.ds(pl.multiple_of(start + part * width, HEAD_DIM), 2 * HEAD_DIM)]
            for head in range(2):
                to = (3 * head + part) * HEAD_DIM
                sent_ref[:, to : to + HEAD_DIM] = both[:, head * HEAD_DIM : (head + 1) * HEAD_DIM]
        sent_ref[:, 6 * HEAD_DIM :] = out_ref[:, pl.ds(start, 2 * HEAD_DIM)]


def group_weights_call(place, attention_in, attention_out):
    rows = attention_in.shape[0]
    one = jax.ShapeDtypeStruct((rows, 8 * HEAD_DIM), jnp.bfloat16)
    return pl.pallas_call(
        group_weights_kernel,
        out_shape=(one,) * 4,
        in_specs=[SMEM, HBM, HBM],
        out_specs=(VMEM,) * 4,
        scratch_shapes=[
            pltpu.VMEM(attention_in.shape, jnp.bfloat16),
            pltpu.VMEM(attention_out.shape, jnp.bfloat16),
            pltpu.SemaphoreType.DMA((2,)),
        ],
        compiler_params=limit(8),
        cost_estimate=pl.CostEstimate(
            flops=0, bytes_accessed=128 * rows * HEAD_DIM, transcendentals=0
        ),
    )(place, attention_in, attention_out)


def attention_kernel(block_count, piece_count, *refs):
    place_ref, gain_ref = refs[:2]
    block_refs = refs[2 : 2 + block_count]
    piece_refs = refs[2 + block_count : 2 + block_count + piece_count]
    keep_top_ref, send_top_ref, keep_low_ref, send_low_ref, weight_ref = refs[-5:]
    rows = block_refs[0].shape[0]
    half = rows // 2
    if piece_count == 1:
        weight_ref = piece_refs[0]
    else:
        layers = piece_count // 2
        for index, piece_ref in enumerate(piece_refs):
            layer, core = place_ref[1] ^ (index // 2), place_ref[3] ^ (index % 2)
            for chip in range(4):
                pair, side = place_ref[0] ^ (chip % 2), place_ref[2] ^ (chip // 2)
                device = ((pair * layers + layer) * 2 + side) * 2 + core
                span = piece_ref.shape[1]
                start = pl.multiple_of(device * span, 16)
                weight_ref[pl.ds(start, span), :] = piece_ref[chip]
    out_weights = weight_ref[:, 6 * HEAD_DIM :]
    causal = lax.broadcasted_iota(jnp.int32, (rows, rows), 0) >= lax.broadcasted_iota(
        jnp.int32, (rows, rows), 1
    )
    inputs = jnp.concatenate(
        [
            rms_scale(ref[...].astype(jnp.float32), gain_ref[...]).astype(jnp.bfloat16)
            for ref in block_refs
        ],
        axis=0,
    )
    heads = []
    for head in range(2):
        projected = jnp.dot(
            inputs,
            weight_ref[:, 3 * head * HEAD_DIM : 3 * (head + 1) * HEAD_DIM],
            preferred_element_type=jnp.float32,
        ).astype(jnp.bfloat16)
        outs = []
        for block in range(block_count):
            own = projected[block * rows : (block + 1) * rows]
            queries = own[:, :HEAD_DIM]
            keys = own[:, HEAD_DIM : 2 * HEAD_DIM]
            values = own[:, 2 * HEAD_DIM :]
            scores = dot_nt(queries, keys) * (1.0 / math.sqrt(HEAD_DIM))
            raised = jnp.where(causal, jnp.exp(jnp.where(causal, scores, 0.0)), 0.0)
            probs = raised / jnp.sum(raised, axis=-1, keepdims=True)
            outs.append(
                jnp.dot(
                    probs.astype(jnp.bfloat16), values, preferred_element_type=jnp.float32
                ).astype(jnp.bfloat16)
            )
        heads.append(jnp.concatenate(outs, axis=0))
    part = dot_nt(jnp.concatenate(heads, axis=1), out_weights).astype(jnp.bfloat16)
    for block in range(block_count):
        across, along = block // 2, block % 2
        top = send_top_ref if across else keep_top_ref
        low = send_low_ref if along else keep_low_ref
        top[along] = part[block * rows : block * rows + half]
        low[across] = part[block * rows + half : (block + 1) * rows]


def attention_call(place, gain, blocks, pieces, after):
    count = len(blocks)
    rows, width = blocks[0].shape
    tokens = count * rows
    out = jax.ShapeDtypeStruct((count // 2, rows // 2, width), jnp.bfloat16)
    return pl.pallas_call(
        functools.partial(attention_kernel, count, len(pieces)),
        out_shape=(out,) * 4,
        in_specs=[SMEM] + [VMEM] * (1 + count + len(pieces)) + [ANYWHERE] * len(after),
        out_specs=(VMEM,) * 4,
        scratch_shapes=[
            pltpu.VMEM((width, 8 * HEAD_DIM) if len(pieces) > 1 else (16, 128), jnp.bfloat16)
        ],
        compiler_params=limit(16),
        cost_estimate=pl.CostEstimate(
            flops=4 * tokens * (width * 4 * HEAD_DIM + 2 * rows * HEAD_DIM),
            bytes_accessed=4 * tokens * width + width * 16 * HEAD_DIM,
            transcendentals=2 * tokens * rows,
        ),
    )(place, gain[None, :], *blocks, *pieces, *after)


def sum_kernel(picks, *refs):
    out_ref = refs[-1]
    total = None
    for ref, pick in zip(refs, picks):
        term = (ref[...] if pick is None else ref[pick]).astype(jnp.float32)
        total = term if total is None else total + term
    out_ref[...] = total.astype(out_ref.dtype)


def sum_call(terms, after=()):
    arrays = [term[0] if isinstance(term, tuple) else term for term in terms]
    picks = [term[1] if isinstance(term, tuple) else None for term in terms]
    shape = arrays[0].shape if picks[0] is None else arrays[0].shape[1:]
    return pl.pallas_call(
        functools.partial(sum_kernel, picks),
        out_shape=jax.ShapeDtypeStruct(shape, jnp.bfloat16),
        in_specs=[VMEM] * len(arrays) + [ANYWHERE] * len(after),
        out_specs=VMEM,
        compiler_params=limit(12),
        cost_estimate=pl.CostEstimate(
            flops=len(arrays) * math.prod(shape),
            bytes_accessed=2 * (len(arrays) + 1) * math.prod(shape),
            transcendentals=0,
        ),
    )(*arrays, *after)


def stream_kernel(tokens_ref, gain_ref, *refs):
    hidden_ref, normed_ref = refs[-2:]
    half = tokens_ref.shape[0] // 2
    for index in range(2):
        keep_ref, near_ref, far_ref = refs[3 * index : 3 * index + 3]
        rows = pl.ds(index * half, half)
        hidden = (
            tokens_ref[rows, :].astype(jnp.float32)
            + keep_ref[0].astype(jnp.float32)
            + near_ref[0].astype(jnp.float32)
            + far_ref[...].astype(jnp.float32)
        )
        hidden_ref[rows, :] = hidden
        normed_ref[rows, :] = rms_scale(hidden, gain_ref[...]).astype(jnp.bfloat16)


def stream_call(tokens, gain, *parts):
    return pl.pallas_call(
        stream_kernel,
        out_shape=(
            jax.ShapeDtypeStruct(tokens.shape, jnp.float32),
            jax.ShapeDtypeStruct(tokens.shape, jnp.bfloat16),
        ),
        in_specs=[VMEM] * 8,
        out_specs=(VMEM, VMEM),
        compiler_params=limit(12),
        cost_estimate=pl.CostEstimate(
            flops=6 * tokens.size, bytes_accessed=14 * tokens.size, transcendentals=0
        ),
    )(tokens, gain[None, :], *parts)


def expert_kernel(tiles, *refs):
    place_ref = refs[0]
    block_refs = refs[1:3]
    scale_ref = refs[3]
    weight_refs = refs[4:10]
    own_ref, side_ref = refs[-2:]
    inputs = jnp.concatenate([ref[...] for ref in block_refs], axis=0)
    result = None
    for expert in range(2):
        gate_ref, up_ref, down_ref = weight_refs[3 * expert : 3 * expert + 3]
        scale = jnp.concatenate(
            [scale_ref[block, pl.ds(place_ref[4 + expert], 1), :] for block in range(2)], axis=1
        )
        for start, size in tiles:
            gate_value = dot_nt(gate_ref[start : start + size, :], inputs)
            up_value = dot_nt(up_ref[start : start + size, :], inputs)
            inner = gate_value / (1.0 + jnp.exp(-gate_value)) * (up_value * scale)
            term = jnp.dot(
                down_ref[:, start : start + size],
                inner.astype(jnp.bfloat16),
                preferred_element_type=jnp.float32,
            )
            result = term if result is None else result + term
    result = result.astype(jnp.bfloat16)
    rows = block_refs[0].shape[0]
    own_ref[...] = result[:, :rows]
    side_ref[...] = result[:, rows:]


def expert_call(place, blocks, scale_map, weights, after):
    rows, width = blocks[0].shape
    hidden = weights[0].shape[0]
    tiles = [(start, min(256, hidden - start)) for start in range(0, hidden, 256)]
    one = jax.ShapeDtypeStruct((width, rows), jnp.bfloat16)
    return pl.pallas_call(
        functools.partial(expert_kernel, tiles),
        out_shape=(one,) * 2,
        in_specs=[SMEM] + [VMEM] * 9 + [ANYWHERE] * len(after),
        out_specs=(VMEM,) * 2,
        compiler_params=limit(20),
        cost_estimate=pl.CostEstimate(
            flops=2 * 4 * rows * width * hidden * 3,
            bytes_accessed=12 * hidden * width + 8 * rows * width,
            transcendentals=4 * rows * hidden,
        ),
    )(place, *blocks, scale_map, *weights, *after)


def scale_kernel(routes_ref, weights_ref, map_ref):
    top_count, rows = routes_ref.shape
    experts = lax.broadcasted_iota(jnp.int32, (map_ref.shape[0], rows), 0)
    total = jnp.zeros(map_ref.shape, jnp.float32)
    for choice in range(top_count):
        chosen = experts == routes_ref[choice : choice + 1, :]
        total = total + jnp.where(chosen, weights_ref[choice : choice + 1, :], 0.0)
    map_ref[...] = total


def scale_call(expert_size, routes, weights):
    rows = routes.shape[1]
    return pl.pallas_call(
        scale_kernel,
        out_shape=jax.ShapeDtypeStruct((expert_size, rows), jnp.float32),
        in_specs=[VMEM] * 2,
        out_specs=VMEM,
        compiler_params=limit(8),
    )(routes, weights)


def pair_kernel(first_ref, second_ref, pair_ref):
    pair_ref[0] = first_ref[...]
    pair_ref[1] = second_ref[...]


def pair_call(first, second):
    return pl.pallas_call(
        pair_kernel,
        out_shape=jax.ShapeDtypeStruct((2, *first.shape), first.dtype),
        in_specs=[VMEM] * 2,
        out_specs=VMEM,
        compiler_params=limit(8),
    )(first, second)


def load_kernel(gate_hbm, up_hbm, down_hbm, after_ref, gate_ref, up_ref, turned_ref, down_ref, sems):
    copies = [
        pltpu.make_async_copy(source, target, sems.at[index])
        for index, (source, target) in enumerate(
            ((down_hbm, down_ref), (gate_hbm, gate_ref), (up_hbm, up_ref))
        )
    ]
    for copy in copies:
        copy.start()
    copies[0].wait()
    columns, rows = down_ref.shape
    turned_ref[:, :columns] = down_ref[...].T
    if turned_ref.shape[1] > columns:
        turned_ref[:, columns:] = jnp.zeros((rows, turned_ref.shape[1] - columns), turned_ref.dtype)
    for copy in copies[1:]:
        copy.wait()


def load_call(weights, after):
    gate, _, down = weights
    rows, columns = down.shape
    return pl.pallas_call(
        load_kernel,
        out_shape=(
            jax.ShapeDtypeStruct(gate.shape, gate.dtype),
            jax.ShapeDtypeStruct(gate.shape, gate.dtype),
            jax.ShapeDtypeStruct((columns, -(-rows // 128) * 128), down.dtype),
        ),
        in_specs=[HBM] * 3 + [ANYWHERE],
        out_specs=(VMEM,) * 3,
        scratch_shapes=[pltpu.VMEM(down.shape, down.dtype), pltpu.SemaphoreType.DMA((3,))],
        compiler_params=limit(16),
        cost_estimate=pl.CostEstimate(
            flops=0, bytes_accessed=12 * gate.size, transcendentals=0
        ),
    )(*weights, after)


def mix_kernel(hidden_ref, *refs):
    total = refs[0][...].astype(jnp.float32)
    for ref in refs[1:-1]:
        total = total + ref[...].astype(jnp.float32)
    refs[-1][...] = (hidden_ref[...] + total.T).astype(jnp.bfloat16)


def mix_call(hidden, terms):
    return pl.pallas_call(
        mix_kernel,
        out_shape=jax.ShapeDtypeStruct(hidden.shape, jnp.bfloat16),
        in_specs=[VMEM] * (1 + len(terms)),
        out_specs=VMEM,
        compiler_params=limit(12),
        cost_estimate=pl.CostEstimate(
            flops=(1 + len(terms)) * hidden.size,
            bytes_accessed=(6 + 2 * len(terms)) * hidden.size,
            transcendentals=0,
        ),
    )(hidden, *terms)


def per_device(
    tokens,
    attention_gain,
    attention_in,
    attention_out,
    expert_gain,
    routes,
    route_weights,
    gate_weight,
    up_weight,
    down_weight,
):
    fsdp_size = lax.axis_size("fsdp")
    expert_size = lax.axis_size("expert")
    row_count, model_width = tokens.shape
    weight_rows = attention_out.shape[0]
    layers = expert_size // 4

    def swap_pair(value):
        return lax.ppermute(value, "fsdp", [(f, f ^ 1) for f in range(fsdp_size)])

    def swap_expert(value, mask):
        return lax.ppermute(value, "expert", [(e, e ^ mask) for e in range(expert_size)])

    def swap_core(value):
        return swap_expert(value, 1)

    def swap_side(value):
        return swap_expert(value, 2)

    def swap_layer(value, mask):
        return swap_expert(value, 4 * mask) if mask else value

    hold = lax.optimization_barrier
    my_pair = lax.axis_index("fsdp").astype(jnp.int32)
    my_expert = lax.axis_index("expert").astype(jnp.int32)
    place = jnp.stack(
        [my_pair, my_expert // 4, my_expert // 2 % 2, my_expert % 2, my_expert, my_expert ^ 1]
    )
    chips = fsdp_size * expert_size // 2
    as_tree = fsdp_size == 2 and layers == 4 and weight_rows % 16 == 0

    blocks = [tokens, swap_pair(tokens), swap_side(tokens)]
    gate_rows, up_rows, down_rows = gate_weight[0].T, up_weight[0].T, down_weight[0]
    if as_tree:
        mine, by_pair, by_side, by_both = group_weights_call(place, attention_in, attention_out)
        both_ways = [
            (f * expert_size + e, (f ^ 1) * expert_size + (e ^ 2))
            for f in range(fsdp_size)
            for e in range(expert_size)
        ]
        rows_here = jnp.stack(
            [mine, swap_pair(by_pair), swap_side(by_side), lax.ppermute(by_both, BOTH, both_ways)]
        )
        rows_here, blocks, gate_rows, up_rows = hold((rows_here, blocks, gate_rows, up_rows))
        far = swap_layer(rows_here, 2)
        near = swap_layer(rows_here, 1)
    else:
        sent = chip_weights_call(layers, chips, attention_in, attention_out)
        same_core = [[2 * chip + core for chip in range(chips)] for core in range(2)]
        got = lax.all_to_all(
            sent, BOTH, split_axis=0, concat_axis=0, axis_index_groups=same_core, tiled=True
        )
        in_order = jnp.stack([got, swap_core(got)], axis=1)
        in_order = jnp.where(my_expert % 2 == 0, in_order, in_order[:, ::-1])
        pieces = [in_order.reshape(model_width, 8 * HEAD_DIM)]
    blocks.append(swap_side(blocks[1]))
    own_expert = [gate_rows, up_rows, down_rows]
    other_expert = [swap_core(gate_rows), swap_core(up_rows)]
    if as_tree:
        far, near, other_expert, route_weights, blocks, down_rows = hold(
            (far, near, other_expert, route_weights, blocks, down_rows)
        )
        pieces = []
        for piece in (rows_here, near, far, swap_layer(far, 1)):
            pieces += [piece, swap_core(piece)]
    other_expert.append(swap_core(down_rows))

    scale_map = scale_call(expert_size, routes.T, route_weights.T)
    scale_map = pair_call(scale_map, swap_side(scale_map))

    keep_top, send_top, keep_low, send_low = attention_call(
        place, attention_gain, blocks, pieces, [scale_map, other_expert[2]]
    )

    near_top = swap_side(send_top)
    near_low = swap_pair(send_low)
    own_expert = load_call(own_expert, keep_top)
    scale_map, _ = hold((scale_map, keep_top))
    scale_maps = [swap_layer(scale_map, mask) for mask in range(layers)]
    near_top, near_low, own_expert, scale_maps = hold(
        (near_top, near_low, own_expert, scale_maps)
    )
    far_top = swap_pair(sum_call([(keep_top, 1), (near_top, 1)]))
    far_low = swap_side(sum_call([(keep_low, 1), (near_low, 1)]))
    other_expert = load_call(other_expert, near_low)
    far_top, far_low, other_expert = hold((far_top, far_low, other_expert))
    hidden_stream, expert_in = stream_call(
        tokens, expert_gain, keep_top, near_top, far_top, keep_low, near_low, far_low
    )

    arrivals = {0: expert_in}
    order = [0] + sorted(range(1, layers), key=lambda mask: (mask == 1, mask))
    sums, finals, crossings = [], [], []
    for step, mask in enumerate(order):
        low = mask & -mask
        source = arrivals[mask ^ low]
        if mask == 1 and step >= 2:
            source, _ = hold((source, block))
        block = swap_layer(source, low)
        if step == 1:
            block, _ = hold((block, crossings[0]))
        arrivals[mask] = block
        own, crossing = expert_call(
            place,
            [block, swap_side(block)],
            scale_maps[mask],
            [*own_expert, *other_expert],
            (sums[step - 3 : step - 2] if step >= 3 else []) + crossings[-1:],
        )
        crossings.append(crossing)
        if step == 0:
            first = own
        else:
            sums.append(sum_call([own, swap_side(crossing)]))
            finals.append(swap_layer(sums[-1], mask))
    crossing, _ = hold((crossings[0], crossings[-1]))
    return mix_call(hidden_stream, [first, *finals, swap_side(crossing)])


def solution(mesh):
    placed = (
        P(("fsdp", "expert"), None),
        P(),
        P(("fsdp", "expert"), None),
        P(("fsdp", "expert"), None),
        P(),
        P(("fsdp", "expert"), None),
        P(("fsdp", "expert"), None),
        P("expert", None, None),
        P("expert", None, None),
        P("expert", None, None),
    )
    return jax.shard_map(
        per_device,
        mesh=mesh,
        in_specs=placed,
        out_specs=P(("fsdp", "expert"), None),
        check_vma=False,
    )
```

```python
import functools
import math

import jax
import jax.numpy as jnp
from jax import lax
from jax.experimental import pallas as pl
from jax.experimental.pallas import tpu as pltpu
from jax.sharding import PartitionSpec as P

HEAD_DIM = 128
BOTH = ("fsdp", "expert")
VMEM = pl.BlockSpec(memory_space=pltpu.VMEM)
SMEM = pl.BlockSpec(memory_space=pltpu.SMEM)
HBM = pl.BlockSpec(memory_space=pltpu.HBM)
ANYWHERE = pl.BlockSpec(memory_space=pl.ANY)
NT = (((1,), (1,)), ((), ()))


def dot_nt(left, right):
    return lax.dot_general(left, right, NT, preferred_element_type=jnp.float32)


def rms_scale(inputs, scale_gain):
    mean_square = jnp.mean(inputs * inputs, axis=-1, keepdims=True)
    return inputs * lax.rsqrt(mean_square + 1e-06) * scale_gain


def limit(mebibytes):
    return pltpu.CompilerParams(vmem_limit_bytes=mebibytes * 2**20)


def chip_weights_kernel(layers, in_ref, out_ref, sent_ref):
    head_count = out_ref.shape[1] // HEAD_DIM
    pairs = []
    for pair in range(head_count // 2):
        parts = []
        for head in (2 * pair, 2 * pair + 1):
            for part in range(3):
                start = (part * head_count + head) * HEAD_DIM
                parts.append(in_ref[:, start : start + HEAD_DIM])
        parts.append(out_ref[:, 2 * pair * HEAD_DIM : (2 * pair + 2) * HEAD_DIM])
        pairs.append(jnp.concatenate(parts, axis=1))
    for chip in range(sent_ref.shape[0]):
        sent_ref[chip] = pairs[(chip // (2 * layers)) % 2 * 2 + chip % 2]


def chip_weights_call(layers, chips, attention_in, attention_out):
    rows = attention_in.shape[0]
    return pl.pallas_call(
        functools.partial(chip_weights_kernel, layers),
        out_shape=jax.ShapeDtypeStruct((chips, rows, 8 * HEAD_DIM), jnp.bfloat16),
        in_specs=[VMEM] * 2,
        out_specs=VMEM,
        compiler_params=limit(12),
        cost_estimate=pl.CostEstimate(
            flops=0, bytes_accessed=16 * chips * rows * HEAD_DIM, transcendentals=0
        ),
    )(attention_in, attention_out)


def group_weights_kernel(place_ref, in_hbm, out_hbm, *refs):
    sent_refs = refs[:4]
    in_ref, out_ref, sems = refs[4:]
    copies = [
        pltpu.make_async_copy(in_hbm, in_ref, sems.at[0]),
        pltpu.make_async_copy(out_hbm, out_ref, sems.at[1]),
    ]
    for copy in copies:
        copy.start()
    for copy in copies:
        copy.wait()
    width = out_ref.shape[1]
    for index, sent_ref in enumerate(sent_refs):
        pair = (place_ref[0] ^ (index % 2)) * 2 + (place_ref[2] ^ (index // 2))
        start = pl.multiple_of(pair * (2 * HEAD_DIM), HEAD_DIM)
        for part in range(3):
            both = in_ref[:, pl.ds(pl.multiple_of(start + part * width, HEAD_DIM), 2 * HEAD_DIM)]
            for head in range(2):
                to = (3 * head + part) * HEAD_DIM
                sent_ref[:, to : to + HEAD_DIM] = both[:, head * HEAD_DIM : (head + 1) * HEAD_DIM]
        sent_ref[:, 6 * HEAD_DIM :] = out_ref[:, pl.ds(start, 2 * HEAD_DIM)]


def group_weights_call(place, attention_in, attention_out):
    rows = attention_in.shape[0]
    one = jax.ShapeDtypeStruct((rows, 8 * HEAD_DIM), jnp.bfloat16)
    return pl.pallas_call(
        group_weights_kernel,
        out_shape=(one,) * 4,
        in_specs=[SMEM, HBM, HBM],
        out_specs=(VMEM,) * 4,
        scratch_shapes=[
            pltpu.VMEM(attention_in.shape, jnp.bfloat16),
            pltpu.VMEM(attention_out.shape, jnp.bfloat16),
            pltpu.SemaphoreType.DMA((2,)),
        ],
        compiler_params=limit(8),
        cost_estimate=pl.CostEstimate(
            flops=0, bytes_accessed=128 * rows * HEAD_DIM, transcendentals=0
        ),
    )(place, attention_in, attention_out)


def attention_kernel(block_count, piece_count, *refs):
    place_ref, gain_ref = refs[:2]
    block_refs = refs[2 : 2 + block_count]
    piece_refs = refs[2 + block_count : 2 + block_count + piece_count]
    keep_top_ref, send_top_ref, keep_low_ref, send_low_ref, weight_ref = refs[-5:]
    rows = block_refs[0].shape[0]
    half = rows // 2
    if piece_count == 1:
        weight_ref = piece_refs[0]
    else:
        layers = piece_count // 2
        for index, piece_ref in enumerate(piece_refs):
            layer, core = place_ref[1] ^ (index // 2), place_ref[3] ^ (index % 2)
            for chip in range(4):
                pair, side = place_ref[0] ^ (chip % 2), place_ref[2] ^ (chip // 2)
                device = ((pair * layers + layer) * 2 + side) * 2 + core
                span = piece_ref.shape[1]
                start = pl.multiple_of(device * span, 16)
                weight_ref[pl.ds(start, span), :] = piece_ref[chip]
    out_weights = weight_ref[:, 6 * HEAD_DIM :]
    causal = lax.broadcasted_iota(jnp.int32, (rows, rows), 0) >= lax.broadcasted_iota(
        jnp.int32, (rows, rows), 1
    )
    inputs = jnp.concatenate(
        [
            rms_scale(ref[...].astype(jnp.float32), gain_ref[...]).astype(jnp.bfloat16)
            for ref in block_refs
        ],
        axis=0,
    )
    heads = []
    for head in range(2):
        projected = jnp.dot(
            inputs,
            weight_ref[:, 3 * head * HEAD_DIM : 3 * (head + 1) * HEAD_DIM],
            preferred_element_type=jnp.float32,
        ).astype(jnp.bfloat16)
        outs = []
        for block in range(block_count):
            own = projected[block * rows : (block + 1) * rows]
            queries = own[:, :HEAD_DIM]
            keys = own[:, HEAD_DIM : 2 * HEAD_DIM]
            values = own[:, 2 * HEAD_DIM :]
            scores = dot_nt(queries, keys) * (1.0 / math.sqrt(HEAD_DIM))
            raised = jnp.where(causal, jnp.exp(jnp.where(causal, scores, 0.0)), 0.0)
            probs = raised / jnp.sum(raised, axis=-1, keepdims=True)
            outs.append(
                jnp.dot(
                    probs.astype(jnp.bfloat16), values, preferred_element_type=jnp.float32
                ).astype(jnp.bfloat16)
            )
        heads.append(jnp.concatenate(outs, axis=0))
    part = dot_nt(jnp.concatenate(heads, axis=1), out_weights).astype(jnp.bfloat16)
    for block in range(block_count):
        across, along = block // 2, block % 2
        top = send_top_ref if across else keep_top_ref
        low = send_low_ref if along else keep_low_ref
        top[along] = part[block * rows : block * rows + half]
        low[across] = part[block * rows + half : (block + 1) * rows]


def attention_call(place, gain, blocks, pieces, after):
    count = len(blocks)
    rows, width = blocks[0].shape
    tokens = count * rows
    out = jax.ShapeDtypeStruct((count // 2, rows // 2, width), jnp.bfloat16)
    return pl.pallas_call(
        functools.partial(attention_kernel, count, len(pieces)),
        out_shape=(out,) * 4,
        in_specs=[SMEM] + [VMEM] * (1 + count + len(pieces)) + [ANYWHERE] * len(after),
        out_specs=(VMEM,) * 4,
        scratch_shapes=[
            pltpu.VMEM((width, 8 * HEAD_DIM) if len(pieces) > 1 else (16, 128), jnp.bfloat16)
        ],
        compiler_params=limit(16),
        cost_estimate=pl.CostEstimate(
            flops=4 * tokens * (width * 4 * HEAD_DIM + 2 * rows * HEAD_DIM),
            bytes_accessed=4 * tokens * width + width * 16 * HEAD_DIM,
            transcendentals=2 * tokens * rows,
        ),
    )(place, gain, *blocks, *pieces, *after)


def sum_kernel(picks, *refs):
    out_ref = refs[-1]
    total = None
    for ref, pick in zip(refs, picks):
        term = (ref[...] if pick is None else ref[pick]).astype(jnp.float32)
        total = term if total is None else total + term
    out_ref[...] = total.astype(out_ref.dtype)


def sum_call(terms, after=()):
    arrays = [term[0] if isinstance(term, tuple) else term for term in terms]
    picks = [term[1] if isinstance(term, tuple) else None for term in terms]
    shape = arrays[0].shape if picks[0] is None else arrays[0].shape[1:]
    return pl.pallas_call(
        functools.partial(sum_kernel, picks),
        out_shape=jax.ShapeDtypeStruct(shape, jnp.bfloat16),
        in_specs=[VMEM] * len(arrays) + [ANYWHERE] * len(after),
        out_specs=VMEM,
        compiler_params=limit(12),
        cost_estimate=pl.CostEstimate(
            flops=len(arrays) * math.prod(shape),
            bytes_accessed=2 * (len(arrays) + 1) * math.prod(shape),
            transcendentals=0,
        ),
    )(*arrays, *after)


def stream_kernel(tokens_ref, gain_ref, *refs):
    hidden_ref, normed_ref = refs[-2:]
    half = tokens_ref.shape[0] // 2
    for index in range(2):
        keep_ref, near_ref, far_ref = refs[3 * index : 3 * index + 3]
        rows = pl.ds(index * half, half)
        hidden = (
            tokens_ref[rows, :].astype(jnp.float32)
            + keep_ref[0].astype(jnp.float32)
            + near_ref[0].astype(jnp.float32)
            + far_ref[...].astype(jnp.float32)
        )
        hidden_ref[rows, :] = hidden
        normed_ref[rows, :] = rms_scale(hidden, gain_ref[...]).astype(jnp.bfloat16)


def stream_call(tokens, gain, *parts):
    return pl.pallas_call(
        stream_kernel,
        out_shape=(
            jax.ShapeDtypeStruct(tokens.shape, jnp.float32),
            jax.ShapeDtypeStruct(tokens.shape, jnp.bfloat16),
        ),
        in_specs=[VMEM] * 8,
        out_specs=(VMEM, VMEM),
        compiler_params=limit(12),
        cost_estimate=pl.CostEstimate(
            flops=6 * tokens.size, bytes_accessed=14 * tokens.size, transcendentals=0
        ),
    )(tokens, gain[None, :], *parts)


def expert_kernel(tiles, *refs):
    place_ref = refs[0]
    block_refs = refs[1:3]
    scale_ref = refs[3]
    weight_refs = refs[4:10]
    own_ref, side_ref = refs[-2:]
    inputs = jnp.concatenate([ref[...] for ref in block_refs], axis=0)
    result = None
    for expert in range(2):
        gate_ref, up_ref, down_ref = weight_refs[3 * expert : 3 * expert + 3]
        scale = jnp.concatenate(
            [scale_ref[block, pl.ds(place_ref[4 + expert], 1), :] for block in range(2)], axis=1
        )
        for start, size in tiles:
            gate_value = dot_nt(gate_ref[start : start + size, :], inputs)
            up_value = dot_nt(up_ref[start : start + size, :], inputs)
            inner = gate_value / (1.0 + jnp.exp(-gate_value)) * (up_value * scale)
            term = jnp.dot(
                down_ref[:, start : start + size],
                inner.astype(jnp.bfloat16),
                preferred_element_type=jnp.float32,
            )
            result = term if result is None else result + term
    result = result.astype(jnp.bfloat16)
    rows = block_refs[0].shape[0]
    own_ref[...] = result[:, :rows]
    side_ref[...] = result[:, rows:]


def expert_call(place, blocks, scale_map, weights, after):
    rows, width = blocks[0].shape
    hidden = weights[0].shape[0]
    tiles = [(start, min(256, hidden - start)) for start in range(0, hidden, 256)]
    one = jax.ShapeDtypeStruct((width, rows), jnp.bfloat16)
    return pl.pallas_call(
        functools.partial(expert_kernel, tiles),
        out_shape=(one,) * 2,
        in_specs=[SMEM] + [VMEM] * 9 + [ANYWHERE] * len(after),
        out_specs=(VMEM,) * 2,
        compiler_params=limit(20),
        cost_estimate=pl.CostEstimate(
            flops=2 * 4 * rows * width * hidden * 3,
            bytes_accessed=12 * hidden * width + 8 * rows * width,
            transcendentals=4 * rows * hidden,
        ),
    )(place, *blocks, scale_map, *weights, *after)


def scale_kernel(routes_ref, weights_ref, tokens_ref, gain_ref, map_ref, tokens_out, gain_out):
    top_count, rows = routes_ref.shape
    experts = lax.broadcasted_iota(jnp.int32, (map_ref.shape[0], rows), 0)
    total = jnp.zeros(map_ref.shape, jnp.float32)
    for choice in range(top_count):
        chosen = experts == routes_ref[choice : choice + 1, :]
        total = total + jnp.where(chosen, weights_ref[choice : choice + 1, :], 0.0)
    map_ref[...] = total
    tokens_out[...] = tokens_ref[...]
    gain_out[...] = gain_ref[...]


def scale_call(expert_size, routes, weights, tokens, gain):
    rows = routes.shape[1]
    return pl.pallas_call(
        scale_kernel,
        out_shape=(
            jax.ShapeDtypeStruct((expert_size, rows), jnp.float32),
            jax.ShapeDtypeStruct(tokens.shape, tokens.dtype),
            jax.ShapeDtypeStruct(gain.shape, gain.dtype),
        ),
        in_specs=[VMEM] * 4,
        out_specs=(VMEM,) * 3,
        compiler_params=limit(8),
    )(routes, weights, tokens, gain)


def pair_kernel(first_ref, second_ref, pair_ref):
    pair_ref[0] = first_ref[...]
    pair_ref[1] = second_ref[...]


def pair_call(first, second):
    return pl.pallas_call(
        pair_kernel,
        out_shape=jax.ShapeDtypeStruct((2, *first.shape), first.dtype),
        in_specs=[VMEM] * 2,
        out_specs=VMEM,
        compiler_params=limit(8),
    )(first, second)


def load_kernel(gate_hbm, up_hbm, down_hbm, after_ref, gate_ref, up_ref, turned_ref, down_ref, sems):
    copies = [
        pltpu.make_async_copy(source, target, sems.at[index])
        for index, (source, target) in enumerate(
            ((down_hbm, down_ref), (gate_hbm, gate_ref), (up_hbm, up_ref))
        )
    ]
    for copy in copies:
        copy.start()
    copies[0].wait()
    columns, rows = down_ref.shape
    turned_ref[:, :columns] = down_ref[...].T
    if turned_ref.shape[1] > columns:
        turned_ref[:, columns:] = jnp.zeros((rows, turned_ref.shape[1] - columns), turned_ref.dtype)
    for copy in copies[1:]:
        copy.wait()


def load_call(weights, after):
    gate, _, down = weights
    rows, columns = down.shape
    return pl.pallas_call(
        load_kernel,
        out_shape=(
            jax.ShapeDtypeStruct(gate.shape, gate.dtype),
            jax.ShapeDtypeStruct(gate.shape, gate.dtype),
            jax.ShapeDtypeStruct((columns, -(-rows // 128) * 128), down.dtype),
        ),
        in_specs=[HBM] * 3 + [ANYWHERE],
        out_specs=(VMEM,) * 3,
        scratch_shapes=[pltpu.VMEM(down.shape, down.dtype), pltpu.SemaphoreType.DMA((3,))],
        compiler_params=limit(16),
        cost_estimate=pl.CostEstimate(
            flops=0, bytes_accessed=12 * gate.size, transcendentals=0
        ),
    )(*weights, after)


def mix_kernel(hidden_ref, *refs):
    total = refs[0][...].astype(jnp.float32)
    for ref in refs[1:-1]:
        total = total + ref[...].astype(jnp.float32)
    refs[-1][...] = (hidden_ref[...] + total.T).astype(jnp.bfloat16)


def mix_call(hidden, terms):
    return pl.pallas_call(
        mix_kernel,
        out_shape=jax.ShapeDtypeStruct(hidden.shape, jnp.bfloat16),
        in_specs=[VMEM] * (1 + len(terms)),
        out_specs=VMEM,
        compiler_params=limit(12),
        cost_estimate=pl.CostEstimate(
            flops=(1 + len(terms)) * hidden.size,
            bytes_accessed=(6 + 2 * len(terms)) * hidden.size,
            transcendentals=0,
        ),
    )(hidden, *terms)


def per_device(
    tokens,
    attention_gain,
    attention_in,
    attention_out,
    expert_gain,
    routes,
    route_weights,
    gate_weight,
    up_weight,
    down_weight,
):
    fsdp_size = lax.axis_size("fsdp")
    expert_size = lax.axis_size("expert")
    row_count, model_width = tokens.shape
    weight_rows = attention_out.shape[0]
    layers = expert_size // 4

    def swap_pair(value):
        return lax.ppermute(value, "fsdp", [(f, f ^ 1) for f in range(fsdp_size)])

    def swap_expert(value, mask):
        return lax.ppermute(value, "expert", [(e, e ^ mask) for e in range(expert_size)])

    def swap_core(value):
        return swap_expert(value, 1)

    def swap_side(value):
        return swap_expert(value, 2)

    def swap_layer(value, mask):
        return swap_expert(value, 4 * mask) if mask else value

    hold = lax.optimization_barrier
    my_pair = lax.axis_index("fsdp").astype(jnp.int32)
    my_expert = lax.axis_index("expert").astype(jnp.int32)
    place = jnp.stack(
        [my_pair, my_expert // 4, my_expert // 2 % 2, my_expert % 2, my_expert, my_expert ^ 1]
    )
    chips = fsdp_size * expert_size // 2
    as_tree = fsdp_size == 2 and layers == 4 and weight_rows % 16 == 0

    gate_rows, up_rows, down_rows = gate_weight[0].T, up_weight[0].T, down_weight[0]
    if as_tree:
        sent = group_weights_call(place, attention_in, attention_out)
        (mine, by_pair, by_side, by_both), sent_tokens = hold((sent, tokens))
        blocks = [tokens, swap_pair(sent_tokens), swap_side(sent_tokens)]
        both_ways = [
            (f * expert_size + e, (f ^ 1) * expert_size + (e ^ 2))
            for f in range(fsdp_size)
            for e in range(expert_size)
        ]
        rows_here = jnp.stack(
            [mine, swap_pair(by_pair), swap_side(by_side), lax.ppermute(by_both, BOTH, both_ways)]
        )
        rows_here, blocks, gate_rows, up_rows, route_weights = hold(
            (rows_here, blocks, gate_rows, up_rows, route_weights)
        )
        far = swap_layer(rows_here, 2)
        near = swap_layer(rows_here, 1)
    else:
        sent = chip_weights_call(layers, chips, attention_in, attention_out)
        same_core = [[2 * chip + core for chip in range(chips)] for core in range(2)]
        got = lax.all_to_all(
            sent, BOTH, split_axis=0, concat_axis=0, axis_index_groups=same_core, tiled=True
        )
        in_order = jnp.stack([got, swap_core(got)], axis=1)
        in_order = jnp.where(my_expert % 2 == 0, in_order, in_order[:, ::-1])
        pieces = [in_order.reshape(model_width, 8 * HEAD_DIM)]
        blocks = [tokens, swap_pair(tokens), swap_side(tokens)]
    blocks.append(swap_side(blocks[1]))
    own_expert = [gate_rows, up_rows, down_rows]
    other_expert = [swap_core(gate_rows), swap_core(up_rows)]
    scale_map, own_tokens, own_gain = scale_call(
        expert_size, routes.T, route_weights.T, blocks[0], attention_gain[None, :]
    )
    blocks[0] = own_tokens
    if as_tree:
        far, near, other_expert, scale_map, blocks, down_rows = hold(
            (far, near, other_expert, scale_map, blocks, down_rows)
        )
        pieces = []
        for piece in (rows_here, near, far, swap_layer(far, 1)):
            pieces += [piece, swap_core(piece)]
    other_expert.append(swap_core(down_rows))

    scale_map = pair_call(scale_map, swap_side(scale_map))

    keep_top, send_top, keep_low, send_low = attention_call(
        place, own_gain, blocks, pieces, [scale_map, other_expert[2]]
    )

    near_top = swap_side(send_top)
    near_low = swap_pair(send_low)
    own_expert = load_call(own_expert, keep_top)
    scale_map, _ = hold((scale_map, keep_top))
    scale_maps = [swap_layer(scale_map, mask) for mask in range(layers)]
    near_top, near_low, own_expert, scale_maps = hold(
        (near_top, near_low, own_expert, scale_maps)
    )
    far_top = swap_pair(sum_call([(keep_top, 1), (near_top, 1)]))
    far_low = swap_side(sum_call([(keep_low, 1), (near_low, 1)]))
    other_expert = load_call(other_expert, near_low)
    far_top, far_low, other_expert = hold((far_top, far_low, other_expert))
    hidden_stream, expert_in = stream_call(
        tokens, expert_gain, keep_top, near_top, far_top, keep_low, near_low, far_low
    )

    arrivals = {0: expert_in}
    order = [0] + sorted(range(1, layers), key=lambda mask: (mask == 1, mask))
    sums, finals, crossings = [], [], []
    for step, mask in enumerate(order):
        low = mask & -mask
        source = arrivals[mask ^ low]
        if mask == 1 and step >= 2:
            source, _ = hold((source, block))
        block = swap_layer(source, low)
        if step == 1:
            block, _ = hold((block, crossings[0]))
        arrivals[mask] = block
        own, crossing = expert_call(
            place,
            [block, swap_side(block)],
            scale_maps[mask],
            [*own_expert, *other_expert],
            (sums[step - 3 : step - 2] if step >= 3 else []) + crossings[-1:],
        )
        crossings.append(crossing)
        if step == 0:
            first = own
        else:
            sums.append(sum_call([own, swap_side(crossing)], finals[:1] if step == 2 else []))
            finals.append(swap_layer(sums[-1], mask))
    crossing, _ = hold((crossings[0], crossings[-1]))
    return mix_call(hidden_stream, [first, *finals, swap_side(crossing)])


def solution(mesh):
    placed = (
        P(("fsdp", "expert"), None),
        P(),
        P(("fsdp", "expert"), None),
        P(("fsdp", "expert"), None),
        P(),
        P(("fsdp", "expert"), None),
        P(("fsdp", "expert"), None),
        P("expert", None, None),
        P("expert", None, None),
        P("expert", None, None),
    )
    return jax.shard_map(
        per_device,
        mesh=mesh,
        in_specs=placed,
        out_specs=P(("fsdp", "expert"), None),
        check_vma=False,
    )
```

```python
import functools
import math

import jax
import jax.numpy as jnp
from jax import lax
from jax.experimental import pallas as pl
from jax.experimental.pallas import tpu as pltpu
from jax.sharding import PartitionSpec as P

HEAD_DIM = 128
BOTH = ("fsdp", "expert")
VMEM = pl.BlockSpec(memory_space=pltpu.VMEM)
SMEM = pl.BlockSpec(memory_space=pltpu.SMEM)
HBM = pl.BlockSpec(memory_space=pltpu.HBM)
ANYWHERE = pl.BlockSpec(memory_space=pl.ANY)
NT = (((1,), (1,)), ((), ()))


def dot_nt(left, right):
    return lax.dot_general(left, right, NT, preferred_element_type=jnp.float32)


def rms_scale(inputs, scale_gain):
    mean_square = jnp.mean(inputs * inputs, axis=-1, keepdims=True)
    return inputs * lax.rsqrt(mean_square + 1e-06) * scale_gain


def limit(mebibytes):
    return pltpu.CompilerParams(vmem_limit_bytes=mebibytes * 2**20)


def chip_weights_kernel(layers, in_ref, out_ref, sent_ref):
    head_count = out_ref.shape[1] // HEAD_DIM
    pairs = []
    for pair in range(head_count // 2):
        parts = []
        for head in (2 * pair, 2 * pair + 1):
            for part in range(3):
                start = (part * head_count + head) * HEAD_DIM
                parts.append(in_ref[:, start : start + HEAD_DIM])
        parts.append(out_ref[:, 2 * pair * HEAD_DIM : (2 * pair + 2) * HEAD_DIM])
        pairs.append(jnp.concatenate(parts, axis=1))
    for chip in range(sent_ref.shape[0]):
        sent_ref[chip] = pairs[(chip // (2 * layers)) % 2 * 2 + chip % 2]


def chip_weights_call(layers, chips, attention_in, attention_out):
    rows = attention_in.shape[0]
    return pl.pallas_call(
        functools.partial(chip_weights_kernel, layers),
        out_shape=jax.ShapeDtypeStruct((chips, rows, 8 * HEAD_DIM), jnp.bfloat16),
        in_specs=[VMEM] * 2,
        out_specs=VMEM,
        compiler_params=limit(12),
        cost_estimate=pl.CostEstimate(
            flops=0, bytes_accessed=16 * chips * rows * HEAD_DIM, transcendentals=0
        ),
    )(attention_in, attention_out)


def group_weights_kernel(place_ref, in_hbm, out_hbm, *refs):
    sent_refs = refs[:4]
    in_ref, out_ref, sems = refs[4:]
    copies = [
        pltpu.make_async_copy(in_hbm, in_ref, sems.at[0]),
        pltpu.make_async_copy(out_hbm, out_ref, sems.at[1]),
    ]
    for copy in copies:
        copy.start()
    for copy in copies:
        copy.wait()
    width = out_ref.shape[1]
    for index, sent_ref in enumerate(sent_refs):
        pair = (place_ref[0] ^ (index % 2)) * 2 + (place_ref[2] ^ (index // 2))
        start = pl.multiple_of(pair * (2 * HEAD_DIM), HEAD_DIM)
        for part in range(3):
            both = in_ref[:, pl.ds(pl.multiple_of(start + part * width, HEAD_DIM), 2 * HEAD_DIM)]
            for head in range(2):
                to = (3 * head + part) * HEAD_DIM
                sent_ref[:, to : to + HEAD_DIM] = both[:, head * HEAD_DIM : (head + 1) * HEAD_DIM]
        sent_ref[:, 6 * HEAD_DIM :] = out_ref[:, pl.ds(start, 2 * HEAD_DIM)]


def group_weights_call(place, attention_in, attention_out):
    rows = attention_in.shape[0]
    one = jax.ShapeDtypeStruct((rows, 8 * HEAD_DIM), jnp.bfloat16)
    return pl.pallas_call(
        group_weights_kernel,
        out_shape=(one,) * 4,
        in_specs=[SMEM, HBM, HBM],
        out_specs=(VMEM,) * 4,
        scratch_shapes=[
            pltpu.VMEM(attention_in.shape, jnp.bfloat16),
            pltpu.VMEM(attention_out.shape, jnp.bfloat16),
            pltpu.SemaphoreType.DMA((2,)),
        ],
        compiler_params=limit(8),
        cost_estimate=pl.CostEstimate(
            flops=0, bytes_accessed=128 * rows * HEAD_DIM, transcendentals=0
        ),
    )(place, attention_in, attention_out)


def attention_kernel(block_count, piece_count, *refs):
    place_ref, gain_ref = refs[:2]
    block_refs = refs[2 : 2 + block_count]
    piece_refs = refs[2 + block_count : 2 + block_count + piece_count]
    keep_top_ref, send_top_ref, keep_low_ref, send_low_ref, weight_ref = refs[-5:]
    rows = block_refs[0].shape[0]
    half = rows // 2
    if piece_count == 1:
        weight_ref = piece_refs[0]
    else:
        layers = piece_count // 2
        for index, piece_ref in enumerate(piece_refs):
            layer, core = place_ref[1] ^ (index // 2), place_ref[3] ^ (index % 2)
            for chip in range(4):
                pair, side = place_ref[0] ^ (chip % 2), place_ref[2] ^ (chip // 2)
                device = ((pair * layers + layer) * 2 + side) * 2 + core
                span = piece_ref.shape[1]
                start = pl.multiple_of(device * span, 16)
                weight_ref[pl.ds(start, span), :] = piece_ref[chip]
    out_weights = weight_ref[:, 6 * HEAD_DIM :]
    causal = lax.broadcasted_iota(jnp.int32, (rows, rows), 0) >= lax.broadcasted_iota(
        jnp.int32, (rows, rows), 1
    )
    inputs = jnp.concatenate(
        [
            rms_scale(ref[...].astype(jnp.float32), gain_ref[...]).astype(jnp.bfloat16)
            for ref in block_refs
        ],
        axis=0,
    )
    heads = []
    for head in range(2):
        projected = jnp.dot(
            inputs,
            weight_ref[:, 3 * head * HEAD_DIM : 3 * (head + 1) * HEAD_DIM],
            preferred_element_type=jnp.float32,
        ).astype(jnp.bfloat16)
        outs = []
        for block in range(block_count):
            own = projected[block * rows : (block + 1) * rows]
            queries = own[:, :HEAD_DIM]
            keys = own[:, HEAD_DIM : 2 * HEAD_DIM]
            values = own[:, 2 * HEAD_DIM :]
            scores = dot_nt(queries, keys) * (1.0 / math.sqrt(HEAD_DIM))
            raised = jnp.where(causal, jnp.exp(jnp.where(causal, scores, 0.0)), 0.0)
            probs = raised / jnp.sum(raised, axis=-1, keepdims=True)
            outs.append(
                jnp.dot(
                    probs.astype(jnp.bfloat16), values, preferred_element_type=jnp.float32
                ).astype(jnp.bfloat16)
            )
        heads.append(jnp.concatenate(outs, axis=0))
    part = dot_nt(jnp.concatenate(heads, axis=1), out_weights).astype(jnp.bfloat16)
    for block in range(block_count):
        across, along = block // 2, block % 2
        top = send_top_ref if across else keep_top_ref
        low = send_low_ref if along else keep_low_ref
        top[along] = part[block * rows : block * rows + half]
        low[across] = part[block * rows + half : (block + 1) * rows]


def attention_call(place, gain, blocks, pieces, after):
    count = len(blocks)
    rows, width = blocks[0].shape
    tokens = count * rows
    out = jax.ShapeDtypeStruct((count // 2, rows // 2, width), jnp.bfloat16)
    return pl.pallas_call(
        functools.partial(attention_kernel, count, len(pieces)),
        out_shape=(out,) * 4,
        in_specs=[SMEM] + [VMEM] * (1 + count + len(pieces)) + [ANYWHERE] * len(after),
        out_specs=(VMEM,) * 4,
        scratch_shapes=[
            pltpu.VMEM((width, 8 * HEAD_DIM) if len(pieces) > 1 else (16, 128), jnp.bfloat16)
        ],
        compiler_params=limit(16),
        cost_estimate=pl.CostEstimate(
            flops=4 * tokens * (width * 4 * HEAD_DIM + 2 * rows * HEAD_DIM),
            bytes_accessed=4 * tokens * width + width * 16 * HEAD_DIM,
            transcendentals=2 * tokens * rows,
        ),
    )(place, gain, *blocks, *pieces, *after)


def sum_kernel(picks, *refs):
    out_ref = refs[-1]
    total = None
    for ref, pick in zip(refs, picks):
        term = (ref[...] if pick is None else ref[pick]).astype(jnp.float32)
        total = term if total is None else total + term
    out_ref[...] = total.astype(out_ref.dtype)


def sum_call(terms, after=()):
    arrays = [term[0] if isinstance(term, tuple) else term for term in terms]
    picks = [term[1] if isinstance(term, tuple) else None for term in terms]
    shape = arrays[0].shape if picks[0] is None else arrays[0].shape[1:]
    return pl.pallas_call(
        functools.partial(sum_kernel, picks),
        out_shape=jax.ShapeDtypeStruct(shape, jnp.bfloat16),
        in_specs=[VMEM] * len(arrays) + [ANYWHERE] * len(after),
        out_specs=VMEM,
        compiler_params=limit(12),
        cost_estimate=pl.CostEstimate(
            flops=len(arrays) * math.prod(shape),
            bytes_accessed=2 * (len(arrays) + 1) * math.prod(shape),
            transcendentals=0,
        ),
    )(*arrays, *after)


def stream_kernel(tokens_ref, gain_ref, *refs):
    hidden_ref, normed_ref = refs[-2:]
    half = tokens_ref.shape[0] // 2
    for index in range(2):
        keep_ref, near_ref, far_ref = refs[3 * index : 3 * index + 3]
        rows = pl.ds(index * half, half)
        hidden = (
            tokens_ref[rows, :].astype(jnp.float32)
            + keep_ref[0].astype(jnp.float32)
            + near_ref[0].astype(jnp.float32)
            + far_ref[...].astype(jnp.float32)
        )
        hidden_ref[rows, :] = hidden
        normed_ref[rows, :] = rms_scale(hidden, gain_ref[...]).astype(jnp.bfloat16)


def stream_call(tokens, gain, *parts):
    return pl.pallas_call(
        stream_kernel,
        out_shape=(
            jax.ShapeDtypeStruct(tokens.shape, jnp.float32),
            jax.ShapeDtypeStruct(tokens.shape, jnp.bfloat16),
        ),
        in_specs=[VMEM] * 8,
        out_specs=(VMEM, VMEM),
        compiler_params=limit(12),
        cost_estimate=pl.CostEstimate(
            flops=6 * tokens.size, bytes_accessed=14 * tokens.size, transcendentals=0
        ),
    )(tokens, gain[None, :], *parts)


def expert_kernel(tiles, pick, *refs):
    place_ref = refs[0]
    block_refs = refs[1:3]
    scale_ref = refs[3]
    weight_refs = refs[4:10]
    own_ref, side_ref = refs[-2:]
    inputs = jnp.concatenate([ref[...] for ref in block_refs], axis=0)
    result = None
    for expert in range(2):
        gate_ref, up_ref, down_ref = weight_refs[3 * expert : 3 * expert + 3]
        scale = jnp.concatenate(
            [scale_ref[*pick, block, pl.ds(place_ref[4 + expert], 1), :] for block in range(2)],
            axis=1,
        )
        for start, size in tiles:
            gate_value = dot_nt(gate_ref[start : start + size, :], inputs)
            up_value = dot_nt(up_ref[start : start + size, :], inputs)
            inner = gate_value / (1.0 + jnp.exp(-gate_value)) * (up_value * scale)
            term = jnp.dot(
                down_ref[:, start : start + size],
                inner.astype(jnp.bfloat16),
                preferred_element_type=jnp.float32,
            )
            result = term if result is None else result + term
    result = result.astype(jnp.bfloat16)
    rows = block_refs[0].shape[0]
    own_ref[...] = result[:, :rows]
    side_ref[...] = result[:, rows:]


def expert_call(place, blocks, picked, weights, after):
    scale_map, pick = picked
    rows, width = blocks[0].shape
    hidden = weights[0].shape[0]
    tiles = [(start, min(256, hidden - start)) for start in range(0, hidden, 256)]
    one = jax.ShapeDtypeStruct((width, rows), jnp.bfloat16)
    return pl.pallas_call(
        functools.partial(expert_kernel, tiles, pick),
        out_shape=(one,) * 2,
        in_specs=[SMEM] + [VMEM] * 9 + [ANYWHERE] * len(after),
        out_specs=(VMEM,) * 2,
        compiler_params=limit(20),
        cost_estimate=pl.CostEstimate(
            flops=2 * 4 * rows * width * hidden * 3,
            bytes_accessed=12 * hidden * width + 8 * rows * width,
            transcendentals=4 * rows * hidden,
        ),
    )(place, *blocks, scale_map, *weights, *after)


def scale_kernel(routes_ref, weights_ref, tokens_ref, gain_ref, map_ref, tokens_out, gain_out):
    top_count, rows = routes_ref.shape
    experts = lax.broadcasted_iota(jnp.int32, (map_ref.shape[0], rows), 0)
    total = jnp.zeros(map_ref.shape, jnp.float32)
    for choice in range(top_count):
        chosen = experts == routes_ref[choice : choice + 1, :]
        total = total + jnp.where(chosen, weights_ref[choice : choice + 1, :], 0.0)
    map_ref[...] = total
    tokens_out[...] = tokens_ref[...]
    gain_out[...] = gain_ref[...]


def scale_call(expert_size, routes, weights, tokens, gain):
    rows = routes.shape[1]
    return pl.pallas_call(
        scale_kernel,
        out_shape=(
            jax.ShapeDtypeStruct((expert_size, rows), jnp.float32),
            jax.ShapeDtypeStruct(tokens.shape, tokens.dtype),
            jax.ShapeDtypeStruct(gain.shape, gain.dtype),
        ),
        in_specs=[VMEM] * 4,
        out_specs=(VMEM,) * 3,
        compiler_params=limit(8),
    )(routes, weights, tokens, gain)


def pair_kernel(first_ref, second_ref, pair_ref):
    pair_ref[0] = first_ref[...]
    pair_ref[1] = second_ref[...]


def pair_call(first, second):
    return pl.pallas_call(
        pair_kernel,
        out_shape=jax.ShapeDtypeStruct((2, *first.shape), first.dtype),
        in_specs=[VMEM] * 2,
        out_specs=VMEM,
        compiler_params=limit(8),
    )(first, second)


def load_kernel(gate_hbm, up_hbm, down_hbm, after_ref, gate_ref, up_ref, turned_ref, down_ref, sems):
    copies = [
        pltpu.make_async_copy(source, target, sems.at[index])
        for index, (source, target) in enumerate(
            ((down_hbm, down_ref), (gate_hbm, gate_ref), (up_hbm, up_ref))
        )
    ]
    for copy in copies:
        copy.start()
    copies[0].wait()
    columns, rows = down_ref.shape
    turned_ref[:, :columns] = down_ref[...].T
    if turned_ref.shape[1] > columns:
        turned_ref[:, columns:] = jnp.zeros((rows, turned_ref.shape[1] - columns), turned_ref.dtype)
    for copy in copies[1:]:
        copy.wait()


def load_call(weights, after):
    gate, _, down = weights
    rows, columns = down.shape
    return pl.pallas_call(
        load_kernel,
        out_shape=(
            jax.ShapeDtypeStruct(gate.shape, gate.dtype),
            jax.ShapeDtypeStruct(gate.shape, gate.dtype),
            jax.ShapeDtypeStruct((columns, -(-rows // 128) * 128), down.dtype),
        ),
        in_specs=[HBM] * 3 + [ANYWHERE],
        out_specs=(VMEM,) * 3,
        scratch_shapes=[pltpu.VMEM(down.shape, down.dtype), pltpu.SemaphoreType.DMA((3,))],
        compiler_params=limit(16),
        cost_estimate=pl.CostEstimate(
            flops=0, bytes_accessed=12 * gate.size, transcendentals=0
        ),
    )(*weights, after)


def mix_kernel(hidden_ref, *refs):
    total = refs[0][...].astype(jnp.float32)
    for ref in refs[1:-1]:
        total = total + ref[...].astype(jnp.float32)
    refs[-1][...] = (hidden_ref[...] + total.T).astype(jnp.bfloat16)


def mix_call(hidden, terms):
    return pl.pallas_call(
        mix_kernel,
        out_shape=jax.ShapeDtypeStruct(hidden.shape, jnp.bfloat16),
        in_specs=[VMEM] * (1 + len(terms)),
        out_specs=VMEM,
        compiler_params=limit(12),
        cost_estimate=pl.CostEstimate(
            flops=(1 + len(terms)) * hidden.size,
            bytes_accessed=(6 + 2 * len(terms)) * hidden.size,
            transcendentals=0,
        ),
    )(hidden, *terms)


def per_device(
    tokens,
    attention_gain,
    attention_in,
    attention_out,
    expert_gain,
    routes,
    route_weights,
    gate_weight,
    up_weight,
    down_weight,
):
    fsdp_size = lax.axis_size("fsdp")
    expert_size = lax.axis_size("expert")
    row_count, model_width = tokens.shape
    weight_rows = attention_out.shape[0]
    layers = expert_size // 4

    def swap_pair(value):
        return lax.ppermute(value, "fsdp", [(f, f ^ 1) for f in range(fsdp_size)])

    def swap_expert(value, mask):
        return lax.ppermute(value, "expert", [(e, e ^ mask) for e in range(expert_size)])

    def swap_core(value):
        return swap_expert(value, 1)

    def swap_side(value):
        return swap_expert(value, 2)

    def swap_layer(value, mask):
        return swap_expert(value, 4 * mask) if mask else value

    hold = lax.optimization_barrier
    my_pair = lax.axis_index("fsdp").astype(jnp.int32)
    my_expert = lax.axis_index("expert").astype(jnp.int32)
    place = jnp.stack(
        [my_pair, my_expert // 4, my_expert // 2 % 2, my_expert % 2, my_expert, my_expert ^ 1]
    )
    chips = fsdp_size * expert_size // 2
    as_tree = fsdp_size == 2 and layers == 4 and weight_rows % 16 == 0

    blocks = [tokens, swap_pair(tokens), swap_side(tokens)]
    gate_rows, up_rows, down_rows = gate_weight[0].T, up_weight[0].T, down_weight[0]
    if as_tree:
        mine, by_pair, by_side, by_both = group_weights_call(place, attention_in, attention_out)
        both_ways = [
            (f * expert_size + e, (f ^ 1) * expert_size + (e ^ 2))
            for f in range(fsdp_size)
            for e in range(expert_size)
        ]
        rows_here = jnp.stack(
            [mine, swap_pair(by_pair), swap_side(by_side), lax.ppermute(by_both, BOTH, both_ways)]
        )
        rows_here, blocks, gate_rows, up_rows, route_weights = hold(
            (rows_here, blocks, gate_rows, up_rows, route_weights)
        )
        far = swap_layer(rows_here, 2)
        near = swap_layer(rows_here, 1)
    else:
        sent = chip_weights_call(layers, chips, attention_in, attention_out)
        same_core = [[2 * chip + core for chip in range(chips)] for core in range(2)]
        got = lax.all_to_all(
            sent, BOTH, split_axis=0, concat_axis=0, axis_index_groups=same_core, tiled=True
        )
        in_order = jnp.stack([got, swap_core(got)], axis=1)
        in_order = jnp.where(my_expert % 2 == 0, in_order, in_order[:, ::-1])
        pieces = [in_order.reshape(model_width, 8 * HEAD_DIM)]
    blocks.append(swap_side(blocks[1]))
    own_expert = [gate_rows, up_rows, down_rows]
    other_expert = [swap_core(gate_rows), swap_core(up_rows)]
    scale_map, own_tokens, own_gain = scale_call(
        expert_size, routes.T, route_weights.T, blocks[0], attention_gain[None, :]
    )
    blocks[0] = own_tokens
    if as_tree:
        far, near, other_expert, scale_map, blocks, down_rows = hold(
            (far, near, other_expert, scale_map, blocks, down_rows)
        )
        pieces = []
        for piece in (rows_here, near, far, swap_layer(far, 1)):
            pieces += [piece, swap_core(piece)]
    other_expert.append(swap_core(down_rows))

    scale_map = pair_call(scale_map, swap_side(scale_map))
    bit = layers // 2
    while bit > 1:
        scale_map = pair_call(scale_map, swap_layer(scale_map, bit))
        bit //= 2

    keep_top, send_top, keep_low, send_low = attention_call(
        place, own_gain, blocks, pieces, [scale_map, other_expert[2]]
    )

    near_top = swap_side(send_top)
    near_low = swap_pair(send_low)
    own_expert = load_call(own_expert, keep_top)
    scale_map, _ = hold((scale_map, keep_top))
    scale_maps = [scale_map, swap_layer(scale_map, 1)]
    near_top, near_low, own_expert, scale_maps = hold(
        (near_top, near_low, own_expert, scale_maps)
    )
    far_top = swap_pair(sum_call([(keep_top, 1), (near_top, 1)]))
    far_low = swap_side(sum_call([(keep_low, 1), (near_low, 1)]))
    other_expert = load_call(other_expert, near_low)
    far_top, far_low, other_expert = hold((far_top, far_low, other_expert))
    hidden_stream, expert_in = stream_call(
        tokens, expert_gain, keep_top, near_top, far_top, keep_low, near_low, far_low
    )

    arrivals = {0: expert_in}
    order = [0] + sorted(range(1, layers), key=lambda mask: (mask == 1, mask))
    sums, finals, crossings = [], [], []
    for step, mask in enumerate(order):
        low = mask & -mask
        source = arrivals[mask ^ low]
        if mask == 1 and step >= 2:
            source, _ = hold((source, block))
        block = swap_layer(source, low)
        if step == 1:
            block, _ = hold((block, crossings[0]))
        arrivals[mask] = block
        own, crossing = expert_call(
            place,
            [block, swap_side(block)],
            (scale_maps[mask % 2], [mask >> bit & 1 for bit in range(1, layers.bit_length() - 1)]),
            [*own_expert, *other_expert],
            (sums[step - 3 : step - 2] if step >= 3 else []) + crossings[-1:],
        )
        crossings.append(crossing)
        if step == 0:
            first = own
        else:
            sums.append(sum_call([own, swap_side(crossing)], finals[:1] if step == 2 else []))
            finals.append(swap_layer(sums[-1], mask))
    crossing, _ = hold((crossings[0], crossings[-1]))
    return mix_call(hidden_stream, [first, *finals, swap_side(crossing)])


def solution(mesh):
    placed = (
        P(("fsdp", "expert"), None),
        P(),
        P(("fsdp", "expert"), None),
        P(("fsdp", "expert"), None),
        P(),
        P(("fsdp", "expert"), None),
        P(("fsdp", "expert"), None),
        P("expert", None, None),
        P("expert", None, None),
        P("expert", None, None),
    )
    return jax.shard_map(
        per_device,
        mesh=mesh,
        in_specs=placed,
        out_specs=P(("fsdp", "expert"), None),
        check_vma=False,
    )
```

```python
import functools
import math

import jax
import jax.numpy as jnp
from jax import lax
from jax.experimental import pallas as pl
from jax.experimental.pallas import tpu as pltpu
from jax.sharding import PartitionSpec as P

HEAD_DIM = 128
BOTH = ("fsdp", "expert")
VMEM = pl.BlockSpec(memory_space=pltpu.VMEM)
SMEM = pl.BlockSpec(memory_space=pltpu.SMEM)
HBM = pl.BlockSpec(memory_space=pltpu.HBM)
ANYWHERE = pl.BlockSpec(memory_space=pl.ANY)
NT = (((1,), (1,)), ((), ()))


def dot_nt(left, right):
    return lax.dot_general(left, right, NT, preferred_element_type=jnp.float32)


def rms_scale(inputs, scale_gain):
    mean_square = jnp.mean(inputs * inputs, axis=-1, keepdims=True)
    return inputs * lax.rsqrt(mean_square + 1e-06) * scale_gain


def limit(mebibytes):
    return pltpu.CompilerParams(vmem_limit_bytes=mebibytes * 2**20)


def chip_weights_kernel(layers, in_ref, out_ref, sent_ref):
    head_count = out_ref.shape[1] // HEAD_DIM
    pairs = []
    for pair in range(head_count // 2):
        parts = []
        for head in (2 * pair, 2 * pair + 1):
            for part in range(3):
                start = (part * head_count + head) * HEAD_DIM
                parts.append(in_ref[:, start : start + HEAD_DIM])
        parts.append(out_ref[:, 2 * pair * HEAD_DIM : (2 * pair + 2) * HEAD_DIM])
        pairs.append(jnp.concatenate(parts, axis=1))
    for chip in range(sent_ref.shape[0]):
        sent_ref[chip] = pairs[(chip // (2 * layers)) % 2 * 2 + chip % 2]


def chip_weights_call(layers, chips, attention_in, attention_out):
    rows = attention_in.shape[0]
    return pl.pallas_call(
        functools.partial(chip_weights_kernel, layers),
        out_shape=jax.ShapeDtypeStruct((chips, rows, 8 * HEAD_DIM), jnp.bfloat16),
        in_specs=[VMEM] * 2,
        out_specs=VMEM,
        compiler_params=limit(12),
        cost_estimate=pl.CostEstimate(
            flops=0, bytes_accessed=16 * chips * rows * HEAD_DIM, transcendentals=0
        ),
    )(attention_in, attention_out)


def group_weights_kernel(place_ref, in_hbm, out_hbm, *refs):
    sent_refs = refs[:4]
    in_ref, out_ref, sems = refs[4:]
    copies = [
        pltpu.make_async_copy(in_hbm, in_ref, sems.at[0]),
        pltpu.make_async_copy(out_hbm, out_ref, sems.at[1]),
    ]
    for copy in copies:
        copy.start()
    for copy in copies:
        copy.wait()
    width = out_ref.shape[1]
    for index, sent_ref in enumerate(sent_refs):
        pair = (place_ref[0] ^ (index % 2)) * 2 + (place_ref[2] ^ (index // 2))
        start = pl.multiple_of(pair * (2 * HEAD_DIM), HEAD_DIM)
        for part in range(3):
            both = in_ref[:, pl.ds(pl.multiple_of(start + part * width, HEAD_DIM), 2 * HEAD_DIM)]
            for head in range(2):
                to = (3 * head + part) * HEAD_DIM
                sent_ref[:, to : to + HEAD_DIM] = both[:, head * HEAD_DIM : (head + 1) * HEAD_DIM]
        sent_ref[:, 6 * HEAD_DIM :] = out_ref[:, pl.ds(start, 2 * HEAD_DIM)]


def group_weights_call(place, attention_in, attention_out):
    rows = attention_in.shape[0]
    one = jax.ShapeDtypeStruct((rows, 8 * HEAD_DIM), jnp.bfloat16)
    return pl.pallas_call(
        group_weights_kernel,
        out_shape=(one,) * 4,
        in_specs=[SMEM, HBM, HBM],
        out_specs=(VMEM,) * 4,
        scratch_shapes=[
            pltpu.VMEM(attention_in.shape, jnp.bfloat16),
            pltpu.VMEM(attention_out.shape, jnp.bfloat16),
            pltpu.SemaphoreType.DMA((2,)),
        ],
        compiler_params=limit(8),
        cost_estimate=pl.CostEstimate(
            flops=0, bytes_accessed=128 * rows * HEAD_DIM, transcendentals=0
        ),
    )(place, attention_in, attention_out)


def attention_kernel(block_count, piece_count, *refs):
    place_ref, gain_ref = refs[:2]
    block_refs = refs[2 : 2 + block_count]
    piece_refs = refs[2 + block_count : 2 + block_count + piece_count]
    keep_top_ref, send_top_ref, keep_low_ref, send_low_ref, weight_ref = refs[-5:]
    rows = block_refs[0].shape[0]
    half = rows // 2
    if piece_count == 1:
        weight_ref = piece_refs[0]
    else:
        layers = piece_count // 2
        for index, piece_ref in enumerate(piece_refs):
            layer, core = place_ref[1] ^ (index // 2), place_ref[3] ^ (index % 2)
            for chip in range(4):
                pair, side = place_ref[0] ^ (chip % 2), place_ref[2] ^ (chip // 2)
                device = ((pair * layers + layer) * 2 + side) * 2 + core
                span = piece_ref.shape[1]
                start = pl.multiple_of(device * span, 16)
                weight_ref[pl.ds(start, span), :] = piece_ref[chip]
    out_weights = weight_ref[:, 6 * HEAD_DIM :]
    causal = lax.broadcasted_iota(jnp.int32, (rows, rows), 0) >= lax.broadcasted_iota(
        jnp.int32, (rows, rows), 1
    )
    inputs = jnp.concatenate(
        [
            rms_scale(ref[...].astype(jnp.float32), gain_ref[...]).astype(jnp.bfloat16)
            for ref in block_refs
        ],
        axis=0,
    )
    heads = []
    for head in range(2):
        projected = jnp.dot(
            inputs,
            weight_ref[:, 3 * head * HEAD_DIM : 3 * (head + 1) * HEAD_DIM],
            preferred_element_type=jnp.float32,
        ).astype(jnp.bfloat16)
        outs = []
        for block in range(block_count):
            own = projected[block * rows : (block + 1) * rows]
            queries = own[:, :HEAD_DIM]
            keys = own[:, HEAD_DIM : 2 * HEAD_DIM]
            values = own[:, 2 * HEAD_DIM :]
            scores = dot_nt(queries, keys) * (1.0 / math.sqrt(HEAD_DIM))
            raised = jnp.where(causal, jnp.exp(jnp.where(causal, scores, 0.0)), 0.0)
            probs = raised / jnp.sum(raised, axis=-1, keepdims=True)
            outs.append(
                jnp.dot(
                    probs.astype(jnp.bfloat16), values, preferred_element_type=jnp.float32
                ).astype(jnp.bfloat16)
            )
        heads.append(jnp.concatenate(outs, axis=0))
    part = dot_nt(jnp.concatenate(heads, axis=1), out_weights).astype(jnp.bfloat16)
    for block in range(block_count):
        across, along = block // 2, block % 2
        top = send_top_ref if across else keep_top_ref
        low = send_low_ref if along else keep_low_ref
        top[along] = part[block * rows : block * rows + half]
        low[across] = part[block * rows + half : (block + 1) * rows]


def attention_call(place, gain, blocks, pieces, after):
    count = len(blocks)
    rows, width = blocks[0].shape
    tokens = count * rows
    out = jax.ShapeDtypeStruct((count // 2, rows // 2, width), jnp.bfloat16)
    return pl.pallas_call(
        functools.partial(attention_kernel, count, len(pieces)),
        out_shape=(out,) * 4,
        in_specs=[SMEM] + [VMEM] * (1 + count + len(pieces)) + [ANYWHERE] * len(after),
        out_specs=(VMEM,) * 4,
        scratch_shapes=[
            pltpu.VMEM((width, 8 * HEAD_DIM) if len(pieces) > 1 else (16, 128), jnp.bfloat16)
        ],
        compiler_params=limit(16),
        cost_estimate=pl.CostEstimate(
            flops=4 * tokens * (width * 4 * HEAD_DIM + 2 * rows * HEAD_DIM),
            bytes_accessed=4 * tokens * width + width * 16 * HEAD_DIM,
            transcendentals=2 * tokens * rows,
        ),
    )(place, gain, *blocks, *pieces, *after)


def sum_kernel(picks, *refs):
    out_ref = refs[-1]
    total = None
    for ref, pick in zip(refs, picks):
        term = (ref[...] if pick is None else ref[pick]).astype(jnp.float32)
        total = term if total is None else total + term
    out_ref[...] = total.astype(out_ref.dtype)


def sum_call(terms, after=()):
    arrays = [term[0] if isinstance(term, tuple) else term for term in terms]
    picks = [term[1] if isinstance(term, tuple) else None for term in terms]
    shape = arrays[0].shape if picks[0] is None else arrays[0].shape[1:]
    return pl.pallas_call(
        functools.partial(sum_kernel, picks),
        out_shape=jax.ShapeDtypeStruct(shape, jnp.bfloat16),
        in_specs=[VMEM] * len(arrays) + [ANYWHERE] * len(after),
        out_specs=VMEM,
        compiler_params=limit(12),
        cost_estimate=pl.CostEstimate(
            flops=len(arrays) * math.prod(shape),
            bytes_accessed=2 * (len(arrays) + 1) * math.prod(shape),
            transcendentals=0,
        ),
    )(*arrays, *after)


def stream_kernel(tokens_ref, gain_ref, *refs):
    hidden_ref, normed_ref = refs[-2:]
    half = tokens_ref.shape[0] // 2
    for index in range(2):
        keep_ref, near_ref, far_ref = refs[3 * index : 3 * index + 3]
        rows = pl.ds(index * half, half)
        hidden = (
            tokens_ref[rows, :].astype(jnp.float32)
            + keep_ref[0].astype(jnp.float32)
            + near_ref[0].astype(jnp.float32)
            + far_ref[...].astype(jnp.float32)
        )
        hidden_ref[rows, :] = hidden
        normed_ref[rows, :] = rms_scale(hidden, gain_ref[...]).astype(jnp.bfloat16)


def stream_call(tokens, gain, *parts):
    return pl.pallas_call(
        stream_kernel,
        out_shape=(
            jax.ShapeDtypeStruct(tokens.shape, jnp.float32),
            jax.ShapeDtypeStruct(tokens.shape, jnp.bfloat16),
        ),
        in_specs=[VMEM] * 8,
        out_specs=(VMEM, VMEM),
        compiler_params=limit(12),
        cost_estimate=pl.CostEstimate(
            flops=6 * tokens.size, bytes_accessed=14 * tokens.size, transcendentals=0
        ),
    )(tokens, gain[None, :], *parts)


def expert_kernel(tiles, pick, *refs):
    place_ref = refs[0]
    block_refs = refs[1:3]
    scale_ref = refs[3]
    weight_refs = refs[4:10]
    own_ref, side_ref = refs[-2:]
    inputs = jnp.concatenate([ref[...] for ref in block_refs], axis=0)
    result = None
    for expert in range(2):
        gate_ref, up_ref, down_ref = weight_refs[3 * expert : 3 * expert + 3]
        scale = jnp.concatenate(
            [scale_ref[*pick, block, pl.ds(place_ref[4 + expert], 1), :] for block in range(2)],
            axis=1,
        )
        for start, size in tiles:
            gate_value = dot_nt(gate_ref[start : start + size, :], inputs)
            up_value = dot_nt(up_ref[start : start + size, :], inputs)
            inner = gate_value / (1.0 + jnp.exp(-gate_value)) * (up_value * scale)
            term = jnp.dot(
                down_ref[:, start : start + size],
                inner.astype(jnp.bfloat16),
                preferred_element_type=jnp.float32,
            )
            result = term if result is None else result + term
    result = result.astype(jnp.bfloat16)
    rows = block_refs[0].shape[0]
    own_ref[...] = result[:, :rows]
    side_ref[...] = result[:, rows:]


def expert_call(place, blocks, picked, weights, after):
    scale_map, pick = picked
    rows, width = blocks[0].shape
    hidden = weights[0].shape[0]
    tiles = [(start, min(256, hidden - start)) for start in range(0, hidden, 256)]
    one = jax.ShapeDtypeStruct((width, rows), jnp.bfloat16)
    return pl.pallas_call(
        functools.partial(expert_kernel, tiles, pick),
        out_shape=(one,) * 2,
        in_specs=[SMEM] + [VMEM] * 9 + [ANYWHERE] * len(after),
        out_specs=(VMEM,) * 2,
        compiler_params=limit(20),
        cost_estimate=pl.CostEstimate(
            flops=2 * 4 * rows * width * hidden * 3,
            bytes_accessed=12 * hidden * width + 8 * rows * width,
            transcendentals=4 * rows * hidden,
        ),
    )(place, *blocks, scale_map, *weights, *after)


def scale_kernel(routes_ref, weights_ref, tokens_ref, gain_ref, map_ref, tokens_out, gain_out):
    top_count, rows = routes_ref.shape
    experts = lax.broadcasted_iota(jnp.int32, (map_ref.shape[0], rows), 0)
    total = jnp.zeros(map_ref.shape, jnp.float32)
    for choice in range(top_count):
        chosen = experts == routes_ref[choice : choice + 1, :]
        total = total + jnp.where(chosen, weights_ref[choice : choice + 1, :], 0.0)
    map_ref[...] = total
    tokens_out[...] = tokens_ref[...]
    gain_out[...] = gain_ref[...]


def scale_call(expert_size, routes, weights, tokens, gain):
    rows = routes.shape[1]
    return pl.pallas_call(
        scale_kernel,
        out_shape=(
            jax.ShapeDtypeStruct((expert_size, rows), jnp.float32),
            jax.ShapeDtypeStruct(tokens.shape, tokens.dtype),
            jax.ShapeDtypeStruct(gain.shape, gain.dtype),
        ),
        in_specs=[VMEM] * 4,
        out_specs=(VMEM,) * 3,
        compiler_params=limit(8),
    )(routes, weights, tokens, gain)


def pair_kernel(first_ref, second_ref, pair_ref):
    pair_ref[0] = first_ref[...]
    pair_ref[1] = second_ref[...]


def pair_call(first, second):
    return pl.pallas_call(
        pair_kernel,
        out_shape=jax.ShapeDtypeStruct((2, *first.shape), first.dtype),
        in_specs=[VMEM] * 2,
        out_specs=VMEM,
        compiler_params=limit(8),
    )(first, second)


def load_kernel(gate_hbm, up_hbm, down_hbm, after_ref, gate_ref, up_ref, turned_ref, down_ref, sems):
    copies = [
        pltpu.make_async_copy(source, target, sems.at[index])
        for index, (source, target) in enumerate(
            ((down_hbm, down_ref), (gate_hbm, gate_ref), (up_hbm, up_ref))
        )
    ]
    for copy in copies:
        copy.start()
    copies[0].wait()
    columns, rows = down_ref.shape
    turned_ref[:, :columns] = down_ref[...].T
    if turned_ref.shape[1] > columns:
        turned_ref[:, columns:] = jnp.zeros((rows, turned_ref.shape[1] - columns), turned_ref.dtype)
    for copy in copies[1:]:
        copy.wait()


def load_call(weights, after):
    gate, _, down = weights
    rows, columns = down.shape
    return pl.pallas_call(
        load_kernel,
        out_shape=(
            jax.ShapeDtypeStruct(gate.shape, gate.dtype),
            jax.ShapeDtypeStruct(gate.shape, gate.dtype),
            jax.ShapeDtypeStruct((columns, -(-rows // 128) * 128), down.dtype),
        ),
        in_specs=[HBM] * 3 + [ANYWHERE],
        out_specs=(VMEM,) * 3,
        scratch_shapes=[pltpu.VMEM(down.shape, down.dtype), pltpu.SemaphoreType.DMA((3,))],
        compiler_params=limit(16),
        cost_estimate=pl.CostEstimate(
            flops=0, bytes_accessed=12 * gate.size, transcendentals=0
        ),
    )(*weights, after)


def mix_kernel(hidden_ref, *refs):
    total = refs[0][...].astype(jnp.float32)
    for ref in refs[1:-1]:
        total = total + ref[...].astype(jnp.float32)
    refs[-1][...] = (hidden_ref[...] + total.T).astype(jnp.bfloat16)


def mix_call(hidden, terms):
    return pl.pallas_call(
        mix_kernel,
        out_shape=jax.ShapeDtypeStruct(hidden.shape, jnp.bfloat16),
        in_specs=[VMEM] * (1 + len(terms)),
        out_specs=VMEM,
        compiler_params=limit(12),
        cost_estimate=pl.CostEstimate(
            flops=(1 + len(terms)) * hidden.size,
            bytes_accessed=(6 + 2 * len(terms)) * hidden.size,
            transcendentals=0,
        ),
    )(hidden, *terms)


def per_device(
    tokens,
    attention_gain,
    attention_in,
    attention_out,
    expert_gain,
    routes,
    route_weights,
    gate_weight,
    up_weight,
    down_weight,
):
    fsdp_size = lax.axis_size("fsdp")
    expert_size = lax.axis_size("expert")
    row_count, model_width = tokens.shape
    weight_rows = attention_out.shape[0]
    layers = expert_size // 4

    def swap_pair(value):
        return lax.ppermute(value, "fsdp", [(f, f ^ 1) for f in range(fsdp_size)])

    def swap_expert(value, mask):
        return lax.ppermute(value, "expert", [(e, e ^ mask) for e in range(expert_size)])

    def swap_core(value):
        return swap_expert(value, 1)

    def swap_side(value):
        return swap_expert(value, 2)

    def swap_layer(value, mask):
        return swap_expert(value, 4 * mask) if mask else value

    hold = lax.optimization_barrier
    my_pair = lax.axis_index("fsdp").astype(jnp.int32)
    my_expert = lax.axis_index("expert").astype(jnp.int32)
    place = jnp.stack(
        [my_pair, my_expert // 4, my_expert // 2 % 2, my_expert % 2, my_expert, my_expert ^ 1]
    )
    chips = fsdp_size * expert_size // 2
    as_tree = fsdp_size == 2 and layers == 4 and weight_rows % 16 == 0

    blocks = [tokens, swap_pair(tokens), swap_side(tokens)]
    gate_rows, up_rows, down_rows = gate_weight[0].T, up_weight[0].T, down_weight[0]
    if as_tree:
        mine, by_pair, by_side, by_both = group_weights_call(place, attention_in, attention_out)
        both_ways = [
            (f * expert_size + e, (f ^ 1) * expert_size + (e ^ 2))
            for f in range(fsdp_size)
            for e in range(expert_size)
        ]
        rows_here = jnp.stack(
            [mine, swap_pair(by_pair), swap_side(by_side), lax.ppermute(by_both, BOTH, both_ways)]
        )
        rows_here, blocks, gate_rows, up_rows, route_weights = hold(
            (rows_here, blocks, gate_rows, up_rows, route_weights)
        )
        far = swap_layer(rows_here, 2)
        near = swap_layer(rows_here, 1)
    else:
        sent = chip_weights_call(layers, chips, attention_in, attention_out)
        same_core = [[2 * chip + core for chip in range(chips)] for core in range(2)]
        got = lax.all_to_all(
            sent, BOTH, split_axis=0, concat_axis=0, axis_index_groups=same_core, tiled=True
        )
        in_order = jnp.stack([got, swap_core(got)], axis=1)
        in_order = jnp.where(my_expert % 2 == 0, in_order, in_order[:, ::-1])
        pieces = [in_order.reshape(model_width, 8 * HEAD_DIM)]
    blocks.append(swap_side(blocks[1]))
    own_expert = [gate_rows, up_rows, down_rows]
    other_expert = [swap_core(gate_rows), swap_core(up_rows)]
    scale_map, own_tokens, own_gain = scale_call(
        expert_size, routes.T, route_weights.T, blocks[0], attention_gain[None, :]
    )
    blocks[0] = own_tokens
    if as_tree:
        far, near, other_expert, scale_map, blocks, down_rows = hold(
            (far, near, other_expert, scale_map, blocks, down_rows)
        )
        pieces = []
        for piece in (rows_here, near, far, swap_layer(far, 1)):
            pieces += [piece, swap_core(piece)]
    other_expert.append(swap_core(down_rows))

    scale_map = pair_call(scale_map, swap_side(scale_map))
    bit = layers // 2
    while bit > 1:
        scale_map = pair_call(scale_map, swap_layer(scale_map, bit))
        bit //= 2

    keep_top, send_top, keep_low, send_low = attention_call(
        place, own_gain, blocks, pieces, [scale_map, other_expert[2]]
    )

    near_top = swap_side(send_top)
    near_low = swap_pair(send_low)
    own_expert = load_call(own_expert, keep_top)
    scale_map, _ = hold((scale_map, keep_top))
    scale_maps = [scale_map, swap_layer(scale_map, 1)]
    near_top, near_low, own_expert, scale_maps = hold(
        (near_top, near_low, own_expert, scale_maps)
    )
    far_top = swap_pair(sum_call([(keep_top, 1), (near_top, 1)]))
    far_low = swap_side(sum_call([(keep_low, 1), (near_low, 1)]))
    other_expert = load_call(other_expert, near_low)
    far_top, far_low, other_expert = hold((far_top, far_low, other_expert))
    hidden_stream, expert_in = stream_call(
        tokens, expert_gain, keep_top, near_top, far_top, keep_low, near_low, far_low
    )

    arrivals = {0: expert_in}
    order = [0] + sorted(range(1, layers), key=lambda mask: (mask == 1, mask))
    sums, finals, crossings = [], [], []
    for step, mask in enumerate(order):
        low = mask & -mask
        source = arrivals[mask ^ low]
        if mask == 1:
            source, across, _ = hold((source, own_across, block))
            block, across = swap_layer(source, 1), swap_layer(across, 1)
        else:
            block = swap_layer(source, low)
            if step == 1:
                block, _ = hold((block, crossings[0]))
            across = swap_side(block)
        if step == 0:
            own_across = across
        arrivals[mask] = block
        own, crossing = expert_call(
            place,
            [block, across],
            (scale_maps[mask % 2], [mask >> bit & 1 for bit in range(1, layers.bit_length() - 1)]),
            [*own_expert, *other_expert],
            (sums[step - 3 : step - 2] if step >= 3 else []) + crossings[-1:],
        )
        crossings.append(crossing)
        if step == 0:
            finals.append(own)
        elif mask == 1:
            finals.append(swap_layer(own, 1))
        else:
            sums.append(sum_call([own, swap_side(crossing)], finals[1:2] if step == 2 else []))
            finals.append(swap_layer(sums[-1], mask))
    crossing = sum_call([crossings[0], swap_layer(crossings[-1], 1)])
    return mix_call(hidden_stream, [*finals, swap_side(crossing)])


def solution(mesh):
    placed = (
        P(("fsdp", "expert"), None),
        P(),
        P(("fsdp", "expert"), None),
        P(("fsdp", "expert"), None),
        P(),
        P(("fsdp", "expert"), None),
        P(("fsdp", "expert"), None),
        P("expert", None, None),
        P("expert", None, None),
        P("expert", None, None),
    )
    return jax.shard_map(
        per_device,
        mesh=mesh,
        in_specs=placed,
        out_specs=P(("fsdp", "expert"), None),
        check_vma=False,
    )
```

```python
import functools
import math

import jax
import jax.numpy as jnp
from jax import lax
from jax.experimental import pallas as pl
from jax.experimental.pallas import tpu as pltpu
from jax.sharding import PartitionSpec as P

HEAD_DIM = 128
BOTH = ("fsdp", "expert")
VMEM = pl.BlockSpec(memory_space=pltpu.VMEM)
SMEM = pl.BlockSpec(memory_space=pltpu.SMEM)
HBM = pl.BlockSpec(memory_space=pltpu.HBM)
ANYWHERE = pl.BlockSpec(memory_space=pl.ANY)
NT = (((1,), (1,)), ((), ()))


def dot_nt(left, right):
    return lax.dot_general(left, right, NT, preferred_element_type=jnp.float32)


def rms_scale(inputs, scale_gain):
    mean_square = jnp.mean(inputs * inputs, axis=-1, keepdims=True)
    return inputs * lax.rsqrt(mean_square + 1e-06) * scale_gain


def limit(mebibytes):
    return pltpu.CompilerParams(vmem_limit_bytes=mebibytes * 2**20)


def chip_weights_kernel(layers, in_ref, out_ref, sent_ref):
    head_count = out_ref.shape[1] // HEAD_DIM
    pairs = []
    for pair in range(head_count // 2):
        parts = []
        for head in (2 * pair, 2 * pair + 1):
            for part in range(3):
                start = (part * head_count + head) * HEAD_DIM
                parts.append(in_ref[:, start : start + HEAD_DIM])
        parts.append(out_ref[:, 2 * pair * HEAD_DIM : (2 * pair + 2) * HEAD_DIM])
        pairs.append(jnp.concatenate(parts, axis=1))
    for chip in range(sent_ref.shape[0]):
        sent_ref[chip] = pairs[(chip // (2 * layers)) % 2 * 2 + chip % 2]


def chip_weights_call(layers, chips, attention_in, attention_out):
    rows = attention_in.shape[0]
    return pl.pallas_call(
        functools.partial(chip_weights_kernel, layers),
        out_shape=jax.ShapeDtypeStruct((chips, rows, 8 * HEAD_DIM), jnp.bfloat16),
        in_specs=[VMEM] * 2,
        out_specs=VMEM,
        compiler_params=limit(12),
        cost_estimate=pl.CostEstimate(
            flops=0, bytes_accessed=16 * chips * rows * HEAD_DIM, transcendentals=0
        ),
    )(attention_in, attention_out)


def group_weights_kernel(place_ref, in_hbm, out_hbm, *refs):
    sent_refs = refs[:4]
    in_ref, out_ref, sems = refs[4:]
    copies = [
        pltpu.make_async_copy(in_hbm, in_ref, sems.at[0]),
        pltpu.make_async_copy(out_hbm, out_ref, sems.at[1]),
    ]
    for copy in copies:
        copy.start()
    for copy in copies:
        copy.wait()
    width = out_ref.shape[1]
    for index, sent_ref in enumerate(sent_refs):
        pair = (place_ref[0] ^ (index % 2)) * 2 + (place_ref[2] ^ (index // 2))
        start = pl.multiple_of(pair * (2 * HEAD_DIM), HEAD_DIM)
        for part in range(3):
            both = in_ref[:, pl.ds(pl.multiple_of(start + part * width, HEAD_DIM), 2 * HEAD_DIM)]
            for head in range(2):
                to = (3 * head + part) * HEAD_DIM
                sent_ref[:, to : to + HEAD_DIM] = both[:, head * HEAD_DIM : (head + 1) * HEAD_DIM]
        sent_ref[:, 6 * HEAD_DIM :] = out_ref[:, pl.ds(start, 2 * HEAD_DIM)]


def group_weights_call(place, attention_in, attention_out):
    rows = attention_in.shape[0]
    one = jax.ShapeDtypeStruct((rows, 8 * HEAD_DIM), jnp.bfloat16)
    return pl.pallas_call(
        group_weights_kernel,
        out_shape=(one,) * 4,
        in_specs=[SMEM, HBM, HBM],
        out_specs=(VMEM,) * 4,
        scratch_shapes=[
            pltpu.VMEM(attention_in.shape, jnp.bfloat16),
            pltpu.VMEM(attention_out.shape, jnp.bfloat16),
            pltpu.SemaphoreType.DMA((2,)),
        ],
        compiler_params=limit(8),
        cost_estimate=pl.CostEstimate(
            flops=0, bytes_accessed=128 * rows * HEAD_DIM, transcendentals=0
        ),
    )(place, attention_in, attention_out)


def attention_kernel(block_count, piece_count, *refs):
    place_ref, gain_ref = refs[:2]
    block_refs = refs[2 : 2 + block_count]
    piece_refs = refs[2 + block_count : 2 + block_count + piece_count]
    keep_top_ref, send_top_ref, keep_low_ref, send_low_ref, weight_ref = refs[-5:]
    rows = block_refs[0].shape[0]
    half = rows // 2
    if piece_count == 1:
        weight_ref = piece_refs[0]
    else:
        layers = piece_count // 2
        for index, piece_ref in enumerate(piece_refs):
            layer, core = place_ref[1] ^ (index // 2), place_ref[3] ^ (index % 2)
            for chip in range(4):
                pair, side = place_ref[0] ^ (chip % 2), place_ref[2] ^ (chip // 2)
                device = ((pair * layers + layer) * 2 + side) * 2 + core
                span = piece_ref.shape[1]
                start = pl.multiple_of(device * span, 16)
                weight_ref[pl.ds(start, span), :] = piece_ref[chip]
    out_weights = weight_ref[:, 6 * HEAD_DIM :]
    causal = lax.broadcasted_iota(jnp.int32, (rows, rows), 0) >= lax.broadcasted_iota(
        jnp.int32, (rows, rows), 1
    )
    inputs = jnp.concatenate(
        [
            rms_scale(ref[...].astype(jnp.float32), gain_ref[...]).astype(jnp.bfloat16)
            for ref in block_refs
        ],
        axis=0,
    )
    heads = []
    for head in range(2):
        projected = jnp.dot(
            inputs,
            weight_ref[:, 3 * head * HEAD_DIM : 3 * (head + 1) * HEAD_DIM],
            preferred_element_type=jnp.float32,
        ).astype(jnp.bfloat16)
        outs = []
        for block in range(block_count):
            own = projected[block * rows : (block + 1) * rows]
            queries = own[:, :HEAD_DIM]
            keys = own[:, HEAD_DIM : 2 * HEAD_DIM]
            values = own[:, 2 * HEAD_DIM :]
            scores = dot_nt(queries, keys) * (1.0 / math.sqrt(HEAD_DIM))
            raised = jnp.where(causal, jnp.exp(jnp.where(causal, scores, 0.0)), 0.0)
            probs = raised / jnp.sum(raised, axis=-1, keepdims=True)
            outs.append(
                jnp.dot(
                    probs.astype(jnp.bfloat16), values, preferred_element_type=jnp.float32
                ).astype(jnp.bfloat16)
            )
        heads.append(jnp.concatenate(outs, axis=0))
    part = dot_nt(jnp.concatenate(heads, axis=1), out_weights).astype(jnp.bfloat16)
    for block in range(block_count):
        across, along = block // 2, block % 2
        top = send_top_ref if across else keep_top_ref
        low = send_low_ref if along else keep_low_ref
        top[along] = part[block * rows : block * rows + half]
        low[across] = part[block * rows + half : (block + 1) * rows]


def attention_call(place, gain, blocks, pieces, after):
    count = len(blocks)
    rows, width = blocks[0].shape
    tokens = count * rows
    out = jax.ShapeDtypeStruct((count // 2, rows // 2, width), jnp.bfloat16)
    return pl.pallas_call(
        functools.partial(attention_kernel, count, len(pieces)),
        out_shape=(out,) * 4,
        in_specs=[SMEM] + [VMEM] * (1 + count + len(pieces)) + [ANYWHERE] * len(after),
        out_specs=(VMEM,) * 4,
        scratch_shapes=[
            pltpu.VMEM((width, 8 * HEAD_DIM) if len(pieces) > 1 else (16, 128), jnp.bfloat16)
        ],
        compiler_params=limit(16),
        cost_estimate=pl.CostEstimate(
            flops=4 * tokens * (width * 4 * HEAD_DIM + 2 * rows * HEAD_DIM),
            bytes_accessed=4 * tokens * width + width * 16 * HEAD_DIM,
            transcendentals=2 * tokens * rows,
        ),
    )(place, gain, *blocks, *pieces, *after)


def sum_kernel(picks, *refs):
    out_ref = refs[-1]
    total = None
    for ref, pick in zip(refs, picks):
        term = (ref[...] if pick is None else ref[pick]).astype(jnp.float32)
        total = term if total is None else total + term
    out_ref[...] = total.astype(out_ref.dtype)


def sum_call(terms, after=()):
    arrays = [term[0] if isinstance(term, tuple) else term for term in terms]
    picks = [term[1] if isinstance(term, tuple) else None for term in terms]
    shape = arrays[0].shape if picks[0] is None else arrays[0].shape[1:]
    return pl.pallas_call(
        functools.partial(sum_kernel, picks),
        out_shape=jax.ShapeDtypeStruct(shape, jnp.bfloat16),
        in_specs=[VMEM] * len(arrays) + [ANYWHERE] * len(after),
        out_specs=VMEM,
        compiler_params=limit(12),
        cost_estimate=pl.CostEstimate(
            flops=len(arrays) * math.prod(shape),
            bytes_accessed=2 * (len(arrays) + 1) * math.prod(shape),
            transcendentals=0,
        ),
    )(*arrays, *after)


def stream_kernel(tokens_ref, gain_ref, *refs):
    hidden_ref, normed_ref = refs[-2:]
    half = tokens_ref.shape[0] // 2
    for index in range(2):
        keep_ref, near_ref, far_ref = refs[3 * index : 3 * index + 3]
        rows = pl.ds(index * half, half)
        hidden = (
            tokens_ref[rows, :].astype(jnp.float32)
            + keep_ref[0].astype(jnp.float32)
            + near_ref[0].astype(jnp.float32)
            + far_ref[...].astype(jnp.float32)
        )
        hidden_ref[rows, :] = hidden
        normed_ref[rows, :] = rms_scale(hidden, gain_ref[...]).astype(jnp.bfloat16)


def stream_call(tokens, gain, *parts):
    return pl.pallas_call(
        stream_kernel,
        out_shape=(
            jax.ShapeDtypeStruct(tokens.shape, jnp.float32),
            jax.ShapeDtypeStruct(tokens.shape, jnp.bfloat16),
        ),
        in_specs=[VMEM] * 8,
        out_specs=(VMEM, VMEM),
        compiler_params=limit(12),
        cost_estimate=pl.CostEstimate(
            flops=6 * tokens.size, bytes_accessed=14 * tokens.size, transcendentals=0
        ),
    )(tokens, gain[None, :], *parts)


def expert_kernel(tiles, pick, *refs):
    place_ref = refs[0]
    block_refs = refs[1:3]
    scale_ref = refs[3]
    weight_refs = refs[4:10]
    own_ref, side_ref = refs[-2:]
    inputs = jnp.concatenate([ref[...] for ref in block_refs], axis=0)
    result = None
    for expert in range(2):
        gate_ref, up_ref, down_ref = weight_refs[3 * expert : 3 * expert + 3]
        scale = jnp.concatenate(
            [scale_ref[*pick, block, pl.ds(place_ref[4 + expert], 1), :] for block in range(2)],
            axis=1,
        )
        for start, size in tiles:
            gate_value = dot_nt(gate_ref[start : start + size, :], inputs)
            up_value = dot_nt(up_ref[start : start + size, :], inputs)
            inner = gate_value / (1.0 + jnp.exp(-gate_value)) * (up_value * scale)
            term = jnp.dot(
                down_ref[:, start : start + size],
                inner.astype(jnp.bfloat16),
                preferred_element_type=jnp.float32,
            )
            result = term if result is None else result + term
    result = result.astype(jnp.bfloat16)
    rows = block_refs[0].shape[0]
    own_ref[...] = result[:, :rows]
    side_ref[...] = result[:, rows:]


def expert_call(place, blocks, picked, weights, after):
    scale_map, pick = picked
    rows, width = blocks[0].shape
    hidden = weights[0].shape[0]
    tiles = [(start, min(256, hidden - start)) for start in range(0, hidden, 256)]
    one = jax.ShapeDtypeStruct((width, rows), jnp.bfloat16)
    return pl.pallas_call(
        functools.partial(expert_kernel, tiles, pick),
        out_shape=(one,) * 2,
        in_specs=[SMEM] + [VMEM] * 9 + [ANYWHERE] * len(after),
        out_specs=(VMEM,) * 2,
        compiler_params=limit(20),
        cost_estimate=pl.CostEstimate(
            flops=2 * 4 * rows * width * hidden * 3,
            bytes_accessed=12 * hidden * width + 8 * rows * width,
            transcendentals=4 * rows * hidden,
        ),
    )(place, *blocks, scale_map, *weights, *after)


def scale_kernel(routes_ref, weights_ref, tokens_ref, gain_ref, map_ref, tokens_out, gain_out):
    top_count, rows = routes_ref.shape
    experts = lax.broadcasted_iota(jnp.int32, (map_ref.shape[0], rows), 0)
    total = jnp.zeros(map_ref.shape, jnp.float32)
    for choice in range(top_count):
        chosen = experts == routes_ref[choice : choice + 1, :]
        total = total + jnp.where(chosen, weights_ref[choice : choice + 1, :], 0.0)
    map_ref[...] = total
    tokens_out[...] = tokens_ref[...]
    gain_out[...] = gain_ref[...]


def scale_call(expert_size, routes, weights, tokens, gain):
    rows = routes.shape[1]
    return pl.pallas_call(
        scale_kernel,
        out_shape=(
            jax.ShapeDtypeStruct((expert_size, rows), jnp.float32),
            jax.ShapeDtypeStruct(tokens.shape, tokens.dtype),
            jax.ShapeDtypeStruct(gain.shape, gain.dtype),
        ),
        in_specs=[VMEM] * 4,
        out_specs=(VMEM,) * 3,
        compiler_params=limit(8),
    )(routes, weights, tokens, gain)


def pair_kernel(first_ref, second_ref, pair_ref):
    pair_ref[0] = first_ref[...]
    pair_ref[1] = second_ref[...]


def pair_call(first, second):
    return pl.pallas_call(
        pair_kernel,
        out_shape=jax.ShapeDtypeStruct((2, *first.shape), first.dtype),
        in_specs=[VMEM] * 2,
        out_specs=VMEM,
        compiler_params=limit(8),
    )(first, second)


def load_kernel(gate_hbm, up_hbm, down_hbm, after_ref, gate_ref, up_ref, turned_ref, down_ref, sems):
    copies = [
        pltpu.make_async_copy(source, target, sems.at[index])
        for index, (source, target) in enumerate(
            ((down_hbm, down_ref), (gate_hbm, gate_ref), (up_hbm, up_ref))
        )
    ]
    for copy in copies:
        copy.start()
    copies[0].wait()
    columns, rows = down_ref.shape
    turned_ref[:, :columns] = down_ref[...].T
    if turned_ref.shape[1] > columns:
        turned_ref[:, columns:] = jnp.zeros((rows, turned_ref.shape[1] - columns), turned_ref.dtype)
    for copy in copies[1:]:
        copy.wait()


def load_call(weights, after):
    gate, _, down = weights
    rows, columns = down.shape
    return pl.pallas_call(
        load_kernel,
        out_shape=(
            jax.ShapeDtypeStruct(gate.shape, gate.dtype),
            jax.ShapeDtypeStruct(gate.shape, gate.dtype),
            jax.ShapeDtypeStruct((columns, -(-rows // 128) * 128), down.dtype),
        ),
        in_specs=[HBM] * 3 + [ANYWHERE],
        out_specs=(VMEM,) * 3,
        scratch_shapes=[pltpu.VMEM(down.shape, down.dtype), pltpu.SemaphoreType.DMA((3,))],
        compiler_params=limit(16),
        cost_estimate=pl.CostEstimate(
            flops=0, bytes_accessed=12 * gate.size, transcendentals=0
        ),
    )(*weights, after)


def mix_kernel(hidden_ref, *refs):
    total = refs[0][...].astype(jnp.float32)
    for ref in refs[1:-1]:
        total = total + ref[...].astype(jnp.float32)
    refs[-1][...] = (hidden_ref[...] + total.T).astype(jnp.bfloat16)


def mix_call(hidden, terms):
    return pl.pallas_call(
        mix_kernel,
        out_shape=jax.ShapeDtypeStruct(hidden.shape, jnp.bfloat16),
        in_specs=[VMEM] * (1 + len(terms)),
        out_specs=VMEM,
        compiler_params=limit(12),
        cost_estimate=pl.CostEstimate(
            flops=(1 + len(terms)) * hidden.size,
            bytes_accessed=(6 + 2 * len(terms)) * hidden.size,
            transcendentals=0,
        ),
    )(hidden, *terms)


def per_device(
    tokens,
    attention_gain,
    attention_in,
    attention_out,
    expert_gain,
    routes,
    route_weights,
    gate_weight,
    up_weight,
    down_weight,
):
    fsdp_size = lax.axis_size("fsdp")
    expert_size = lax.axis_size("expert")
    row_count, model_width = tokens.shape
    weight_rows = attention_out.shape[0]
    layers = expert_size // 4

    def swap_pair(value):
        return lax.ppermute(value, "fsdp", [(f, f ^ 1) for f in range(fsdp_size)])

    def swap_expert(value, mask):
        return lax.ppermute(value, "expert", [(e, e ^ mask) for e in range(expert_size)])

    def swap_core(value):
        return swap_expert(value, 1)

    def swap_side(value):
        return swap_expert(value, 2)

    def swap_layer(value, mask):
        return swap_expert(value, 4 * mask) if mask else value

    hold = lax.optimization_barrier
    my_pair = lax.axis_index("fsdp").astype(jnp.int32)
    my_expert = lax.axis_index("expert").astype(jnp.int32)
    place = jnp.stack(
        [my_pair, my_expert // 4, my_expert // 2 % 2, my_expert % 2, my_expert, my_expert ^ 1]
    )
    chips = fsdp_size * expert_size // 2
    as_tree = fsdp_size == 2 and layers == 4 and weight_rows % 16 == 0

    blocks = [tokens, swap_pair(tokens), swap_side(tokens)]
    gate_rows, up_rows, down_rows = gate_weight[0].T, up_weight[0].T, down_weight[0]
    if as_tree:
        mine, by_pair, by_side, by_both = group_weights_call(place, attention_in, attention_out)
        both_ways = [
            (f * expert_size + e, (f ^ 1) * expert_size + (e ^ 2))
            for f in range(fsdp_size)
            for e in range(expert_size)
        ]
        rows_here = jnp.stack(
            [mine, swap_pair(by_pair), swap_side(by_side), lax.ppermute(by_both, BOTH, both_ways)]
        )
        rows_here, blocks, gate_rows, up_rows, route_weights = hold(
            (rows_here, blocks, gate_rows, up_rows, route_weights)
        )
        far = swap_layer(rows_here, 2)
        near = swap_layer(rows_here, 1)
    else:
        sent = chip_weights_call(layers, chips, attention_in, attention_out)
        same_core = [[2 * chip + core for chip in range(chips)] for core in range(2)]
        got = lax.all_to_all(
            sent, BOTH, split_axis=0, concat_axis=0, axis_index_groups=same_core, tiled=True
        )
        in_order = jnp.stack([got, swap_core(got)], axis=1)
        in_order = jnp.where(my_expert % 2 == 0, in_order, in_order[:, ::-1])
        pieces = [in_order.reshape(model_width, 8 * HEAD_DIM)]
    blocks.append(swap_side(blocks[1]))
    own_expert = [gate_rows, up_rows, down_rows]
    other_expert = [swap_core(gate_rows), swap_core(up_rows)]
    scale_map, own_tokens, own_gain = scale_call(
        expert_size, routes.T, route_weights.T, blocks[0], attention_gain[None, :]
    )
    blocks[0] = own_tokens
    if as_tree:
        far, near, other_expert, scale_map, blocks, down_rows = hold(
            (far, near, other_expert, scale_map, blocks, down_rows)
        )
        pieces = []
        for piece in (rows_here, near, far, swap_layer(far, 1)):
            pieces += [piece, swap_core(piece)]
    other_expert.append(swap_core(down_rows))

    scale_map = pair_call(scale_map, swap_side(scale_map))
    bit = layers // 2
    while bit > 1:
        scale_map = pair_call(scale_map, swap_layer(scale_map, bit))
        bit //= 2

    keep_top, send_top, keep_low, send_low = attention_call(
        place, own_gain, blocks, pieces, [scale_map, other_expert[2]]
    )

    near_top = swap_side(send_top)
    near_low = swap_pair(send_low)
    own_expert = load_call(own_expert, keep_top)
    scale_map, _ = hold((scale_map, keep_top))
    scale_maps = [scale_map, swap_layer(scale_map, 1)]
    near_top, near_low, own_expert, scale_maps = hold(
        (near_top, near_low, own_expert, scale_maps)
    )
    far_top = swap_pair(sum_call([(keep_top, 1), (near_top, 1)]))
    far_low = swap_side(sum_call([(keep_low, 1), (near_low, 1)]))
    other_expert = load_call(other_expert, near_low)
    far_top, far_low, other_expert = hold((far_top, far_low, other_expert))
    hidden_stream, expert_in = stream_call(
        tokens, expert_gain, keep_top, near_top, far_top, keep_low, near_low, far_low
    )

    arrivals = {0: expert_in}
    order = [0] + sorted(range(1, layers), key=lambda mask: (mask == 1, mask))
    sums, finals, crossings = [], [], []
    for step, mask in enumerate(order):
        low = mask & -mask
        source = arrivals[mask ^ low]
        if mask == 1 and step >= 2:
            source, _ = hold((source, block))
        block = swap_layer(source, low)
        if step == 1:
            block, _ = hold((block, crossings[0]))
        arrivals[mask] = block
        own, crossing = expert_call(
            place,
            [block, swap_side(block)],
            (scale_maps[mask % 2], [mask >> bit & 1 for bit in range(1, layers.bit_length() - 1)]),
            [*own_expert, *other_expert],
            (sums[step - 3 : step - 2] if step >= 3 else []) + crossings[-1:],
        )
        crossings.append(crossing)
        if step == 0:
            first = own
        else:
            sums.append(sum_call([own, swap_side(crossing)], finals[:1] if step == 2 else []))
            finals.append(swap_layer(sums[-1], mask))
    crossing, _ = hold((crossings[0], sums[-1]))
    return mix_call(hidden_stream, [first, *finals, swap_side(crossing)])


def solution(mesh):
    placed = (
        P(("fsdp", "expert"), None),
        P(),
        P(("fsdp", "expert"), None),
        P(("fsdp", "expert"), None),
        P(),
        P(("fsdp", "expert"), None),
        P(("fsdp", "expert"), None),
        P("expert", None, None),
        P("expert", None, None),
        P("expert", None, None),
    )
    return jax.shard_map(
        per_device,
        mesh=mesh,
        in_specs=placed,
        out_specs=P(("fsdp", "expert"), None),
        check_vma=False,
    )
```

```python
import functools
import math

import jax
import jax.numpy as jnp
from jax import lax
from jax.experimental import pallas as pl
from jax.experimental.pallas import tpu as pltpu
from jax.sharding import PartitionSpec as P

HEAD_DIM = 128
BOTH = ("fsdp", "expert")
VMEM = pl.BlockSpec(memory_space=pltpu.VMEM)
SMEM = pl.BlockSpec(memory_space=pltpu.SMEM)
HBM = pl.BlockSpec(memory_space=pltpu.HBM)
ANYWHERE = pl.BlockSpec(memory_space=pl.ANY)
NT = (((1,), (1,)), ((), ()))


def dot_nt(left, right):
    return lax.dot_general(left, right, NT, preferred_element_type=jnp.float32)


def rms_scale(inputs, scale_gain):
    mean_square = jnp.mean(inputs * inputs, axis=-1, keepdims=True)
    return inputs * lax.rsqrt(mean_square + 1e-06) * scale_gain


def limit(mebibytes):
    return pltpu.CompilerParams(vmem_limit_bytes=mebibytes * 2**20)


def chip_weights_kernel(layers, in_ref, out_ref, sent_ref):
    head_count = out_ref.shape[1] // HEAD_DIM
    pairs = []
    for pair in range(head_count // 2):
        parts = []
        for head in (2 * pair, 2 * pair + 1):
            for part in range(3):
                start = (part * head_count + head) * HEAD_DIM
                parts.append(in_ref[:, start : start + HEAD_DIM])
        parts.append(out_ref[:, 2 * pair * HEAD_DIM : (2 * pair + 2) * HEAD_DIM])
        pairs.append(jnp.concatenate(parts, axis=1))
    for chip in range(sent_ref.shape[0]):
        sent_ref[chip] = pairs[(chip // (2 * layers)) % 2 * 2 + chip % 2]


def chip_weights_call(layers, chips, attention_in, attention_out):
    rows = attention_in.shape[0]
    return pl.pallas_call(
        functools.partial(chip_weights_kernel, layers),
        out_shape=jax.ShapeDtypeStruct((chips, rows, 8 * HEAD_DIM), jnp.bfloat16),
        in_specs=[VMEM] * 2,
        out_specs=VMEM,
        compiler_params=limit(12),
        cost_estimate=pl.CostEstimate(
            flops=0, bytes_accessed=16 * chips * rows * HEAD_DIM, transcendentals=0
        ),
    )(attention_in, attention_out)


def group_weights_kernel(place_ref, in_hbm, out_hbm, *refs):
    sent_refs = refs[:4]
    in_ref, out_ref, sems = refs[4:]
    copies = [
        pltpu.make_async_copy(in_hbm, in_ref, sems.at[0]),
        pltpu.make_async_copy(out_hbm, out_ref, sems.at[1]),
    ]
    for copy in copies:
        copy.start()
    for copy in copies:
        copy.wait()
    width = out_ref.shape[1]
    for index, sent_ref in enumerate(sent_refs):
        pair = (place_ref[0] ^ (index % 2)) * 2 + (place_ref[2] ^ (index // 2))
        start = pl.multiple_of(pair * (2 * HEAD_DIM), HEAD_DIM)
        for part in range(3):
            both = in_ref[:, pl.ds(pl.multiple_of(start + part * width, HEAD_DIM), 2 * HEAD_DIM)]
            for head in range(2):
                to = (3 * head + part) * HEAD_DIM
                sent_ref[:, to : to + HEAD_DIM] = both[:, head * HEAD_DIM : (head + 1) * HEAD_DIM]
        sent_ref[:, 6 * HEAD_DIM :] = out_ref[:, pl.ds(start, 2 * HEAD_DIM)]


def group_weights_call(place, attention_in, attention_out):
    rows = attention_in.shape[0]
    one = jax.ShapeDtypeStruct((rows, 8 * HEAD_DIM), jnp.bfloat16)
    return pl.pallas_call(
        group_weights_kernel,
        out_shape=(one,) * 4,
        in_specs=[SMEM, HBM, HBM],
        out_specs=(VMEM,) * 4,
        scratch_shapes=[
            pltpu.VMEM(attention_in.shape, jnp.bfloat16),
            pltpu.VMEM(attention_out.shape, jnp.bfloat16),
            pltpu.SemaphoreType.DMA((2,)),
        ],
        compiler_params=limit(8),
        cost_estimate=pl.CostEstimate(
            flops=0, bytes_accessed=128 * rows * HEAD_DIM, transcendentals=0
        ),
    )(place, attention_in, attention_out)


def attention_kernel(block_count, piece_count, *refs):
    place_ref, gain_ref = refs[:2]
    block_refs = refs[2 : 2 + block_count]
    piece_refs = refs[2 + block_count : 2 + block_count + piece_count]
    keep_top_ref, send_top_ref, keep_low_ref, send_low_ref, weight_ref = refs[-5:]
    rows = block_refs[0].shape[0]
    half = rows // 2
    if piece_count == 1:
        weight_ref = piece_refs[0]
    else:
        layers = piece_count // 2
        for index, piece_ref in enumerate(piece_refs):
            layer, core = place_ref[1] ^ (index // 2), place_ref[3] ^ (index % 2)
            for chip in range(4):
                pair, side = place_ref[0] ^ (chip % 2), place_ref[2] ^ (chip // 2)
                device = ((pair * layers + layer) * 2 + side) * 2 + core
                span = piece_ref.shape[1]
                start = pl.multiple_of(device * span, 16)
                weight_ref[pl.ds(start, span), :] = piece_ref[chip]
    out_weights = weight_ref[:, 6 * HEAD_DIM :]
    causal = lax.broadcasted_iota(jnp.int32, (rows, rows), 0) >= lax.broadcasted_iota(
        jnp.int32, (rows, rows), 1
    )
    inputs = jnp.concatenate(
        [
            rms_scale(ref[...].astype(jnp.float32), gain_ref[...]).astype(jnp.bfloat16)
            for ref in block_refs
        ],
        axis=0,
    )
    heads = []
    for head in range(2):
        projected = jnp.dot(
            inputs,
            weight_ref[:, 3 * head * HEAD_DIM : 3 * (head + 1) * HEAD_DIM],
            preferred_element_type=jnp.float32,
        ).astype(jnp.bfloat16)
        outs = []
        for block in range(block_count):
            own = projected[block * rows : (block + 1) * rows]
            queries = own[:, :HEAD_DIM]
            keys = own[:, HEAD_DIM : 2 * HEAD_DIM]
            values = own[:, 2 * HEAD_DIM :]
            scores = dot_nt(queries, keys) * (1.0 / math.sqrt(HEAD_DIM))
            raised = jnp.where(causal, jnp.exp(jnp.where(causal, scores, 0.0)), 0.0)
            probs = raised * (1.0 / jnp.sum(raised, axis=-1, keepdims=True))
            outs.append(
                jnp.dot(
                    probs.astype(jnp.bfloat16), values, preferred_element_type=jnp.float32
                ).astype(jnp.bfloat16)
            )
        heads.append(jnp.concatenate(outs, axis=0))
    part = dot_nt(jnp.concatenate(heads, axis=1), out_weights).astype(jnp.bfloat16)
    for block in range(block_count):
        across, along = block // 2, block % 2
        top = send_top_ref if across else keep_top_ref
        low = send_low_ref if along else keep_low_ref
        top[along] = part[block * rows : block * rows + half]
        low[across] = part[block * rows + half : (block + 1) * rows]


def attention_call(place, gain, blocks, pieces, after):
    count = len(blocks)
    rows, width = blocks[0].shape
    tokens = count * rows
    out = jax.ShapeDtypeStruct((count // 2, rows // 2, width), jnp.bfloat16)
    return pl.pallas_call(
        functools.partial(attention_kernel, count, len(pieces)),
        out_shape=(out,) * 4,
        in_specs=[SMEM] + [VMEM] * (1 + count + len(pieces)) + [ANYWHERE] * len(after),
        out_specs=(VMEM,) * 4,
        scratch_shapes=[
            pltpu.VMEM((width, 8 * HEAD_DIM) if len(pieces) > 1 else (16, 128), jnp.bfloat16)
        ],
        compiler_params=limit(16),
        cost_estimate=pl.CostEstimate(
            flops=4 * tokens * (width * 4 * HEAD_DIM + 2 * rows * HEAD_DIM),
            bytes_accessed=4 * tokens * width + width * 16 * HEAD_DIM,
            transcendentals=2 * tokens * rows,
        ),
    )(place, gain, *blocks, *pieces, *after)


def sum_kernel(picks, *refs):
    out_ref = refs[-1]
    total = None
    for ref, pick in zip(refs, picks):
        term = (ref[...] if pick is None else ref[pick]).astype(jnp.float32)
        total = term if total is None else total + term
    out_ref[...] = total.astype(out_ref.dtype)


def sum_call(terms, after=()):
    arrays = [term[0] if isinstance(term, tuple) else term for term in terms]
    picks = [term[1] if isinstance(term, tuple) else None for term in terms]
    shape = arrays[0].shape if picks[0] is None else arrays[0].shape[1:]
    return pl.pallas_call(
        functools.partial(sum_kernel, picks),
        out_shape=jax.ShapeDtypeStruct(shape, jnp.bfloat16),
        in_specs=[VMEM] * len(arrays) + [ANYWHERE] * len(after),
        out_specs=VMEM,
        compiler_params=limit(12),
        cost_estimate=pl.CostEstimate(
            flops=len(arrays) * math.prod(shape),
            bytes_accessed=2 * (len(arrays) + 1) * math.prod(shape),
            transcendentals=0,
        ),
    )(*arrays, *after)


def stream_kernel(tokens_ref, gain_ref, *refs):
    hidden_ref, normed_ref = refs[-2:]
    half = tokens_ref.shape[0] // 2
    for index in range(2):
        keep_ref, near_ref, far_ref = refs[3 * index : 3 * index + 3]
        rows = pl.ds(index * half, half)
        hidden = (
            tokens_ref[rows, :].astype(jnp.float32)
            + keep_ref[0].astype(jnp.float32)
            + near_ref[0].astype(jnp.float32)
            + far_ref[...].astype(jnp.float32)
        )
        hidden_ref[rows, :] = hidden
        normed_ref[rows, :] = rms_scale(hidden, gain_ref[...]).astype(jnp.bfloat16)


def stream_call(tokens, gain, *parts):
    return pl.pallas_call(
        stream_kernel,
        out_shape=(
            jax.ShapeDtypeStruct(tokens.shape, jnp.float32),
            jax.ShapeDtypeStruct(tokens.shape, jnp.bfloat16),
        ),
        in_specs=[VMEM] * 8,
        out_specs=(VMEM, VMEM),
        compiler_params=limit(12),
        cost_estimate=pl.CostEstimate(
            flops=6 * tokens.size, bytes_accessed=14 * tokens.size, transcendentals=0
        ),
    )(tokens, gain[None, :], *parts)


def expert_kernel(tiles, pick, *refs):
    place_ref = refs[0]
    block_refs = refs[1:3]
    scale_ref = refs[3]
    weight_refs = refs[4:10]
    own_ref, side_ref = refs[-2:]
    inputs = jnp.concatenate([ref[...] for ref in block_refs], axis=0)
    result = None
    for expert in range(2):
        gate_ref, up_ref, down_ref = weight_refs[3 * expert : 3 * expert + 3]
        scale = jnp.concatenate(
            [scale_ref[*pick, block, pl.ds(place_ref[4 + expert], 1), :] for block in range(2)],
            axis=1,
        )
        inner = []
        for start, size in tiles:
            gate_value = dot_nt(gate_ref[start : start + size, :], inputs)
            up_value = dot_nt(up_ref[start : start + size, :], inputs)
            half = 0.5 * gate_value
            inner.append(((half + half * jnp.tanh(half)) * (up_value * scale)).astype(jnp.bfloat16))
        inner = jnp.concatenate(inner, axis=0)
        term = jnp.dot(
            down_ref[:, : inner.shape[0]], inner, preferred_element_type=jnp.float32
        )
        result = term if result is None else result + term
    result = result.astype(jnp.bfloat16)
    rows = block_refs[0].shape[0]
    own_ref[...] = result[:, :rows]
    side_ref[...] = result[:, rows:]


def expert_call(place, blocks, picked, weights, after):
    scale_map, pick = picked
    rows, width = blocks[0].shape
    hidden = weights[0].shape[0]
    tiles = [(start, min(256, hidden - start)) for start in range(0, hidden, 256)]
    one = jax.ShapeDtypeStruct((width, rows), jnp.bfloat16)
    return pl.pallas_call(
        functools.partial(expert_kernel, tiles, pick),
        out_shape=(one,) * 2,
        in_specs=[SMEM] + [VMEM] * 9 + [ANYWHERE] * len(after),
        out_specs=(VMEM,) * 2,
        compiler_params=limit(20),
        cost_estimate=pl.CostEstimate(
            flops=2 * 4 * rows * width * hidden * 3,
            bytes_accessed=12 * hidden * width + 8 * rows * width,
            transcendentals=4 * rows * hidden,
        ),
    )(place, *blocks, scale_map, *weights, *after)


def scale_kernel(routes_ref, weights_ref, tokens_ref, gain_ref, map_ref, tokens_out, gain_out):
    top_count, rows = routes_ref.shape
    experts = lax.broadcasted_iota(jnp.int32, (map_ref.shape[0], rows), 0)
    total = jnp.zeros(map_ref.shape, jnp.float32)
    for choice in range(top_count):
        chosen = experts == routes_ref[choice : choice + 1, :]
        total = total + jnp.where(chosen, weights_ref[choice : choice + 1, :], 0.0)
    map_ref[...] = total
    tokens_out[...] = tokens_ref[...]
    gain_out[...] = gain_ref[...]


def scale_call(expert_size, routes, weights, tokens, gain):
    rows = routes.shape[1]
    return pl.pallas_call(
        scale_kernel,
        out_shape=(
            jax.ShapeDtypeStruct((expert_size, rows), jnp.float32),
            jax.ShapeDtypeStruct(tokens.shape, tokens.dtype),
            jax.ShapeDtypeStruct(gain.shape, gain.dtype),
        ),
        in_specs=[VMEM] * 4,
        out_specs=(VMEM,) * 3,
        compiler_params=limit(8),
    )(routes, weights, tokens, gain)


def pair_kernel(first_ref, second_ref, pair_ref):
    pair_ref[0] = first_ref[...]
    pair_ref[1] = second_ref[...]


def pair_call(first, second):
    return pl.pallas_call(
        pair_kernel,
        out_shape=jax.ShapeDtypeStruct((2, *first.shape), first.dtype),
        in_specs=[VMEM] * 2,
        out_specs=VMEM,
        compiler_params=limit(8),
    )(first, second)


def load_kernel(gate_hbm, up_hbm, down_hbm, after_ref, gate_ref, up_ref, turned_ref, down_ref, sems):
    copies = [
        pltpu.make_async_copy(source, target, sems.at[index])
        for index, (source, target) in enumerate(
            ((down_hbm, down_ref), (gate_hbm, gate_ref), (up_hbm, up_ref))
        )
    ]
    for copy in copies:
        copy.start()
    copies[0].wait()
    columns, rows = down_ref.shape
    turned_ref[:, :columns] = down_ref[...].T
    if turned_ref.shape[1] > columns:
        turned_ref[:, columns:] = jnp.zeros((rows, turned_ref.shape[1] - columns), turned_ref.dtype)
    for copy in copies[1:]:
        copy.wait()


def load_call(weights, after):
    gate, _, down = weights
    rows, columns = down.shape
    return pl.pallas_call(
        load_kernel,
        out_shape=(
            jax.ShapeDtypeStruct(gate.shape, gate.dtype),
            jax.ShapeDtypeStruct(gate.shape, gate.dtype),
            jax.ShapeDtypeStruct((columns, -(-rows // 128) * 128), down.dtype),
        ),
        in_specs=[HBM] * 3 + [ANYWHERE],
        out_specs=(VMEM,) * 3,
        scratch_shapes=[pltpu.VMEM(down.shape, down.dtype), pltpu.SemaphoreType.DMA((3,))],
        compiler_params=limit(16),
        cost_estimate=pl.CostEstimate(
            flops=0, bytes_accessed=12 * gate.size, transcendentals=0
        ),
    )(*weights, after)


def mix_kernel(hidden_ref, *refs):
    total = refs[0][...].astype(jnp.float32)
    for ref in refs[1:-1]:
        total = total + ref[...].astype(jnp.float32)
    refs[-1][...] = (hidden_ref[...] + total.T).astype(jnp.bfloat16)


def mix_call(hidden, terms):
    return pl.pallas_call(
        mix_kernel,
        out_shape=jax.ShapeDtypeStruct(hidden.shape, jnp.bfloat16),
        in_specs=[VMEM] * (1 + len(terms)),
        out_specs=VMEM,
        compiler_params=limit(12),
        cost_estimate=pl.CostEstimate(
            flops=(1 + len(terms)) * hidden.size,
            bytes_accessed=(6 + 2 * len(terms)) * hidden.size,
            transcendentals=0,
        ),
    )(hidden, *terms)


def per_device(
    tokens,
    attention_gain,
    attention_in,
    attention_out,
    expert_gain,
    routes,
    route_weights,
    gate_weight,
    up_weight,
    down_weight,
):
    fsdp_size = lax.axis_size("fsdp")
    expert_size = lax.axis_size("expert")
    row_count, model_width = tokens.shape
    weight_rows = attention_out.shape[0]
    layers = expert_size // 4

    def swap_pair(value):
        return lax.ppermute(value, "fsdp", [(f, f ^ 1) for f in range(fsdp_size)])

    def swap_expert(value, mask):
        return lax.ppermute(value, "expert", [(e, e ^ mask) for e in range(expert_size)])

    def swap_core(value):
        return swap_expert(value, 1)

    def swap_side(value):
        return swap_expert(value, 2)

    def swap_layer(value, mask):
        return swap_expert(value, 4 * mask) if mask else value

    hold = lax.optimization_barrier
    my_pair = lax.axis_index("fsdp").astype(jnp.int32)
    my_expert = lax.axis_index("expert").astype(jnp.int32)
    place = jnp.stack(
        [my_pair, my_expert // 4, my_expert // 2 % 2, my_expert % 2, my_expert, my_expert ^ 1]
    )
    chips = fsdp_size * expert_size // 2
    as_tree = fsdp_size == 2 and layers == 4 and weight_rows % 16 == 0

    blocks = [tokens, swap_pair(tokens), swap_side(tokens)]
    gate_rows, up_rows, down_rows = gate_weight[0].T, up_weight[0].T, down_weight[0]
    if as_tree:
        mine, by_pair, by_side, by_both = group_weights_call(place, attention_in, attention_out)
        both_ways = [
            (f * expert_size + e, (f ^ 1) * expert_size + (e ^ 2))
            for f in range(fsdp_size)
            for e in range(expert_size)
        ]
        rows_here = jnp.stack(
            [mine, swap_pair(by_pair), swap_side(by_side), lax.ppermute(by_both, BOTH, both_ways)]
        )
        rows_here, blocks, gate_rows, up_rows, route_weights = hold(
            (rows_here, blocks, gate_rows, up_rows, route_weights)
        )
        far = swap_layer(rows_here, 2)
        near = swap_layer(rows_here, 1)
    else:
        sent = chip_weights_call(layers, chips, attention_in, attention_out)
        same_core = [[2 * chip + core for chip in range(chips)] for core in range(2)]
        got = lax.all_to_all(
            sent, BOTH, split_axis=0, concat_axis=0, axis_index_groups=same_core, tiled=True
        )
        in_order = jnp.stack([got, swap_core(got)], axis=1)
        in_order = jnp.where(my_expert % 2 == 0, in_order, in_order[:, ::-1])
        pieces = [in_order.reshape(model_width, 8 * HEAD_DIM)]
    blocks.append(swap_side(blocks[1]))
    own_expert = [gate_rows, up_rows, down_rows]
    other_expert = [swap_core(gate_rows), swap_core(up_rows)]
    scale_map, own_tokens, own_gain = scale_call(
        expert_size, routes.T, route_weights.T, blocks[0], attention_gain[None, :]
    )
    blocks[0] = own_tokens
    if as_tree:
        far, near, other_expert, scale_map, blocks, down_rows = hold(
            (far, near, other_expert, scale_map, blocks, down_rows)
        )
        pieces = []
        for piece in (rows_here, near, far, swap_layer(far, 1)):
            pieces += [piece, swap_core(piece)]
    other_expert.append(swap_core(down_rows))

    scale_map = pair_call(scale_map, swap_side(scale_map))
    bit = layers // 2
    while bit > 1:
        scale_map = pair_call(scale_map, swap_layer(scale_map, bit))
        bit //= 2

    keep_top, send_top, keep_low, send_low = attention_call(
        place, own_gain, blocks, pieces, [scale_map, other_expert[2]]
    )

    near_top = swap_side(send_top)
    near_low = swap_pair(send_low)
    own_expert = load_call(own_expert, keep_top)
    scale_map, _ = hold((scale_map, keep_top))
    scale_maps = [scale_map, swap_layer(scale_map, 1)]
    near_top, near_low, own_expert, scale_maps = hold(
        (near_top, near_low, own_expert, scale_maps)
    )
    far_top = swap_pair(sum_call([(keep_top, 1), (near_top, 1)]))
    far_low = swap_side(sum_call([(keep_low, 1), (near_low, 1)]))
    other_expert = load_call(other_expert, near_low)
    far_top, far_low, other_expert = hold((far_top, far_low, other_expert))
    hidden_stream, expert_in = stream_call(
        tokens, expert_gain, keep_top, near_top, far_top, keep_low, near_low, far_low
    )

    arrivals = {0: expert_in}
    order = [0] + sorted(range(1, layers), key=lambda mask: (mask == 1, mask))
    sums, finals, crossings = [], [], []
    for step, mask in enumerate(order):
        low = mask & -mask
        source = arrivals[mask ^ low]
        if mask == 1 and step >= 2:
            source, _ = hold((source, block))
        block = swap_layer(source, low)
        if step == 1:
            block, _ = hold((block, crossings[0]))
        arrivals[mask] = block
        own, crossing = expert_call(
            place,
            [block, swap_side(block)],
            (scale_maps[mask % 2], [mask >> bit & 1 for bit in range(1, layers.bit_length() - 1)]),
            [*own_expert, *other_expert],
            (sums[step - 3 : step - 2] if step >= 3 else []) + crossings[-1:],
        )
        crossings.append(crossing)
        if step == 0:
            first = own
        else:
            sums.append(sum_call([own, swap_side(crossing)], finals[:1] if step == 2 else []))
            finals.append(swap_layer(sums[-1], mask))
    crossing, _ = hold((crossings[0], crossings[-1]))
    return mix_call(hidden_stream, [first, *finals, swap_side(crossing)])


def solution(mesh):
    placed = (
        P(("fsdp", "expert"), None),
        P(),
        P(("fsdp", "expert"), None),
        P(("fsdp", "expert"), None),
        P(),
        P(("fsdp", "expert"), None),
        P(("fsdp", "expert"), None),
        P("expert", None, None),
        P("expert", None, None),
        P("expert", None, None),
    )
    return jax.shard_map(
        per_device,
        mesh=mesh,
        in_specs=placed,
        out_specs=P(("fsdp", "expert"), None),
        check_vma=False,
    )
```

```python
import functools
import math

import jax
import jax.numpy as jnp
from jax import lax
from jax.experimental import pallas as pl
from jax.experimental.pallas import tpu as pltpu
from jax.sharding import PartitionSpec as P

HEAD_DIM = 128
BOTH = ("fsdp", "expert")
VMEM = pl.BlockSpec(memory_space=pltpu.VMEM)
SMEM = pl.BlockSpec(memory_space=pltpu.SMEM)
HBM = pl.BlockSpec(memory_space=pltpu.HBM)
ANYWHERE = pl.BlockSpec(memory_space=pl.ANY)
NT = (((1,), (1,)), ((), ()))


def dot_nt(left, right):
    return lax.dot_general(left, right, NT, preferred_element_type=jnp.float32)


def rms_scale(inputs, scale_gain):
    mean_square = jnp.mean(inputs * inputs, axis=-1, keepdims=True)
    return inputs * lax.rsqrt(mean_square + 1e-06) * scale_gain


def limit(mebibytes):
    return pltpu.CompilerParams(vmem_limit_bytes=mebibytes * 2**20)


def chip_weights_kernel(layers, in_ref, out_ref, sent_ref):
    head_count = out_ref.shape[1] // HEAD_DIM
    pairs = []
    for pair in range(head_count // 2):
        parts = []
        for head in (2 * pair, 2 * pair + 1):
            for part in range(3):
                start = (part * head_count + head) * HEAD_DIM
                parts.append(in_ref[:, start : start + HEAD_DIM])
        parts.append(out_ref[:, 2 * pair * HEAD_DIM : (2 * pair + 2) * HEAD_DIM])
        pairs.append(jnp.concatenate(parts, axis=1))
    for chip in range(sent_ref.shape[0]):
        sent_ref[chip] = pairs[(chip // (2 * layers)) % 2 * 2 + chip % 2]


def chip_weights_call(layers, chips, attention_in, attention_out):
    rows = attention_in.shape[0]
    return pl.pallas_call(
        functools.partial(chip_weights_kernel, layers),
        out_shape=jax.ShapeDtypeStruct((chips, rows, 8 * HEAD_DIM), jnp.bfloat16),
        in_specs=[VMEM] * 2,
        out_specs=VMEM,
        compiler_params=limit(12),
        cost_estimate=pl.CostEstimate(
            flops=0, bytes_accessed=16 * chips * rows * HEAD_DIM, transcendentals=0
        ),
    )(attention_in, attention_out)


def group_weights_kernel(place_ref, in_hbm, out_hbm, *refs):
    sent_refs = refs[:4]
    in_ref, out_ref, sems = refs[4:]
    copies = [
        pltpu.make_async_copy(in_hbm, in_ref, sems.at[0]),
        pltpu.make_async_copy(out_hbm, out_ref, sems.at[1]),
    ]
    for copy in copies:
        copy.start()
    for copy in copies:
        copy.wait()
    width = out_ref.shape[1]
    for index, sent_ref in enumerate(sent_refs):
        pair = (place_ref[0] ^ (index % 2)) * 2 + (place_ref[2] ^ (index // 2))
        start = pl.multiple_of(pair * (2 * HEAD_DIM), HEAD_DIM)
        for part in range(3):
            both = in_ref[:, pl.ds(pl.multiple_of(start + part * width, HEAD_DIM), 2 * HEAD_DIM)]
            for head in range(2):
                to = (3 * head + part) * HEAD_DIM
                sent_ref[:, to : to + HEAD_DIM] = both[:, head * HEAD_DIM : (head + 1) * HEAD_DIM]
        sent_ref[:, 6 * HEAD_DIM :] = out_ref[:, pl.ds(start, 2 * HEAD_DIM)]


def group_weights_call(place, attention_in, attention_out):
    rows = attention_in.shape[0]
    one = jax.ShapeDtypeStruct((rows, 8 * HEAD_DIM), jnp.bfloat16)
    return pl.pallas_call(
        group_weights_kernel,
        out_shape=(one,) * 4,
        in_specs=[SMEM, HBM, HBM],
        out_specs=(VMEM,) * 4,
        scratch_shapes=[
            pltpu.VMEM(attention_in.shape, jnp.bfloat16),
            pltpu.VMEM(attention_out.shape, jnp.bfloat16),
            pltpu.SemaphoreType.DMA((2,)),
        ],
        compiler_params=limit(8),
        cost_estimate=pl.CostEstimate(
            flops=0, bytes_accessed=128 * rows * HEAD_DIM, transcendentals=0
        ),
    )(place, attention_in, attention_out)


def attention_kernel(block_count, piece_count, *refs):
    place_ref, gain_ref = refs[:2]
    block_refs = refs[2 : 2 + block_count]
    piece_refs = refs[2 + block_count : 2 + block_count + piece_count]
    keep_top_ref, send_top_ref, keep_low_ref, send_low_ref, weight_ref = refs[-5:]
    rows = block_refs[0].shape[0]
    half = rows // 2
    if piece_count == 1:
        weight_ref = piece_refs[0]
    else:
        layers = piece_count // 2
        for index, piece_ref in enumerate(piece_refs):
            layer, core = place_ref[1] ^ (index // 2), place_ref[3] ^ (index % 2)
            for chip in range(4):
                pair, side = place_ref[0] ^ (chip % 2), place_ref[2] ^ (chip // 2)
                device = ((pair * layers + layer) * 2 + side) * 2 + core
                span = piece_ref.shape[1]
                start = pl.multiple_of(device * span, 16)
                weight_ref[pl.ds(start, span), :] = piece_ref[chip]
    out_weights = weight_ref[:, 6 * HEAD_DIM :]
    causal = lax.broadcasted_iota(jnp.int32, (rows, rows), 0) >= lax.broadcasted_iota(
        jnp.int32, (rows, rows), 1
    )
    inputs = jnp.concatenate(
        [
            rms_scale(ref[...].astype(jnp.float32), gain_ref[...]).astype(jnp.bfloat16)
            for ref in block_refs
        ],
        axis=0,
    )
    heads = []
    for head in range(2):
        projected = jnp.dot(
            inputs,
            weight_ref[:, 3 * head * HEAD_DIM : 3 * (head + 1) * HEAD_DIM],
            preferred_element_type=jnp.float32,
        ).astype(jnp.bfloat16)
        outs = []
        for block in range(block_count):
            own = projected[block * rows : (block + 1) * rows]
            queries = own[:, :HEAD_DIM]
            keys = own[:, HEAD_DIM : 2 * HEAD_DIM]
            values = own[:, 2 * HEAD_DIM :]
            scores = dot_nt(queries, keys) * (1.0 / math.sqrt(HEAD_DIM))
            raised = jnp.where(causal, jnp.exp(jnp.where(causal, scores, 0.0)), 0.0)
            probs = raised / jnp.sum(raised, axis=-1, keepdims=True)
            outs.append(
                jnp.dot(
                    probs.astype(jnp.bfloat16), values, preferred_element_type=jnp.float32
                ).astype(jnp.bfloat16)
            )
        heads.append(jnp.concatenate(outs, axis=0))
    part = dot_nt(jnp.concatenate(heads, axis=1), out_weights).astype(jnp.bfloat16)
    for block in range(block_count):
        across, along = block // 2, block % 2
        top = send_top_ref if across else keep_top_ref
        low = send_low_ref if along else keep_low_ref
        top[along] = part[block * rows : block * rows + half]
        low[across] = part[block * rows + half : (block + 1) * rows]


def attention_call(place, gain, blocks, pieces, after):
    count = len(blocks)
    rows, width = blocks[0].shape
    tokens = count * rows
    out = jax.ShapeDtypeStruct((count // 2, rows // 2, width), jnp.bfloat16)
    return pl.pallas_call(
        functools.partial(attention_kernel, count, len(pieces)),
        out_shape=(out,) * 4,
        in_specs=[SMEM] + [VMEM] * (1 + count + len(pieces)) + [ANYWHERE] * len(after),
        out_specs=(VMEM,) * 4,
        scratch_shapes=[
            pltpu.VMEM((width, 8 * HEAD_DIM) if len(pieces) > 1 else (16, 128), jnp.bfloat16)
        ],
        compiler_params=limit(16),
        cost_estimate=pl.CostEstimate(
            flops=4 * tokens * (width * 4 * HEAD_DIM + 2 * rows * HEAD_DIM),
            bytes_accessed=4 * tokens * width + width * 16 * HEAD_DIM,
            transcendentals=2 * tokens * rows,
        ),
    )(place, gain, *blocks, *pieces, *after)


def sum_kernel(picks, *refs):
    out_ref = refs[-1]
    total = None
    for ref, pick in zip(refs, picks):
        term = (ref[...] if pick is None else ref[pick]).astype(jnp.float32)
        total = term if total is None else total + term
    out_ref[...] = total.astype(out_ref.dtype)


def sum_call(terms, after=()):
    arrays = [term[0] if isinstance(term, tuple) else term for term in terms]
    picks = [term[1] if isinstance(term, tuple) else None for term in terms]
    shape = arrays[0].shape if picks[0] is None else arrays[0].shape[1:]
    return pl.pallas_call(
        functools.partial(sum_kernel, picks),
        out_shape=jax.ShapeDtypeStruct(shape, jnp.bfloat16),
        in_specs=[VMEM] * len(arrays) + [ANYWHERE] * len(after),
        out_specs=VMEM,
        compiler_params=limit(12),
        cost_estimate=pl.CostEstimate(
            flops=len(arrays) * math.prod(shape),
            bytes_accessed=2 * (len(arrays) + 1) * math.prod(shape),
            transcendentals=0,
        ),
    )(*arrays, *after)


def stream_kernel(tokens_ref, gain_ref, *refs):
    hidden_ref, normed_ref = refs[-2:]
    half = tokens_ref.shape[0] // 2
    for index in range(2):
        keep_ref, near_ref, far_ref = refs[3 * index : 3 * index + 3]
        rows = pl.ds(index * half, half)
        hidden = (
            tokens_ref[rows, :].astype(jnp.float32)
            + keep_ref[0].astype(jnp.float32)
            + near_ref[0].astype(jnp.float32)
            + far_ref[...].astype(jnp.float32)
        )
        hidden_ref[rows, :] = hidden
        normed_ref[rows, :] = rms_scale(hidden, gain_ref[...]).astype(jnp.bfloat16)


def stream_call(tokens, gain, *parts):
    return pl.pallas_call(
        stream_kernel,
        out_shape=(
            jax.ShapeDtypeStruct(tokens.shape, jnp.float32),
            jax.ShapeDtypeStruct(tokens.shape, jnp.bfloat16),
        ),
        in_specs=[VMEM] * 8,
        out_specs=(VMEM, VMEM),
        compiler_params=limit(12),
        cost_estimate=pl.CostEstimate(
            flops=6 * tokens.size, bytes_accessed=14 * tokens.size, transcendentals=0
        ),
    )(tokens, gain[None, :], *parts)


def expert_kernel(tiles, pick, *refs):
    place_ref = refs[0]
    block_refs = refs[1:3]
    scale_ref = refs[3]
    weight_refs = refs[4:10]
    own_ref, side_ref = refs[-2:]
    inputs = jnp.concatenate([ref[...] for ref in block_refs], axis=0)
    result = None
    for expert in range(2):
        gate_ref, up_ref, down_ref = weight_refs[3 * expert : 3 * expert + 3]
        scale = jnp.concatenate(
            [scale_ref[*pick, block, pl.ds(place_ref[4 + expert], 1), :] for block in range(2)],
            axis=1,
        )
        inner = []
        for start, size in tiles:
            gate_value = dot_nt(gate_ref[start : start + size, :], inputs)
            up_value = dot_nt(up_ref[start : start + size, :], inputs)
            half = 0.5 * gate_value
            inner.append(((half + half * jnp.tanh(half)) * (up_value * scale)).astype(jnp.bfloat16))
        inner = jnp.concatenate(inner, axis=0)
        term = jnp.dot(
            down_ref[:, : inner.shape[0]], inner, preferred_element_type=jnp.float32
        )
        result = term if result is None else result + term
    result = result.astype(jnp.bfloat16)
    rows = block_refs[0].shape[0]
    own_ref[...] = result[:, :rows]
    side_ref[...] = result[:, rows:]


def expert_call(place, blocks, picked, weights, after):
    scale_map, pick = picked
    rows, width = blocks[0].shape
    hidden = weights[0].shape[0]
    tiles = [(start, min(256, hidden - start)) for start in range(0, hidden, 256)]
    one = jax.ShapeDtypeStruct((width, rows), jnp.bfloat16)
    return pl.pallas_call(
        functools.partial(expert_kernel, tiles, pick),
        out_shape=(one,) * 2,
        in_specs=[SMEM] + [VMEM] * 9 + [ANYWHERE] * len(after),
        out_specs=(VMEM,) * 2,
        compiler_params=limit(20),
        cost_estimate=pl.CostEstimate(
            flops=2 * 4 * rows * width * hidden * 3,
            bytes_accessed=12 * hidden * width + 8 * rows * width,
            transcendentals=4 * rows * hidden,
        ),
    )(place, *blocks, scale_map, *weights, *after)


def scale_kernel(routes_ref, weights_ref, tokens_ref, gain_ref, map_ref, tokens_out, gain_out):
    top_count, rows = routes_ref.shape
    experts = lax.broadcasted_iota(jnp.int32, (map_ref.shape[0], rows), 0)
    total = jnp.zeros(map_ref.shape, jnp.float32)
    for choice in range(top_count):
        chosen = experts == routes_ref[choice : choice + 1, :]
        total = total + jnp.where(chosen, weights_ref[choice : choice + 1, :], 0.0)
    map_ref[...] = total
    tokens_out[...] = tokens_ref[...]
    gain_out[...] = gain_ref[...]


def scale_call(expert_size, routes, weights, tokens, gain):
    rows = routes.shape[1]
    return pl.pallas_call(
        scale_kernel,
        out_shape=(
            jax.ShapeDtypeStruct((expert_size, rows), jnp.float32),
            jax.ShapeDtypeStruct(tokens.shape, tokens.dtype),
            jax.ShapeDtypeStruct(gain.shape, gain.dtype),
        ),
        in_specs=[VMEM] * 4,
        out_specs=(VMEM,) * 3,
        compiler_params=limit(8),
    )(routes, weights, tokens, gain)


def pair_kernel(first_ref, second_ref, pair_ref):
    pair_ref[0] = first_ref[...]
    pair_ref[1] = second_ref[...]


def pair_call(first, second):
    return pl.pallas_call(
        pair_kernel,
        out_shape=jax.ShapeDtypeStruct((2, *first.shape), first.dtype),
        in_specs=[VMEM] * 2,
        out_specs=VMEM,
        compiler_params=limit(8),
    )(first, second)


def load_kernel(gate_hbm, up_hbm, down_hbm, after_ref, gate_ref, up_ref, turned_ref, down_ref, sems):
    copies = [
        pltpu.make_async_copy(source, target, sems.at[index])
        for index, (source, target) in enumerate(
            ((down_hbm, down_ref), (gate_hbm, gate_ref), (up_hbm, up_ref))
        )
    ]
    for copy in copies:
        copy.start()
    copies[0].wait()
    columns, rows = down_ref.shape
    turned_ref[:, :columns] = down_ref[...].T
    if turned_ref.shape[1] > columns:
        turned_ref[:, columns:] = jnp.zeros((rows, turned_ref.shape[1] - columns), turned_ref.dtype)
    for copy in copies[1:]:
        copy.wait()


def load_call(weights, after):
    gate, _, down = weights
    rows, columns = down.shape
    return pl.pallas_call(
        load_kernel,
        out_shape=(
            jax.ShapeDtypeStruct(gate.shape, gate.dtype),
            jax.ShapeDtypeStruct(gate.shape, gate.dtype),
            jax.ShapeDtypeStruct((columns, -(-rows // 128) * 128), down.dtype),
        ),
        in_specs=[HBM] * 3 + [ANYWHERE],
        out_specs=(VMEM,) * 3,
        scratch_shapes=[pltpu.VMEM(down.shape, down.dtype), pltpu.SemaphoreType.DMA((3,))],
        compiler_params=limit(16),
        cost_estimate=pl.CostEstimate(
            flops=0, bytes_accessed=12 * gate.size, transcendentals=0
        ),
    )(*weights, after)


def mix_kernel(hidden_ref, *refs):
    total = refs[0][...].astype(jnp.float32)
    for ref in refs[1:-1]:
        total = total + ref[...].astype(jnp.float32)
    refs[-1][...] = (hidden_ref[...] + total.T).astype(jnp.bfloat16)


def mix_call(hidden, terms):
    return pl.pallas_call(
        mix_kernel,
        out_shape=jax.ShapeDtypeStruct(hidden.shape, jnp.bfloat16),
        in_specs=[VMEM] * (1 + len(terms)),
        out_specs=VMEM,
        compiler_params=limit(12),
        cost_estimate=pl.CostEstimate(
            flops=(1 + len(terms)) * hidden.size,
            bytes_accessed=(6 + 2 * len(terms)) * hidden.size,
            transcendentals=0,
        ),
    )(hidden, *terms)


def per_device(
    tokens,
    attention_gain,
    attention_in,
    attention_out,
    expert_gain,
    routes,
    route_weights,
    gate_weight,
    up_weight,
    down_weight,
):
    fsdp_size = lax.axis_size("fsdp")
    expert_size = lax.axis_size("expert")
    row_count, model_width = tokens.shape
    weight_rows = attention_out.shape[0]
    layers = expert_size // 4

    def swap_pair(value):
        return lax.ppermute(value, "fsdp", [(f, f ^ 1) for f in range(fsdp_size)])

    def swap_expert(value, mask):
        return lax.ppermute(value, "expert", [(e, e ^ mask) for e in range(expert_size)])

    def swap_core(value):
        return swap_expert(value, 1)

    def swap_side(value):
        return swap_expert(value, 2)

    def swap_layer(value, mask):
        return swap_expert(value, 4 * mask) if mask else value

    hold = lax.optimization_barrier
    my_pair = lax.axis_index("fsdp").astype(jnp.int32)
    my_expert = lax.axis_index("expert").astype(jnp.int32)
    place = jnp.stack(
        [my_pair, my_expert // 4, my_expert // 2 % 2, my_expert % 2, my_expert, my_expert ^ 1]
    )
    chips = fsdp_size * expert_size // 2
    as_tree = fsdp_size == 2 and layers == 4 and weight_rows % 16 == 0

    blocks = [tokens, swap_pair(tokens), swap_side(tokens)]
    gate_rows, up_rows, down_rows = gate_weight[0].T, up_weight[0].T, down_weight[0]
    if as_tree:
        mine, by_pair, by_side, by_both = group_weights_call(place, attention_in, attention_out)
        both_ways = [
            (f * expert_size + e, (f ^ 1) * expert_size + (e ^ 2))
            for f in range(fsdp_size)
            for e in range(expert_size)
        ]
        rows_here = jnp.stack(
            [mine, swap_pair(by_pair), swap_side(by_side), lax.ppermute(by_both, BOTH, both_ways)]
        )
        rows_here, blocks, gate_rows, up_rows, route_weights = hold(
            (rows_here, blocks, gate_rows, up_rows, route_weights)
        )
        far = swap_layer(rows_here, 2)
        near = swap_layer(rows_here, 1)
    else:
        sent = chip_weights_call(layers, chips, attention_in, attention_out)
        same_core = [[2 * chip + core for chip in range(chips)] for core in range(2)]
        got = lax.all_to_all(
            sent, BOTH, split_axis=0, concat_axis=0, axis_index_groups=same_core, tiled=True
        )
        in_order = jnp.stack([got, swap_core(got)], axis=1)
        in_order = jnp.where(my_expert % 2 == 0, in_order, in_order[:, ::-1])
        pieces = [in_order.reshape(model_width, 8 * HEAD_DIM)]
    blocks.append(swap_side(blocks[1]))
    own_expert = [gate_rows, up_rows, down_rows]
    other_expert = [swap_core(gate_rows), swap_core(up_rows)]
    scale_map, own_tokens, own_gain = scale_call(
        expert_size, routes.T, route_weights.T, blocks[0], attention_gain[None, :]
    )
    blocks[0] = own_tokens
    if as_tree:
        far, near, other_expert, scale_map, blocks, down_rows = hold(
            (far, near, other_expert, scale_map, blocks, down_rows)
        )
        pieces = []
        for piece in (rows_here, near, far, swap_layer(far, 1)):
            pieces += [piece, swap_core(piece)]
    other_expert.append(swap_core(down_rows))

    scale_map = pair_call(scale_map, swap_side(scale_map))
    bit = layers // 2
    while bit > 1:
        scale_map = pair_call(scale_map, swap_layer(scale_map, bit))
        bit //= 2

    keep_top, send_top, keep_low, send_low = attention_call(
        place, own_gain, blocks, pieces, [scale_map, other_expert[2]]
    )

    near_top = swap_side(send_top)
    near_low = swap_pair(send_low)
    own_expert = load_call(own_expert, keep_top)
    scale_map, _ = hold((scale_map, keep_top))
    scale_maps = [scale_map, swap_layer(scale_map, 1)]
    near_top, near_low, own_expert, scale_maps = hold(
        (near_top, near_low, own_expert, scale_maps)
    )
    far_top = swap_pair(sum_call([(keep_top, 1), (near_top, 1)]))
    far_low = swap_side(sum_call([(keep_low, 1), (near_low, 1)]))
    other_expert = load_call(other_expert, near_low)
    far_top, far_low, other_expert = hold((far_top, far_low, other_expert))
    hidden_stream, expert_in = stream_call(
        tokens, expert_gain, keep_top, near_top, far_top, keep_low, near_low, far_low
    )

    arrivals = {0: expert_in}
    order = [0] + sorted(range(1, layers), key=lambda mask: (mask == 1, mask))
    sums, finals, crossings = [], [], []
    for step, mask in enumerate(order):
        low = mask & -mask
        source = arrivals[mask ^ low]
        if mask == 1 and step >= 2:
            source, _ = hold((source, block))
        block = swap_layer(source, low)
        if step == 1:
            block, _ = hold((block, crossings[0]))
        arrivals[mask] = block
        own, crossing = expert_call(
            place,
            [block, swap_side(block)],
            (scale_maps[mask % 2], [mask >> bit & 1 for bit in range(1, layers.bit_length() - 1)]),
            [*own_expert, *other_expert],
            (sums[step - 3 : step - 2] if step >= 3 else []) + crossings[-1:],
        )
        crossings.append(crossing)
        if step == 0:
            first = own
        else:
            sums.append(sum_call([own, swap_side(crossing)], finals[:1] if step == 2 else []))
            finals.append(swap_layer(sums[-1], mask))
    crossing, _ = hold((crossings[0], crossings[-1]))
    return mix_call(hidden_stream, [first, *finals, swap_side(crossing)])


def solution(mesh):
    placed = (
        P(("fsdp", "expert"), None),
        P(),
        P(("fsdp", "expert"), None),
        P(("fsdp", "expert"), None),
        P(),
        P(("fsdp", "expert"), None),
        P(("fsdp", "expert"), None),
        P("expert", None, None),
        P("expert", None, None),
        P("expert", None, None),
    )
    return jax.shard_map(
        per_device,
        mesh=mesh,
        in_specs=placed,
        out_specs=P(("fsdp", "expert"), None),
        check_vma=False,
    )
```
